32 devices in a mesh: ctx: 16 (over z, y, x), dp: 2 (over core).
Axes of the slice: x: 2, y: 2, z: 4, core: 2. Of those that a mesh axis runs over, the one named last changes fastest.
Arguments:
- queries: bfloat16 [2, 2048, 1024], P('dp', 'ctx'), may hold values from -45 to 45
- key_rows: bfloat16 [2, 2048, 1024], P('dp', 'ctx'), may hold values from -6 to 6
- value_rows: bfloat16 [2, 2048, 1024], P('dp', 'ctx'), may hold values from -6 to 6
- out_grad: bfloat16 [2, 2048, 1024], P('dp', 'ctx'), may hold values from -6 to 6
- norm_gain: float32 [1024], replicated, may hold values from 0.25 to 1.75
- offsets: int32 [3, 8], replicated, may hold values from 0 to 7, as said below
Outputs:
- attended: bfloat16 [2, 2048, 1024], P('dp', 'ctx')
- query_grad: bfloat16 [2, 2048, 1024], P('dp', 'ctx')
- key_grad: bfloat16 [2, 2048, 1024], P('dp', 'ctx')
- value_grad: bfloat16 [2, 2048, 1024], P('dp', 'ctx')
- gain_grad: float32 [1024], replicated
The draws below stay inside these ranges and needn't reach their ends.
Inputs may be any that keep to these rules, and one draw needn't show every extreme that they name: `offsets`: row l holds each head's offset at level l + 1, from 0 to that level's rate minus 1 (2, 8, 4); in every row some head has offset 0 and some head the rate minus 1.
All inputs are finite; a program needn't handle non-finite values.
Results may differ from the reference program's by a relative error of at most 0.0085.
Values may be sent and summed in bfloat16 or wider, within the bound.
No kernel may reach another device: no remote copies, remote signals or barrier semaphores. Data moves between devices by JAX's collectives and lax.ppermute only.
A program may use at most 64 MiB of HBM per device.

```python
import math
import jax
import jax.numpy as jnp
from jax import lax

H = 8
HD = 128
D = 1024
TOK_DEV = 128
TOKENS = 2048
BATCH = 2
SPAN_A = 2
RATE_A = 1
SPAN_B = 4
RATE_B = 2
SPAN_C = 16
RATE_C = 8
SPAN_D = 8
RATE_D = 4


def base_keys(key):
    shape = (BATCH, TOKENS, D)
    return jnp.clip(jax.random.normal(jax.random.fold_in(key, 7), shape, jnp.float32), -6.0, 6.0)


def draw_key_rows(key, part):
    result = base_keys(key)
    return result.astype(jnp.bfloat16)


def draw_queries(key, part):
    shape = (BATCH, TOKENS, D)
    result = jnp.clip(jax.random.normal(jax.random.fold_in(key, 8), shape, jnp.float32), -6.0, 6.0)
    return result.astype(jnp.bfloat16)


def draw_offsets(key, part):
    rates = jnp.array([RATE_B, RATE_C, RATE_D], dtype=jnp.int32)[:, None]
    base_draw = jax.random.randint(jax.random.fold_in(key, 21), (3, H), 0, 1 << 20, dtype=jnp.int32) % rates
    pick_high = jax.random.randint(jax.random.fold_in(key, 22), (3,), 0, H, dtype=jnp.int32)
    pick_low = (pick_high + 1 + jax.random.randint(jax.random.fold_in(key, 23), (3,), 0, H - 1, dtype=jnp.int32)) % H
    heads = jnp.arange(H, dtype=jnp.int32)[None, :]
    result = jnp.where(heads == pick_high[:, None], rates - 1, base_draw)
    result = jnp.where(heads == pick_low[:, None], 0, result)
    return result.astype(jnp.int32)


def steps_of(rng, shape, cuts, least, largest):
    level, own = 1.0, jax.random.fold_in(rng, 6)
    for dim, parts in cuts:
        steps = jnp.exp(jax.random.uniform(jax.random.fold_in(own, dim), (parts,), jnp.float32, least / len(cuts), largest / len(cuts)))
        level = level * jnp.repeat(steps, shape[dim] // parts).reshape([-1 if axis == dim else 1 for axis in range(len(shape))])
    return level


def scatter_about(stream_key, dims, deviation, limit, pieces=(), kind=jnp.bfloat16):
    gain = steps_of(stream_key, dims, pieces, -0.22, 0.18) if pieces else 1.0
    values = jax.random.normal(stream_key, dims, jnp.float32) * deviation * gain
    return jnp.minimum(jnp.maximum(values, -limit), limit).astype(kind)


def setup_inputs(seed: int = 0) -> dict:
    arg_keys = jax.random.split(jax.random.key(seed), 7)
    return {
        "queries": draw_queries(jax.random.fold_in(arg_keys[6], 71), 0),
        "key_rows": draw_key_rows(jax.random.fold_in(arg_keys[6], 71), 0),
        "value_rows": scatter_about(arg_keys[2], (BATCH, TOKENS, D), 1.0, 6.0, ((0, 2), (1, 16))),
        "out_grad": scatter_about(arg_keys[3], (BATCH, TOKENS, D), 1.0, 6.0, ((0, 2), (1, 16))),
        "norm_gain": jnp.clip(1.0 + 0.15 * jax.random.normal(arg_keys[4], (D,), jnp.float32), 0.25, 1.75),
        "offsets": draw_offsets(jax.random.fold_in(arg_keys[6], 71), 0),
    }


EPSILON = 1e-05

def select_active(tensor, stride, chosen):
    if chosen is None:
        return tensor
    grouped = tensor.reshape((tensor.shape[0] // stride, stride) + tensor.shape[1:])
    index = chosen.astype(jnp.int32).reshape((1, 1, chosen.shape[0]) + (1,) * (tensor.ndim - 2))
    index = jnp.broadcast_to(index, (grouped.shape[0], 1) + grouped.shape[2:])
    return jnp.take_along_axis(grouped, index, axis=1)[:, 0]

def spread(tensor, stride, chosen, filler):
    if chosen is None:
        return tensor
    marked = jnp.arange(stride, dtype=jnp.int32)[:, None] == chosen.astype(jnp.int32)[None, :]
    marked = marked.reshape((1, stride, chosen.shape[0]) + (1,) * (tensor.ndim - 2))
    widened = jnp.where(marked, tensor[:, None], filler)
    return widened.reshape((tensor.shape[0] * stride,) + tensor.shape[1:])

def rounded(tensor):
    return lax.optimization_barrier(tensor.astype(jnp.bfloat16)).astype(jnp.float32)

def one_sequence(queries, key_rows, value_rows, out_grad, norm_gain, offsets):
    scale = HD ** (-0.5)
    plan = [(SPAN_A, RATE_A, None), (SPAN_B, RATE_B, offsets[0]), (SPAN_C, RATE_C, offsets[1]), (SPAN_D, RATE_D, offsets[2])]
    query_heads = queries.reshape(TOKENS, H, HD)
    key_heads = key_rows.reshape(TOKENS, H, HD)
    value_heads = value_rows.reshape(TOKENS, H, HD)

    def segments(tensor, span_size, stride, chosen):
        seg_rows = span_size * TOK_DEV // stride
        picked = select_active(tensor, stride, chosen)
        return picked.reshape((picked.shape[0] // seg_rows, seg_rows) + tensor.shape[1:])
    maxima = []
    totals = []
    weighted = []
    for span_size, stride, chosen in plan:
        act_q = segments(query_heads, span_size, stride, chosen).astype(jnp.float32)
        act_k = segments(key_heads, span_size, stride, chosen).astype(jnp.float32)
        act_v = segments(value_heads, span_size, stride, chosen).astype(jnp.float32)
        scores = jnp.einsum('gqhd,gkhd->ghqk', act_q, act_k) * scale
        level_max = lax.optimization_barrier(jnp.max(scores, axis=-1))
        weights = jnp.exp(scores - level_max[..., None])
        level_total = lax.optimization_barrier(jnp.sum(weights, axis=-1))
        level_sum = jnp.einsum('ghqk,gkhd->gqhd', rounded(weights), act_v)
        maxima.append(spread(jnp.transpose(level_max, (0, 2, 1)).reshape(-1, H), stride, chosen, -jnp.inf))
        totals.append(spread(jnp.transpose(level_total, (0, 2, 1)).reshape(-1, H), stride, chosen, 0.0))
        weighted.append(spread(level_sum.reshape(-1, H, HD), stride, chosen, 0.0))
    maxima = jnp.stack(maxima)
    top_max = lax.optimization_barrier(jnp.max(maxima, axis=0))
    factors = jnp.exp(maxima - top_max[None])
    total = lax.optimization_barrier(jnp.sum(factors * jnp.stack(totals), axis=0))
    mixed = lax.optimization_barrier(jnp.sum(factors[..., None] * jnp.stack(weighted), axis=0)) / total[..., None]
    attn = mixed.reshape(TOKENS, D).astype(jnp.bfloat16)
    log_total = top_max + jnp.log(total)
    features = attn.astype(jnp.float32)
    centered = features - lax.optimization_barrier(jnp.mean(features, axis=-1, keepdims=True))
    inverse = lax.rsqrt(lax.optimization_barrier(jnp.mean(centered * centered, axis=-1, keepdims=True)) + EPSILON)
    normed = centered * inverse
    attended = (normed * norm_gain).astype(jnp.bfloat16)
    upstream = out_grad.astype(jnp.float32)
    scaled = upstream * norm_gain
    attn_grad = (inverse * (scaled - lax.optimization_barrier(jnp.mean(scaled, axis=-1, keepdims=True)) - normed * lax.optimization_barrier(jnp.mean(scaled * normed, axis=-1, keepdims=True)))).astype(jnp.bfloat16)
    gain_part = lax.optimization_barrier(jnp.sum(upstream * normed, axis=0))
    correction = lax.optimization_barrier(jnp.sum((attn_grad.astype(jnp.float32) * features).reshape(TOKENS, H, HD), axis=-1))
    grad_heads = attn_grad.reshape(TOKENS, H, HD)
    query_grad = jnp.zeros((TOKENS, H, HD), jnp.float32)
    key_grad = jnp.zeros((TOKENS, H, HD), jnp.float32)
    value_grad = jnp.zeros((TOKENS, H, HD), jnp.float32)
    for span_size, stride, chosen in plan:
        seg_rows = span_size * TOK_DEV // stride
        share = seg_rows // span_size
        act_q = segments(query_heads, span_size, stride, chosen).astype(jnp.float32)
        act_k = segments(key_heads, span_size, stride, chosen).astype(jnp.float32)
        act_v = segments(value_heads, span_size, stride, chosen).astype(jnp.float32)
        act_g = segments(grad_heads, span_size, stride, chosen).astype(jnp.float32)
        act_log = jnp.transpose(segments(log_total, span_size, stride, chosen), (0, 2, 1))
        act_corr = jnp.transpose(segments(correction, span_size, stride, chosen), (0, 2, 1))
        groups = act_q.shape[0]
        scores = jnp.einsum('gqhd,gkhd->ghqk', act_q, act_k) * scale
        probs = jnp.exp(scores - act_log[..., None])
        probs_low = rounded(probs)
        prob_grad = jnp.einsum('gqhd,gkhd->ghqk', act_g, act_v)
        score_grad = rounded(probs * (prob_grad - act_corr[..., None]))
        query_part = jnp.einsum('ghqk,gkhd->gqhd', score_grad, act_k) * scale
        query_grad = query_grad + spread(query_part.reshape(-1, H, HD), stride, chosen, 0.0)
        split_grad = score_grad.reshape(groups, H, span_size, share, seg_rows)
        split_probs = probs_low.reshape(groups, H, span_size, share, seg_rows)
        split_q = act_q.reshape(groups, span_size, share, H, HD)
        split_g = act_g.reshape(groups, span_size, share, H, HD)
        key_parts = jnp.einsum('ghsqk,gsqhd->gskhd', split_grad, split_q) * scale
        value_parts = jnp.einsum('ghsqk,gsqhd->gskhd', split_probs, split_g)
        owner = jnp.arange(seg_rows, dtype=jnp.int32) // share
        own_mask = (jnp.arange(span_size, dtype=jnp.int32)[:, None] == owner[None, :])[None, :, :, None, None]
        key_sel = lax.optimization_barrier(jnp.sum(jnp.where(own_mask, key_parts, rounded(key_parts)), axis=1))
        value_sel = lax.optimization_barrier(jnp.sum(jnp.where(own_mask, value_parts, rounded(value_parts)), axis=1))
        key_grad = key_grad + spread(key_sel.reshape(-1, H, HD), stride, chosen, 0.0)
        value_grad = value_grad + spread(value_sel.reshape(-1, H, HD), stride, chosen, 0.0)
    return (attended, query_grad.reshape(TOKENS, D).astype(jnp.bfloat16), key_grad.reshape(TOKENS, D).astype(jnp.bfloat16), value_grad.reshape(TOKENS, D).astype(jnp.bfloat16), gain_part)

def reference(queries, key_rows, value_rows, out_grad, norm_gain, offsets):

    def run_one(inputs):
        return one_sequence(inputs[0], inputs[1], inputs[2], inputs[3], norm_gain, offsets)
    attended, query_grad, key_grad, value_grad, gain_parts = lax.map(run_one, (queries, key_rows, value_rows, out_grad))
    gain_grad = lax.optimization_barrier(jnp.sum(gain_parts, axis=0)) / math.sqrt(BATCH * TOKENS)
    return (attended, query_grad, key_grad, value_grad, gain_grad)
```

```python
import functools
import math

import jax
import jax.numpy as jnp
from jax import lax
from jax.experimental import pallas as pl
from jax.experimental.pallas import tpu as pltpu
from jax.sharding import PartitionSpec as P

SPAN_A = 2
RATE_A = 1
SPAN_B = 4
RATE_B = 2
SPAN_C = 16
RATE_C = 8

EPSILON = 1e-05
LOG2E = math.log2(math.e)
TILE = 16
F32 = jnp.float32
BF16 = jnp.bfloat16

NT = (((1,), (1,)), ((), ()))
TN = (((0,), (0,)), ((), ()))
NN = (((1,), (0,)), ((), ()))


def dot(left, right, dims):
    return lax.dot_general(left, right, dims, preferred_element_type=F32)


def row_order(tokens, rate, transposed):
    short = tokens // rate
    placed = lax.broadcasted_iota(jnp.int32, (tokens, tokens), 1 if transposed else 0)
    source = lax.broadcasted_iota(jnp.int32, (tokens, tokens), 0 if transposed else 1)
    return (source == (placed % short) * rate + placed // short).astype(BF16)


def split_kernel(rate, q_ref, k_ref, v_ref, g_ref, out_ref):
    group, _, tokens, hd = out_ref.shape
    order = row_order(tokens, rate, False)
    for t, ref in enumerate((q_ref, k_ref, v_ref, g_ref)):
        moved = dot(order, ref[0], NN).astype(BF16)
        for h in range(group):
            out_ref[h, t] = moved[:, h * hd : (h + 1) * hd]


class Level:
    def __init__(self, index, span, rate, top_rate, fold, group):
        self.index = index
        self.rate = rate
        self.count = top_rate // rate
        self.crossing = span > group
        self.bits = span.bit_length() - group.bit_length()
        self.pieces = min(span, group) // fold
        self.segments = 1 if self.crossing else group // span

    def starts(self, offs_ref):
        first = 0 if self.index == 0 else offs_ref[self.index - 1]
        return [first + self.rate * i for i in range(self.count)]

    def places(self, offs_ref, segment):
        low = segment * self.pieces
        return [(nb, b) for b in self.starts(offs_ref) for nb in range(low, low + self.pieces)]


def gather(read, places):
    return jnp.concatenate([read(nb, b) for nb, b in places], axis=0)


def scores_of(query, key, scale):
    return dot(query, key, NT) * scale


def forward(query, key, value, scale):
    scores = scores_of(query, key, scale)
    top = jnp.max(scores, axis=-1, keepdims=True)
    weights = jnp.exp2(scores - top)
    total = jnp.sum(weights, axis=-1, keepdims=True)
    mixed = dot(weights.astype(BF16), value, NN) / total
    return mixed, jnp.broadcast_to(top + jnp.log2(total), mixed.shape)


def merge(mixed, lse, more, more_lse):
    top = jnp.maximum(lse, more_lse)
    left, right = jnp.exp2(lse - top), jnp.exp2(more_lse - top)
    total = left + right
    return (mixed * left + more * right) / total, top + jnp.log2(total)


def merge_into(o_ref, lse_ref, places, more, more_lse):
    mixed, lse = merge(
        gather(lambda nb, b: o_ref[nb, b], places),
        gather(lambda nb, b: lse_ref[nb, b], places),
        more,
        more_lse,
    )
    put(o_ref, places, mixed)
    put(lse_ref, places, lse)


def put(ref, places, rows):
    size = ref.shape[-2]
    for i, (nb, b) in enumerate(places):
        ref[nb, b] = rows[i * size : (i + 1) * size]


def add(ref, places, rows):
    size = ref.shape[-2]
    for i, (nb, b) in enumerate(places):
        ref[nb, b] += rows[i * size : (i + 1) * size]


def local_kernel(levels, scale, offs_ref, x_ref, o_ref, lse_ref):
    for level in levels:
        for segment in range(level.segments):
            places = level.places(offs_ref, segment)
            query, key, value = (gather(lambda nb, b, t=t: x_ref[nb, t, b], places) for t in range(3))
            mixed, lse = forward(query, key, value, scale)
            if level.index == 0:
                put(o_ref, places, mixed)
                put(lse_ref, places, lse)
            else:
                merge_into(o_ref, lse_ref, places, mixed, lse)


def crossing_keys(level, places, x_ref, other_ref, t):
    found = [x_ref[nb, t, b] for nb, b in places]
    for e in range(other_ref.shape[0]):
        for i in range(level.count):
            found += [other_ref[e, nb, t - 1, i] for nb in range(level.pieces)]
    return jnp.concatenate(found, axis=0)


def stats_kernel(levels, scale, offs_ref, x_ref, o_in, lse_in, gain_ref, *refs):
    others, (attn_ref, lse_ref, stats_ref, o_ref) = refs[: len(levels)], refs[len(levels) :]
    pieces, rate, size, hd = o_ref.shape
    o_ref[...] = o_in[...]
    lse_ref[...] = lse_in[...]
    for level, other_ref in zip(levels, others):
        places = level.places(offs_ref, 0)
        query = gather(lambda nb, b: x_ref[nb, 0, b], places)
        key = crossing_keys(level, places, x_ref, other_ref, 1)
        value = crossing_keys(level, places, x_ref, other_ref, 2)
        merge_into(o_ref, lse_ref, places, *forward(query, key, value, scale))
    chunks = pieces * rate * size // hd
    per = chunks // pieces
    lane = lax.broadcasted_iota(jnp.int32, (hd, hd), 1)
    table = jnp.zeros((hd, hd), F32)
    for nb in range(pieces):
        attn_ref[nb] = o_ref[nb].astype(BF16)
        attn_all = attn_ref[nb].reshape(rate * size, hd).astype(F32)
        grad_all = x_ref[nb, 3].reshape(rate * size, hd).astype(F32)
        for part in range(per):
            attn = attn_all[part * hd : (part + 1) * hd]
            scaled = grad_all[part * hd : (part + 1) * hd] * gain_ref[...]
            total = jnp.sum(attn, axis=-1, keepdims=True)
            away = attn - total * (1.0 / hd)
            sums = (
                total,
                jnp.sum(away * away, axis=-1, keepdims=True),
                jnp.sum(scaled, axis=-1, keepdims=True),
                jnp.sum(scaled * away, axis=-1, keepdims=True),
            )
            for i, column in enumerate(sums):
                table = jnp.where(lane == i * chunks + nb * per + part, column, table)
    turned = table.T[: 4 * chunks]
    for peer in range(stats_ref.shape[0]):
        stats_ref[peer] = turned


def norm_kernel(levels, scale, score_scale, offs_ref, x_ref, attn_ref, lse_ref, gain_ref, stats_ref, *refs):
    count = len(levels)
    others, refs = refs[:count], refs[count:]
    attended_ref, grad_ref, delta_ref, gsum_ref = refs[:4]
    own_refs, sent_refs = refs[4 : 4 + count], refs[4 + count :]
    pieces, rate, size, hd = attn_ref.shape
    chunks = pieces * rate * size // hd
    per = chunks // pieces
    heads = stats_ref.shape[0]
    width = heads * hd
    sums, squares, scaleds, products = (
        [stats_ref[h, i * chunks : (i + 1) * chunks, :] for h in range(heads)] for i in range(4)
    )
    mean = functools.reduce(jnp.add, sums) * (1.0 / width)
    apart = [total * (1.0 / hd) - mean for total in sums]
    variance = functools.reduce(
        jnp.add, [square + hd * a * a for square, a in zip(squares, apart)]
    ) * (1.0 / width)
    inverse = lax.rsqrt(variance + EPSILON)
    first = functools.reduce(jnp.add, scaleds) * (1.0 / width)
    second = (
        functools.reduce(jnp.add, [p + a * s for p, a, s in zip(products, apart, scaleds)])
        * (1.0 / width)
        * inverse
    )
    table = jnp.concatenate(
        [mean, inverse, first, second, jnp.zeros((hd - 4 * chunks, hd), F32)], axis=0
    ).T
    gsum = jnp.zeros((1, hd), F32)
    for nb in range(pieces):
        attn_all = attn_ref[nb].reshape(rate * size, hd).astype(F32)
        grad_all = x_ref[nb, 3].reshape(rate * size, hd).astype(F32)
        attended, grads, deltas = [], [], []
        for part in range(per):
            chunk = nb * per + part
            mean_c, inv_c, first_c, second_c = (
                table[:, i * chunks + chunk : i * chunks + chunk + 1] for i in range(4)
            )
            attn = attn_all[part * hd : (part + 1) * hd]
            upstream = grad_all[part * hd : (part + 1) * hd]
            normed = (attn - mean_c) * inv_c
            attended.append((normed * gain_ref[...]).astype(BF16))
            grad = (inv_c * (upstream * gain_ref[...] - first_c - normed * second_c)).astype(BF16)
            grads.append(grad)
            delta = jnp.sum(grad.astype(F32) * attn, axis=-1, keepdims=True)
            deltas.append(jnp.broadcast_to(delta, attn.shape))
            gsum = gsum + jnp.sum(upstream * normed, axis=0, keepdims=True)
        shape = (rate, size, hd)
        attended_ref[nb] = jnp.concatenate(attended, axis=0).reshape(shape)
        grad_ref[nb] = jnp.concatenate(grads, axis=0).reshape(shape)
        delta_ref[nb] = jnp.concatenate(deltas, axis=0).reshape(shape)
    gsum_ref[...] = gsum
    for level, other_ref, own_ref, sent_ref in zip(levels, others, own_refs, sent_refs):
        places = level.places(offs_ref, 0)
        query = gather(lambda nb, b: x_ref[nb, 0, b], places)
        key = crossing_keys(level, places, x_ref, other_ref, 1)
        value = crossing_keys(level, places, x_ref, other_ref, 2)
        parts = backward(
            query,
            key,
            value,
            gather(lambda nb, b: grad_ref[nb, b], places),
            gather(lambda nb, b: lse_ref[nb, b], places),
            gather(lambda nb, b: delta_ref[nb, b], places),
            scale,
            score_scale,
        )
        own = len(places) * size
        steps = [(i, nb) for i in range(level.count) for nb in range(level.pieces)]
        for t, part in enumerate(parts):
            for j, (i, nb) in enumerate(steps):
                own_ref[t, nb, i] = part[j * size : (j + 1) * size]
                if t > 0:
                    for e in range(sent_ref.shape[0]):
                        low = (e + 1) * own + j * size
                        sent_ref[e, nb, t - 1, i] = part[low : low + size].astype(sent_ref.dtype)


def backward(query, key, value, grad, lse, delta, scale, score_scale):
    wide = key.shape[0] // lse.shape[1]
    spread = lambda column: jnp.concatenate([column] * wide, axis=1)
    probs = jnp.exp2(scores_of(query, key, score_scale) - spread(lse))
    prob_grad = dot(grad, value, NT)
    score_grad = (probs * (prob_grad - spread(delta))).astype(BF16)
    return (
        dot(score_grad, key, NN) * scale,
        dot(score_grad, query, TN) * scale,
        dot(probs.astype(BF16), grad, TN),
    )


def grads_kernel(levels, crossing, scale, score_scale, offs_ref, x_ref, attended_ref, grad_ref, lse_ref, delta_ref, *refs):
    own_refs, (out_ref, kv_ref, dq_ref) = refs[: len(crossing)], refs[len(crossing) :]
    accumulators = (dq_ref, kv_ref.at[0], kv_ref.at[1])
    for level in levels:
        for segment in range(level.segments):
            places = level.places(offs_ref, segment)
            query, key, value = (gather(lambda nb, b, t=t: x_ref[nb, t, b], places) for t in range(3))
            parts = backward(
                query,
                key,
                value,
                gather(lambda nb, b: grad_ref[nb, b], places),
                gather(lambda nb, b: lse_ref[nb, b], places),
                gather(lambda nb, b: delta_ref[nb, b], places),
                scale,
                score_scale,
            )
            for ref, part in zip(accumulators, parts):
                (put if level.index == 0 else add)(ref, places, part)
    for level, own_ref in zip(crossing, own_refs):
        starts = level.starts(offs_ref)
        for t, ref in enumerate(accumulators):
            for i, b in enumerate(starts):
                for nb in range(level.pieces):
                    ref[nb, b] += own_ref[t, nb, i]
    out_ref[:, 0] = dq_ref[...].astype(BF16)
    out_ref[:, 1] = attended_ref[...]


def pack_kernel(crossing, fold, offs_ref, main_ref, kv_in, gsum_ref, *refs):
    arrived_refs, (out_ref, kv_ref) = refs[: len(crossing)], refs[len(crossing) :]
    pieces, _, rate, size, hd = main_ref.shape
    rows = rate * size
    kv_ref[...] = kv_in[...]
    for level, arrived_ref in zip(crossing, arrived_refs):
        for i, b in enumerate(level.starts(offs_ref)):
            for nb in range(level.pieces):
                for t in range(2):
                    kv_ref[t, nb, b] += arrived_ref[nb, t, i].astype(F32)
    total = jnp.broadcast_to(gsum_ref[...], (TILE, hd))
    high = total.astype(BF16).astype(F32)
    middle = (total - high).astype(BF16).astype(F32)
    low = total - high - middle
    row = lax.broadcasted_iota(jnp.int32, (TILE, hd), 0)
    coded = jnp.where(row == 0, high, jnp.where(row == 1, middle, jnp.where(row == 2, low, 0.0)))
    for nb in range(pieces):
        for t in range(2):
            out_ref[nb, t * rows : (t + 1) * rows] = main_ref[nb, t].reshape(rows, hd)
            out_ref[nb, (t + 2) * rows : (t + 3) * rows] = (
                kv_ref[t, nb].reshape(rows, hd).astype(BF16)
            )
        for f in range(fold):
            out_ref[nb, 4 * rows + f * TILE : 4 * rows + (f + 1) * TILE] = coded.astype(BF16)


def join_kernel(rate, factor, in_ref, dq_ref, attended_ref, dk_ref, dv_ref, gain_ref):
    group = in_ref.shape[0]
    hd = in_ref.shape[2]
    tokens = dq_ref.shape[1]
    order = row_order(tokens, rate, True)
    for t, ref in enumerate((dq_ref, attended_ref, dk_ref, dv_ref)):
        for h in range(group):
            moved = dot(order, in_ref[h, t * tokens : (t + 1) * tokens, :], NN)
            ref[0, :, h * hd : (h + 1) * hd] = moved.astype(BF16)
    for h in range(group):
        coded = in_ref[h, 4 * tokens : 4 * tokens + TILE, :].astype(F32)
        gain_ref[:, h * hd : (h + 1) * hd] = jnp.sum(coded, axis=0, keepdims=True) * factor


SMEM = pl.BlockSpec(memory_space=pltpu.SMEM)
VMEM = pl.BlockSpec(memory_space=pltpu.VMEM)


def call(body, name, inputs, outputs, scratch=(), flops=0, limit=24):
    shapes = [jax.ShapeDtypeStruct(*output) for output in outputs]
    moved = sum(x.size * x.dtype.itemsize for x in list(inputs) + shapes)
    return pl.pallas_call(
        body,
        name=name,
        in_specs=[SMEM if x.dtype == jnp.int32 else VMEM for x in inputs],
        out_specs=[VMEM] * len(shapes),
        out_shape=shapes,
        scratch_shapes=[pltpu.VMEM(*each) for each in scratch],
        cost_estimate=pl.CostEstimate(flops=flops, bytes_accessed=moved, transcendentals=0),
        compiler_params=pltpu.CompilerParams(vmem_limit_bytes=limit * 1024 * 1024),
    )(*inputs)


def flip(value, axis, bit):
    pairs = [(source, source ^ (1 << bit)) for source in range(lax.axis_size(axis))]
    return lax.ppermute(value, axis, pairs)


def shards(queries, key_rows, value_rows, out_grad, norm_gain, offsets):
    tokens, width = queries.shape[1:]
    group = offsets.shape[1]
    hd = width // group
    ctx_count = lax.axis_size("ctx")
    dp_count = lax.axis_size("dp")
    scale = hd ** (-0.5)
    score_scale = scale * LOG2E
    spans = [
        (SPAN_A, RATE_A),
        (SPAN_B, RATE_B),
        (SPAN_C, RATE_C),
        (ctx_count // 2, ctx_count // 4),
    ]
    rate = max(r for _, r in spans)
    short = tokens // rate
    fold = max(1, TILE // short)
    size = short * fold
    pieces = group // fold
    levels = [Level(i, span, r, rate, fold, group) for i, (span, r) in enumerate(spans)]
    local = [level for level in levels if not level.crossing]
    crossing = [level for level in levels if level.crossing]
    groups = [list(range(low, low + group)) for low in range(0, ctx_count, group)]
    low_bit = group.bit_length() - 1

    def exchange(value):
        return lax.all_to_all(value, "ctx", 0, 0, tiled=True, axis_index_groups=groups)

    head = lax.axis_index("ctx") % group
    offs = lax.dynamic_slice(offsets, (0, head), (offsets.shape[0], 1))[:, 0]
    gain = lax.dynamic_slice(norm_gain, (head * hd,), (hd,))[None]

    (sent,) = call(
        functools.partial(split_kernel, rate),
        "split",
        [queries, key_rows, value_rows, out_grad],
        [((group, 4, tokens, hd), BF16)],
    )
    x = exchange(sent)
    if fold > 1:
        x = x.reshape(pieces, fold, 4, rate, short, hd).transpose(0, 2, 3, 1, 4, 5)
    x = x.reshape(pieces, 4, rate, size, hd)

    others = []
    for level in crossing:
        own = jnp.concatenate(
            [
                lax.dynamic_slice(x, (0, 1, b, 0, 0), (pieces, 2, 1, size, hd))
                for b in level.starts(offs)
            ],
            axis=2,
        )
        blocks = [own]
        for bit in range(level.bits):
            blocks += [flip(block, "ctx", low_bit + bit) for block in blocks]
        others.append(jnp.stack(blocks[1:]))

    state = (pieces, rate, size, hd)
    o, lse = call(
        functools.partial(local_kernel, local, score_scale),
        "local_forward",
        [offs, x],
        [(state, F32), (state, F32)],
        flops=10**8,
    )
    chunks = group * tokens // hd
    attn, lse, stats = call(
        functools.partial(stats_kernel, crossing, score_scale),
        "crossing_forward",
        [offs, x, o, lse, gain] + others,
        [(state, BF16), (state, F32), ((group, 4 * chunks, hd), F32)],
        scratch=[(state, F32)],
    )
    stats = exchange(stats)
    outs = [(state, BF16), (state, BF16), (state, F32), ((1, hd), F32)]
    outs += [((3, pieces, level.count, size, hd), F32) for level in crossing]
    sent_types = [BF16 if level.bits == 1 else F32 for level in crossing]
    outs += [(other.shape, kind) for other, kind in zip(others, sent_types)]
    attended, grad, delta, gsum, *rest = call(
        functools.partial(norm_kernel, crossing, scale, score_scale),
        "norm_and_crossing",
        [offs, x, attn, lse, gain, stats] + others,
        outs,
    )
    owns, parts = rest[: len(crossing)], rest[len(crossing) :]

    arrived = []
    for level, part in zip(crossing, parts):
        blocks = [None] + [part[e] for e in range(part.shape[0])]
        for bit in reversed(range(level.bits)):
            half = 1 << bit
            came = [flip(block.astype(BF16), "ctx", low_bit + bit) for block in blocks[half:]]
            blocks = [
                c if b is None else b.astype(F32) + c.astype(F32)
                for b, c in zip(blocks[:half], came)
            ]
        arrived.append(blocks[0])
    for axis, count, first in (("dp", dp_count, 0), ("ctx", ctx_count, low_bit)):
        for bit in range(first, count.bit_length() - 1):
            gsum = gsum + flip(gsum, axis, bit)

    main, kv = call(
        functools.partial(grads_kernel, local, crossing, scale, score_scale),
        "local_backward",
        [offs, x, attended, grad, lse, delta] + owns,
        [((pieces, 2, rate, size, hd), BF16), ((2,) + state, F32)],
        scratch=[(state, F32)],
        flops=3 * 10**8,
    )
    tail = TILE * fold
    (packed,) = call(
        functools.partial(pack_kernel, crossing, fold),
        "pack",
        [offs, main, kv, gsum] + arrived,
        [((pieces, 4 * rate * size + tail, hd), BF16)],
        scratch=[((2,) + state, F32)],
    )
    if fold > 1:
        rows = packed[:, : 4 * rate * size].reshape(pieces, 4, rate, fold, short, hd)
        rows = rows.transpose(0, 3, 1, 2, 4, 5).reshape(group, 4 * tokens, hd)
        packed = jnp.concatenate([rows, packed[:, 4 * rate * size :].reshape(group, TILE, hd)], 1)
    back = exchange(packed)
    factor = 1.0 / math.sqrt(ctx_count * dp_count * tokens)
    row = ((1, tokens, width), BF16)
    dq, attended, dk, dv, gain_grad = call(
        functools.partial(join_kernel, rate, factor),
        "join",
        [back],
        [row, row, row, row, ((1, width), F32)],
    )
    return attended, dq, dk, dv, gain_grad[0]


def solution(mesh):
    rows = P("dp", "ctx", None)
    return jax.shard_map(
        shards,
        mesh=mesh,
        in_specs=(rows, rows, rows, rows, P(), P()),
        out_specs=(rows, rows, rows, rows, P()),
        check_vma=False,
    )
```

```python
import functools
import math

import jax
import jax.numpy as jnp
from jax import lax
from jax.experimental import pallas as pl
from jax.experimental.pallas import tpu as pltpu
from jax.sharding import PartitionSpec as P

SPAN_A = 2
RATE_A = 1
SPAN_B = 4
RATE_B = 2
SPAN_C = 16
RATE_C = 8

EPSILON = 1e-05
LOG2E = math.log2(math.e)
TILE = 16
STAGED = 4
F32 = jnp.float32
BF16 = jnp.bfloat16

NT = (((1,), (1,)), ((), ()))
TN = (((0,), (0,)), ((), ()))
NN = (((1,), (0,)), ((), ()))


def dot(left, right, dims):
    return lax.dot_general(left, right, dims, preferred_element_type=F32)


def two_parts(value):
    high = value.astype(BF16)
    return jnp.concatenate([high, (value - high.astype(F32)).astype(BF16)], axis=1)


def row_order(tokens, rate, transposed):
    short = tokens // rate
    placed = lax.broadcasted_iota(jnp.int32, (tokens, tokens), 1 if transposed else 0)
    source = lax.broadcasted_iota(jnp.int32, (tokens, tokens), 0 if transposed else 1)
    return (source == (placed % short) * rate + placed // short).astype(BF16)


def split_kernel(rate, q_ref, k_ref, v_ref, g_ref, out_ref):
    group, _, tokens, hd = out_ref.shape
    order = row_order(tokens, rate, False)
    for t, ref in enumerate((q_ref, k_ref, v_ref, g_ref)):
        moved = dot(order, ref[0], NN).astype(BF16)
        for h in range(group):
            out_ref[h, t] = moved[:, h * hd : (h + 1) * hd]


class Level:
    def __init__(self, index, span, rate, top_rate, fold, group):
        self.index = index
        self.rate = rate
        self.count = top_rate // rate
        self.crossing = span > group
        self.bits = span.bit_length() - group.bit_length()
        self.pieces = min(span, group) // fold
        self.segments = 1 if self.crossing else group // span

    def starts(self, offs):
        first = 0 if self.index == 0 else offs[self.index - 1, 0]
        return [first + self.rate * i for i in range(self.count)]

    def places(self, offs_ref, segment):
        low = segment * self.pieces
        return [(nb, b) for b in self.starts(offs_ref) for nb in range(low, low + self.pieces)]


def gather(read, places):
    return jnp.concatenate([read(nb, b) for nb, b in places], axis=0)


def scores_of(query, key, scale):
    return dot(query, key, NT) * scale


def forward(query, key, value, scale):
    hd = value.shape[1]
    scores = scores_of(query, key, scale)
    top = jnp.max(scores, axis=-1, keepdims=True)
    weights = jnp.exp2(scores - top).astype(BF16)
    both = dot(weights, jnp.concatenate([value, jnp.ones_like(value)], axis=1), NN)
    mixed, total = both[:, :hd], both[:, hd:]
    return mixed / total, top + jnp.log2(total)


def merge(mixed, lse, more, more_lse):
    top = jnp.maximum(lse, more_lse)
    left, right = jnp.exp2(lse - top), jnp.exp2(more_lse - top)
    total = left + right
    return (mixed * left + more * right) / total, top + jnp.log2(total)


def merge_into(o_ref, lse_ref, places, more, more_lse):
    mixed, lse = merge(
        gather(lambda nb, b: o_ref[nb, b], places),
        gather(lambda nb, b: lse_ref[nb, b], places),
        more,
        more_lse,
    )
    put(o_ref, places, mixed)
    put(lse_ref, places, lse)


def put(ref, places, rows):
    size = ref.shape[-2]
    for i, (nb, b) in enumerate(places):
        ref[nb, b] = rows[i * size : (i + 1) * size]


def add(ref, places, rows):
    size = ref.shape[-2]
    for i, (nb, b) in enumerate(places):
        ref[nb, b] += rows[i * size : (i + 1) * size]


def crossing_keys(places, x_ref, other_ref, t):
    found = [x_ref[nb, t, b] for nb, b in places]
    others, pieces, _, count = other_ref.shape[:4]
    found += [
        other_ref[e, nb, t - 1, i]
        for e in range(others)
        for i in range(count)
        for nb in range(pieces)
    ]
    return jnp.concatenate(found, axis=0)


def all_blocks(levels, offs_ref, x_ref, others):
    crossing = 0
    for level in levels:
        if level.crossing:
            other_ref = others[crossing]
            crossing += 1
        for segment in range(level.segments):
            places = level.places(offs_ref, segment)
            query = gather(lambda nb, b: x_ref[nb, 0, b], places)
            if level.crossing:
                key, value = (crossing_keys(places, x_ref, other_ref, t) for t in (1, 2))
            else:
                key, value = (gather(lambda nb, b, t=t: x_ref[nb, t, b], places) for t in (1, 2))
            yield level, places, query, key, value


def row_sums(attn, grad, gain):
    hd = attn.shape[-1]
    attn = attn.astype(BF16).astype(F32)
    scaled = grad.astype(F32) * gain
    total = jnp.sum(attn, axis=-1, keepdims=True)
    away = attn - total * (1.0 / hd)
    return (
        total,
        jnp.sum(away * away, axis=-1, keepdims=True),
        jnp.sum(scaled, axis=-1, keepdims=True),
        jnp.sum(scaled * away, axis=-1, keepdims=True),
    )


def forward_kernel(levels, scale, offs_ref, gain_ref, x_ref, o_ref, lse_ref, table_ref):
    pieces, rate, size, hd = o_ref.shape
    for level, places, query, key, value in all_blocks(levels, offs_ref, x_ref, ()):
        mixed, lse = forward(query, key, value, scale)
        if level.index == 0:
            put(o_ref, places, mixed)
            put(lse_ref, places, lse)
        else:
            merge_into(o_ref, lse_ref, places, mixed, lse)
    per = rate * size // hd
    chunks = pieces * per
    lane = lax.broadcasted_iota(jnp.int32, (hd, hd), 1)
    table = jnp.zeros((hd, hd), F32)
    for nb in range(pieces):
        attn = o_ref[nb].reshape(rate * size, hd)
        grad = x_ref[nb, 3].reshape(rate * size, hd)
        for part in range(per):
            rows = slice(part * hd, (part + 1) * hd)
            for i, column in enumerate(row_sums(attn[rows], grad[rows], gain_ref[...])):
                table = jnp.where(lane == i * chunks + nb * per + part, column, table)
    table_ref[...] = table


def crossing_forward_kernel(levels, scale, offs_ref, gain_ref, x_ref, o_in, lse_in, table_ref, *refs):
    others, (attn_ref, lse_ref, stats_ref, o_ref, sums_ref) = refs[:-5], refs[-5:]
    pieces, rate, size, hd = o_ref.shape
    per = rate * size // hd
    chunks = pieces * per
    lane = lax.broadcasted_iota(jnp.int32, (size, hd), 1)
    o_ref[...] = o_in[...]
    lse_ref[...] = lse_in[...]
    sums_ref[...] = table_ref[...]
    for level, places, query, key, value in all_blocks(levels, offs_ref, x_ref, others):
        merge_into(o_ref, lse_ref, places, *forward(query, key, value, scale))
        sums = row_sums(
            gather(lambda nb, b: o_ref[nb, b], places),
            gather(lambda nb, b: x_ref[nb, 3, b], places),
            gain_ref[...],
        )
        for j, (nb, b) in enumerate(places):
            chunk = nb * per + b * size // hd
            rows = pl.ds(pl.multiple_of(b * size % hd, size), size)
            table = sums_ref[rows, :]
            for i, column in enumerate(sums):
                table = jnp.where(lane == i * chunks + chunk, column[j * size : (j + 1) * size], table)
            sums_ref[rows, :] = table
    attn_ref[...] = o_ref[...].astype(BF16)
    turned = sums_ref[...].T[: 4 * chunks]
    for peer in range(stats_ref.shape[0]):
        stats_ref[peer] = turned


def norm_kernel(heads, levels, scale, score_scale, offs_ref, x_ref, attn_ref, lse_ref, gain_ref, stats_ref, *refs):
    count = len(levels)
    others, refs = refs[:count], refs[count:]
    attended_ref, grad_ref, delta_ref, gsum_ref = refs[:4]
    own_refs, sent_refs = refs[4 : 4 + count], refs[4 + count :]
    pieces, rate, size, hd = attn_ref.shape
    chunks = pieces * rate * size // hd
    per = chunks // pieces
    width = heads * hd
    sums, squares, scaleds, products = (
        [stats_ref[h, i * chunks : (i + 1) * chunks, :] for h in range(heads)] for i in range(4)
    )
    mean = functools.reduce(jnp.add, sums) * (1.0 / width)
    apart = [total * (1.0 / hd) - mean for total in sums]
    variance = functools.reduce(
        jnp.add, [square + hd * a * a for square, a in zip(squares, apart)]
    ) * (1.0 / width)
    inverse = lax.rsqrt(variance + EPSILON)
    first = functools.reduce(jnp.add, scaleds) * (1.0 / width)
    second = (
        functools.reduce(jnp.add, [p + a * s for p, a, s in zip(products, apart, scaleds)])
        * (1.0 / width)
        * inverse
    )
    table = jnp.concatenate(
        [mean, inverse, first, second, jnp.zeros((hd - 4 * chunks, hd), F32)], axis=0
    )
    table = two_parts(table.T)
    lane = lax.broadcasted_iota(jnp.int32, (hd, 2 * hd), 1) % chunks
    picker = lax.broadcasted_iota(jnp.int32, (2 * hd, 4 * hd), 0) % hd // chunks
    picker = (picker == lax.broadcasted_iota(jnp.int32, (2 * hd, 4 * hd), 1) // hd).astype(BF16)
    picked = [jnp.where(lane == chunk, table, jnp.zeros_like(table)) for chunk in range(chunks)]
    columns = dot(jnp.concatenate(picked, axis=0), picker, NN)
    gsum = jnp.zeros((1, hd), F32)
    products = []
    shape = (rate, size, hd)
    for nb in range(pieces):
        attn_all = attn_ref[nb].reshape(rate * size, hd).astype(F32)
        grad_all = x_ref[nb, 3].reshape(rate * size, hd).astype(F32)
        attended, grads = [], []
        for part in range(per):
            chunk = nb * per + part
            mean_c, inv_c, first_c, second_c = (
                columns[chunk * hd : (chunk + 1) * hd, i * hd : (i + 1) * hd] for i in range(4)
            )
            attn = attn_all[part * hd : (part + 1) * hd]
            upstream = grad_all[part * hd : (part + 1) * hd]
            normed = (attn - mean_c) * inv_c
            attended.append((normed * gain_ref[...]).astype(BF16))
            grad = (inv_c * (upstream * gain_ref[...] - first_c - normed * second_c)).astype(BF16)
            grads.append(grad)
            products.append(two_parts(grad.astype(F32) * attn))
            gsum = gsum + jnp.sum(upstream * normed, axis=0, keepdims=True)
        attended_ref[nb] = jnp.concatenate(attended, axis=0).reshape(shape)
        grad_ref[nb] = jnp.concatenate(grads, axis=0).reshape(shape)
    ones = jnp.ones((2 * hd, hd), BF16)
    deltas = dot(jnp.concatenate(products, axis=0), ones, NN)
    for nb in range(pieces):
        delta_ref[nb] = deltas[nb * rate * size : (nb + 1) * rate * size].reshape(shape)
    gsum_ref[...] = gsum
    blocks = list(all_blocks(levels, offs_ref, x_ref, others))
    results = backward(blocks, grad_ref, lse_ref, delta_ref, scale, score_scale)
    for i, parts in enumerate(results):
        own = parts[0].shape[0]
        others_count, pieces, _, steps, size, _ = sent_refs[i].shape
        for t, part in enumerate(parts):
            own_refs[i][t] = part[:own]
            if t > 0:
                low = own
                for e in range(others_count):
                    for step in range(steps):
                        for nb in range(pieces):
                            rows = part[low : low + size].astype(sent_refs[i].dtype)
                            sent_refs[i][e, nb, t - 1, step] = rows
                            low += size


def backward(blocks, grad_ref, lse_ref, delta_ref, scale, score_scale):
    def wide(ref, places, key):
        column = gather(lambda nb, b: ref[nb, b], places)
        return jnp.concatenate([column] * (key.shape[0] // column.shape[1]), axis=1)

    grads = [gather(lambda nb, b: grad_ref[nb, b], places) for _, places, _, _, _ in blocks]
    scores = [scores_of(query, key, score_scale) for _, _, query, key, _ in blocks]
    prob_grads = [dot(grad, block[4], NT) for grad, block in zip(grads, blocks)]
    probs = [
        jnp.exp2(score - wide(lse_ref, places, key))
        for score, (_, places, _, key, _) in zip(scores, blocks)
    ]
    score_grads = [
        (prob * (prob_grad - wide(delta_ref, places, key))).astype(BF16)
        for prob, prob_grad, (_, places, _, key, _) in zip(probs, prob_grads, blocks)
    ]
    queries = [dot(each, block[3], NN) * scale for each, block in zip(score_grads, blocks)]
    keys = [dot(each, block[2], TN) * scale for each, block in zip(score_grads, blocks)]
    values = [dot(prob.astype(BF16), grad, TN) for prob, grad in zip(probs, grads)]
    return list(zip(queries, keys, values))


def local_kernel(levels, crossing, scale, score_scale, offs_ref, x_ref, attended_ref, grad_ref, lse_ref, delta_ref, *refs):
    own_refs, (out_ref, kv_ref, dq_ref) = refs[: len(crossing)], refs[len(crossing) :]
    accumulators = (dq_ref, kv_ref.at[0], kv_ref.at[1])
    blocks = list(all_blocks(levels, offs_ref, x_ref, ()))
    for low in range(0, len(blocks), STAGED):
        some = blocks[low : low + STAGED]
        results = backward(some, grad_ref, lse_ref, delta_ref, scale, score_scale)
        for i, ref in enumerate(accumulators):
            for (level, places, *_), parts in zip(some, results):
                (put if level.index == 0 else add)(ref, places, parts[i])
    for level, own_ref in zip(crossing, own_refs):
        places = level.places(offs_ref, 0)
        for t, ref in enumerate(accumulators):
            add(ref, places, own_ref[t])
    out_ref[:, 0] = dq_ref[...].astype(BF16)
    out_ref[:, 1] = attended_ref[...]


def pack_kernel(crossing, fold, offs_ref, main_ref, kv_in, gsum_ref, *refs):
    arrived_refs, (out_ref, kv_ref) = refs[: len(crossing)], refs[len(crossing) :]
    pieces, _, rate, size, hd = main_ref.shape
    rows = rate * size
    kv_ref[...] = kv_in[...]
    for level, arrived_ref in zip(crossing, arrived_refs):
        for i, b in enumerate(level.starts(offs_ref)):
            for nb in range(level.pieces):
                for t in range(2):
                    kv_ref[t, nb, b] += arrived_ref[nb, t, i].astype(F32)
    total = jnp.broadcast_to(gsum_ref[...], (TILE, hd))
    high = total.astype(BF16).astype(F32)
    middle = (total - high).astype(BF16).astype(F32)
    low = total - high - middle
    row = lax.broadcasted_iota(jnp.int32, (TILE, hd), 0)
    coded = jnp.where(row == 0, high, jnp.where(row == 1, middle, jnp.where(row == 2, low, 0.0)))
    for nb in range(pieces):
        for t in range(2):
            out_ref[nb, t * rows : (t + 1) * rows] = main_ref[nb, t].reshape(rows, hd)
            out_ref[nb, (t + 2) * rows : (t + 3) * rows] = (
                kv_ref[t, nb].reshape(rows, hd).astype(BF16)
            )
        for f in range(fold):
            out_ref[nb, 4 * rows + f * TILE : 4 * rows + (f + 1) * TILE] = coded.astype(BF16)


def join_kernel(rate, factor, in_ref, dq_ref, attended_ref, dk_ref, dv_ref, gain_ref):
    group, _, hd = in_ref.shape
    tokens = dq_ref.shape[1]
    order = row_order(tokens, rate, True)
    for t, ref in enumerate((dq_ref, attended_ref, dk_ref, dv_ref)):
        for h in range(group):
            moved = dot(order, in_ref[h, t * tokens : (t + 1) * tokens, :], NN)
            ref[0, :, h * hd : (h + 1) * hd] = moved.astype(BF16)
    for h in range(group):
        coded = in_ref[h, 4 * tokens : 4 * tokens + TILE, :].astype(F32)
        gain_ref[:, h * hd : (h + 1) * hd] = jnp.sum(coded, axis=0, keepdims=True) * factor


VMEM = pl.BlockSpec(memory_space=pltpu.VMEM)


def call(body, name, inputs, outputs, scratch=(), flops=0, limit=24):
    shapes = [jax.ShapeDtypeStruct(*output) for output in outputs]
    moved = sum(x.size * x.dtype.itemsize for x in list(inputs) + shapes)
    return list(pl.pallas_call(
        body,
        name=name,
        in_specs=[VMEM] * len(inputs),
        out_specs=[VMEM] * len(shapes),
        out_shape=shapes,
        scratch_shapes=[pltpu.VMEM(*each) for each in scratch],
        cost_estimate=pl.CostEstimate(flops=flops, bytes_accessed=moved, transcendentals=0),
        compiler_params=pltpu.CompilerParams(vmem_limit_bytes=limit * 1024 * 1024),
    )(*inputs))


def flip(value, axis, bit):
    pairs = [(source, source ^ (1 << bit)) for source in range(lax.axis_size(axis))]
    return lax.ppermute(value, axis, pairs)


def shards(queries, key_rows, value_rows, out_grad, norm_gain, offsets):
    tokens, width = queries.shape[1:]
    group = offsets.shape[1]
    hd = width // group
    ctx_count = lax.axis_size("ctx")
    dp_count = lax.axis_size("dp")
    scale = hd ** (-0.5)
    score_scale = scale * LOG2E
    spans = [
        (SPAN_A, RATE_A),
        (SPAN_B, RATE_B),
        (SPAN_C, RATE_C),
        (ctx_count // 2, ctx_count // 4),
    ]
    rate = max(r for _, r in spans)
    short = tokens // rate
    fold = max(1, TILE // short)
    size = short * fold
    pieces = group // fold
    levels = [Level(i, span, r, rate, fold, group) for i, (span, r) in enumerate(spans)]
    local = [level for level in levels if not level.crossing]
    crossing = [level for level in levels if level.crossing]
    groups = [list(range(low, low + group)) for low in range(0, ctx_count, group)]
    low_bit = group.bit_length() - 1

    def exchange(value):
        return lax.all_to_all(value, "ctx", 0, 0, tiled=True, axis_index_groups=groups)

    head = lax.axis_index("ctx") % group
    offs = lax.dynamic_slice(offsets, (0, head), (offsets.shape[0], 1))
    offs_rows = jnp.broadcast_to(offs, (offsets.shape[0], hd))
    gain = lax.dynamic_slice(norm_gain, (head * hd,), (hd,))[None]

    (sent,) = call(
        functools.partial(split_kernel, rate),
        "split",
        [queries, key_rows, value_rows, out_grad],
        [((group, 4, tokens, hd), BF16)],
        limit=60,
    )
    x = exchange(sent)
    if fold > 1:
        x = x.reshape(pieces, fold, 4, rate, short, hd).transpose(0, 2, 3, 1, 4, 5)
    x = x.reshape(pieces, 4, rate, size, hd)

    others = []
    for level in crossing:
        own = [
            lax.dynamic_slice(x, (0, 1, b, 0, 0), (pieces, 2, 1, size, hd))
            for b in level.starts(offs)
        ]
        blocks = [jnp.concatenate(own, axis=2)]
        for bit in range(level.bits):
            blocks += [flip(block, "ctx", low_bit + bit) for block in blocks]
        others.append(jnp.stack(blocks[1:]))

    state = (pieces, rate, size, hd)
    chunks = group * tokens // hd
    o, lse, table = call(
        functools.partial(forward_kernel, local, score_scale),
        "local_forward",
        [offs_rows, gain, x],
        [(state, F32), (state, F32), ((hd, hd), F32)],
        flops=10**8,
    )
    attn, lse, stats = call(
        functools.partial(crossing_forward_kernel, crossing, score_scale),
        "crossing_forward",
        [offs_rows, gain, x, o, lse, table] + others,
        [(state, BF16), (state, F32), ((group, 4 * chunks, hd), F32)],
        scratch=[(state, F32), ((hd, hd), F32)],
    )
    stats = exchange(stats)
    outs = [(state, BF16), (state, BF16), (state, F32), ((1, hd), F32)]
    outs += [((3, pieces * level.count * size, hd), F32) for level in crossing]
    sent_types = [BF16 if level.bits == 1 else F32 for level in crossing]
    outs += [(other.shape, kind) for other, kind in zip(others, sent_types)]
    attended, grad, delta, gsum, *rest = call(
        functools.partial(norm_kernel, group, crossing, scale, score_scale),
        "norm_and_crossing",
        [offs_rows, x, attn, lse, gain, stats] + others,
        outs,
        flops=10**7,
    )
    owns, parts = rest[: len(crossing)], rest[len(crossing) :]

    arrived = []
    for level, part in zip(crossing, parts):
        partial = [None] + [part[e] for e in range(part.shape[0])]
        for bit in reversed(range(level.bits)):
            half = 1 << bit
            came = [flip(block.astype(BF16), "ctx", low_bit + bit) for block in partial[half:]]
            partial = [
                c if b is None else b.astype(F32) + c.astype(F32)
                for b, c in zip(partial[:half], came)
            ]
        arrived.append(partial[0])
    for axis, count, first in (("dp", dp_count, 0), ("ctx", ctx_count, low_bit)):
        for bit in range(first, count.bit_length() - 1):
            gsum = gsum + flip(gsum, axis, bit)

    main, kv = call(
        functools.partial(local_kernel, local, crossing, scale, score_scale),
        "local_backward",
        [offs_rows, x, attended, grad, lse, delta] + owns,
        [((pieces, 2, rate, size, hd), BF16), ((2,) + state, F32)],
        scratch=[(state, F32)],
        flops=3 * 10**8,
    )
    (packed,) = call(
        functools.partial(pack_kernel, crossing, fold),
        "pack",
        [offs_rows, main, kv, gsum] + arrived,
        [((pieces, 4 * rate * size + TILE * fold, hd), BF16)],
        scratch=[((2,) + state, F32)],
    )
    if fold > 1:
        rows = packed[:, : 4 * rate * size].reshape(pieces, 4, rate, fold, short, hd)
        rows = rows.transpose(0, 3, 1, 2, 4, 5).reshape(group, 4 * tokens, hd)
        packed = jnp.concatenate([rows, packed[:, 4 * rate * size :].reshape(group, TILE, hd)], 1)
    back = exchange(packed)
    factor = 1.0 / math.sqrt(ctx_count * dp_count * tokens)
    row = ((1, tokens, width), BF16)
    dq, attended, dk, dv, gain_grad = call(
        functools.partial(join_kernel, rate, factor),
        "join",
        [back],
        [row, row, row, row, ((1, width), F32)],
    )
    return attended, dq, dk, dv, gain_grad[0]


def solution(mesh):
    rows = P("dp", "ctx", None)
    return jax.shard_map(
        shards,
        mesh=mesh,
        in_specs=(rows, rows, rows, rows, P(), P()),
        out_specs=(rows, rows, rows, rows, P()),
        check_vma=False,
    )
```

```python
import functools
import math

import jax
import jax.numpy as jnp
from jax import lax
from jax.experimental import pallas as pl
from jax.experimental.pallas import tpu as pltpu
from jax.sharding import PartitionSpec as P

SPAN_A = 2
RATE_A = 1
SPAN_B = 4
RATE_B = 2
SPAN_C = 16
RATE_C = 8

EPSILON = 1e-05
LOG2E = math.log2(math.e)
TILE = 16
STAGED = 4
F32 = jnp.float32
BF16 = jnp.bfloat16

NT = (((1,), (1,)), ((), ()))
TN = (((0,), (0,)), ((), ()))
NN = (((1,), (0,)), ((), ()))


def dot(left, right, dims):
    return lax.dot_general(left, right, dims, preferred_element_type=F32)


def two_parts(value):
    high = value.astype(BF16)
    return jnp.concatenate([high, (value - high.astype(F32)).astype(BF16)], axis=1)


def three_parts(row):
    total = jnp.broadcast_to(row, (TILE, row.shape[1]))
    high = total.astype(BF16).astype(F32)
    middle = (total - high).astype(BF16).astype(F32)
    low = total - high - middle
    place = lax.broadcasted_iota(jnp.int32, total.shape, 0)
    parts = jnp.where(place == 0, high, jnp.where(place == 1, middle, low))
    return jnp.where(place < 3, parts, 0.0).astype(BF16)


def row_order(tokens, rate, transposed):
    short = tokens // rate
    placed = lax.broadcasted_iota(jnp.int32, (tokens, tokens), 1 if transposed else 0)
    source = lax.broadcasted_iota(jnp.int32, (tokens, tokens), 0 if transposed else 1)
    return (source == (placed % short) * rate + placed // short).astype(BF16)


def split_kernel(rate, q_ref, k_ref, v_ref, g_ref, out_ref):
    group, _, tokens, hd = out_ref.shape
    order = row_order(tokens, rate, False)
    for t, ref in enumerate((q_ref, k_ref, v_ref, g_ref)):
        moved = dot(order, ref[0], NN).astype(BF16)
        for h in range(group):
            out_ref[h, t] = moved[:, h * hd : (h + 1) * hd]


class Level:
    def __init__(self, index, span, rate, top_rate, fold, group):
        self.index = index
        self.rate = rate
        self.count = top_rate // rate
        self.crossing = span > group
        self.bits = span.bit_length() - group.bit_length()
        self.pieces = min(span, group) // fold
        self.segments = 1 if self.crossing else group // span

    def starts(self, offs):
        first = 0 if self.index == 0 else offs[self.index - 1, 0]
        return [first + self.rate * i for i in range(self.count)]

    def places(self, offs_ref, segment):
        low = segment * self.pieces
        return [(nb, b) for b in self.starts(offs_ref) for nb in range(low, low + self.pieces)]


def gather(read, places):
    return jnp.concatenate([read(nb, b) for nb, b in places], axis=0)


def scores_of(query, key, scale):
    return dot(query, key, NT) * scale


def forward(query, key, value, scale):
    hd = value.shape[1]
    scores = scores_of(query, key, scale)
    top = jnp.max(scores, axis=-1, keepdims=True)
    weights = jnp.exp2(scores - top).astype(BF16)
    both = dot(weights, jnp.concatenate([value, jnp.ones_like(value)], axis=1), NN)
    mixed, total = both[:, :hd], both[:, hd:]
    return mixed / total, top + jnp.log2(total)


def merge(mixed, lse, more, more_lse):
    top = jnp.maximum(lse, more_lse)
    left, right = jnp.exp2(lse - top), jnp.exp2(more_lse - top)
    total = left + right
    return (mixed * left + more * right) / total, top + jnp.log2(total)


def merge_into(o_ref, lse_ref, places, more, more_lse):
    mixed, lse = merge(
        gather(lambda nb, b: o_ref[nb, b], places),
        gather(lambda nb, b: lse_ref[nb, b], places),
        more,
        more_lse,
    )
    put(o_ref, places, mixed)
    put(lse_ref, places, lse)


def put(ref, places, rows):
    size = ref.shape[-2]
    for i, (nb, b) in enumerate(places):
        ref[nb, b] = rows[i * size : (i + 1) * size]


def add(ref, places, rows):
    size = ref.shape[-2]
    for i, (nb, b) in enumerate(places):
        ref[nb, b] += rows[i * size : (i + 1) * size]


def crossing_keys(places, x_ref, other_ref, t):
    found = [x_ref[nb, t, b] for nb, b in places]
    others, pieces, _, count = other_ref.shape[:4]
    found += [
        other_ref[e, nb, t - 1, i]
        for e in range(others)
        for i in range(count)
        for nb in range(pieces)
    ]
    return jnp.concatenate(found, axis=0)


def all_blocks(levels, offs_ref, x_ref, others):
    crossing = 0
    for level in levels:
        if level.crossing:
            other_ref = others[crossing]
            crossing += 1
        for segment in range(level.segments):
            places = level.places(offs_ref, segment)
            query = gather(lambda nb, b: x_ref[nb, 0, b], places)
            if level.crossing:
                key, value = (crossing_keys(places, x_ref, other_ref, t) for t in (1, 2))
            else:
                key, value = (gather(lambda nb, b, t=t: x_ref[nb, t, b], places) for t in (1, 2))
            yield level, places, query, key, value


def row_sums(attn, grad, gain):
    hd = attn.shape[-1]
    attn = attn.astype(BF16).astype(F32)
    scaled = grad.astype(F32) * gain
    total = jnp.sum(attn, axis=-1, keepdims=True)
    away = attn - total * (1.0 / hd)
    return (
        total,
        jnp.sum(away * away, axis=-1, keepdims=True),
        jnp.sum(scaled, axis=-1, keepdims=True),
        jnp.sum(scaled * away, axis=-1, keepdims=True),
    )


def forward_kernel(levels, scale, offs_ref, gain_ref, x_ref, o_ref, lse_ref, table_ref):
    pieces, rate, size, hd = o_ref.shape
    for level, places, query, key, value in all_blocks(levels, offs_ref, x_ref, ()):
        mixed, lse = forward(query, key, value, scale)
        if level.index == 0:
            put(o_ref, places, mixed)
            put(lse_ref, places, lse)
        else:
            merge_into(o_ref, lse_ref, places, mixed, lse)
    per = rate * size // hd
    chunks = pieces * per
    lane = lax.broadcasted_iota(jnp.int32, (hd, hd), 1)
    table = jnp.zeros((hd, hd), F32)
    for nb in range(pieces):
        attn = o_ref[nb].reshape(rate * size, hd)
        grad = x_ref[nb, 3].reshape(rate * size, hd)
        for part in range(per):
            rows = slice(part * hd, (part + 1) * hd)
            for i, column in enumerate(row_sums(attn[rows], grad[rows], gain_ref[...])):
                table = jnp.where(lane == i * chunks + nb * per + part, column, table)
    table_ref[...] = table


def crossing_forward_kernel(levels, scale, offs_ref, gain_ref, x_ref, o_in, lse_in, table_ref, *refs):
    others, (attn_ref, lse_ref, stats_ref, o_ref, sums_ref) = refs[:-5], refs[-5:]
    pieces, rate, size, hd = o_ref.shape
    per = rate * size // hd
    chunks = pieces * per
    lane = lax.broadcasted_iota(jnp.int32, (size, hd), 1)
    o_ref[...] = o_in[...]
    lse_ref[...] = lse_in[...]
    sums_ref[...] = table_ref[...]
    for level, places, query, key, value in all_blocks(levels, offs_ref, x_ref, others):
        merge_into(o_ref, lse_ref, places, *forward(query, key, value, scale))
        sums = row_sums(
            gather(lambda nb, b: o_ref[nb, b], places),
            gather(lambda nb, b: x_ref[nb, 3, b], places),
            gain_ref[...],
        )
        for j, (nb, b) in enumerate(places):
            chunk = nb * per + b * size // hd
            rows = pl.ds(pl.multiple_of(b * size % hd, size), size)
            table = sums_ref[rows, :]
            for i, column in enumerate(sums):
                table = jnp.where(lane == i * chunks + chunk, column[j * size : (j + 1) * size], table)
            sums_ref[rows, :] = table
    attn_ref[...] = o_ref[...].astype(BF16)
    turned = sums_ref[...].T[: 4 * chunks]
    for peer in range(stats_ref.shape[0]):
        stats_ref[peer] = turned


def norm_kernel(heads, levels, scale, score_scale, offs_ref, x_ref, attn_ref, lse_ref, gain_ref, stats_ref, *refs):
    count = len(levels)
    others, refs = refs[:count], refs[count:]
    attended_ref, grad_ref, delta_ref, gsum_ref = refs[:4]
    own_refs, sent_refs = refs[4 : 4 + count], refs[4 + count :]
    pieces, rate, size, hd = attn_ref.shape
    chunks = pieces * rate * size // hd
    per = chunks // pieces
    width = heads * hd
    sums, squares, scaleds, products = (
        [stats_ref[h, i * chunks : (i + 1) * chunks, :] for h in range(heads)] for i in range(4)
    )
    mean = functools.reduce(jnp.add, sums) * (1.0 / width)
    apart = [total * (1.0 / hd) - mean for total in sums]
    variance = functools.reduce(
        jnp.add, [square + hd * a * a for square, a in zip(squares, apart)]
    ) * (1.0 / width)
    inverse = lax.rsqrt(variance + EPSILON)
    first = functools.reduce(jnp.add, scaleds) * (1.0 / width)
    second = (
        functools.reduce(jnp.add, [p + a * s for p, a, s in zip(products, apart, scaleds)])
        * (1.0 / width)
        * inverse
    )
    table = jnp.concatenate(
        [mean, inverse, first, second, jnp.zeros((hd - 4 * chunks, hd), F32)], axis=0
    )
    table = two_parts(table.T)
    lane = lax.broadcasted_iota(jnp.int32, (hd, 2 * hd), 1) % chunks
    picker = lax.broadcasted_iota(jnp.int32, (2 * hd, 4 * hd), 0) % hd // chunks
    picker = (picker == lax.broadcasted_iota(jnp.int32, (2 * hd, 4 * hd), 1) // hd).astype(BF16)
    picked = [jnp.where(lane == chunk, table, jnp.zeros_like(table)) for chunk in range(chunks)]
    columns = dot(jnp.concatenate(picked, axis=0), picker, NN)
    gsum = jnp.zeros((1, hd), F32)
    products = []
    shape = (rate, size, hd)
    for nb in range(pieces):
        attn_all = attn_ref[nb].reshape(rate * size, hd).astype(F32)
        grad_all = x_ref[nb, 3].reshape(rate * size, hd).astype(F32)
        attended, grads = [], []
        for part in range(per):
            chunk = nb * per + part
            mean_c, inv_c, first_c, second_c = (
                columns[chunk * hd : (chunk + 1) * hd, i * hd : (i + 1) * hd] for i in range(4)
            )
            attn = attn_all[part * hd : (part + 1) * hd]
            upstream = grad_all[part * hd : (part + 1) * hd]
            normed = (attn - mean_c) * inv_c
            attended.append((normed * gain_ref[...]).astype(BF16))
            grad = (inv_c * (upstream * gain_ref[...] - first_c - normed * second_c)).astype(BF16)
            grads.append(grad)
            products.append(two_parts(grad.astype(F32) * attn))
            gsum = gsum + jnp.sum(upstream * normed, axis=0, keepdims=True)
        attended_ref[nb] = jnp.concatenate(attended, axis=0).reshape(shape)
        grad_ref[nb] = jnp.concatenate(grads, axis=0).reshape(shape)
    ones = jnp.ones((2 * hd, hd), BF16)
    deltas = dot(jnp.concatenate(products, axis=0), ones, NN)
    for nb in range(pieces):
        delta_ref[nb] = deltas[nb * rate * size : (nb + 1) * rate * size].reshape(shape)
    gsum_ref[...] = gsum
    blocks = list(all_blocks(levels, offs_ref, x_ref, others))
    results = backward(blocks, grad_ref, lse_ref, delta_ref, scale, score_scale)
    for i, parts in enumerate(results):
        own = parts[0].shape[0]
        level, coded = levels[i], three_parts(gsum)
        steps = level.count
        for t, part in enumerate(parts):
            own_refs[i][t] = part[:own]
            if t > 0:
                low = own
                for e in range(sent_refs[i].shape[0]):
                    for step in range(steps):
                        for nb in range(level.pieces):
                            rows = part[low : low + size].astype(sent_refs[i].dtype)
                            sent_refs[i][e, (nb * 2 + t - 1) * steps + step] = rows
                            low += size
                    sent_refs[i][e, 2 * steps * level.pieces] = coded.astype(sent_refs[i].dtype)


def backward(blocks, grad_ref, lse_ref, delta_ref, scale, score_scale):
    def wide(ref, places, key):
        column = gather(lambda nb, b: ref[nb, b], places)
        return jnp.concatenate([column] * (key.shape[0] // column.shape[1]), axis=1)

    grads = [gather(lambda nb, b: grad_ref[nb, b], places) for _, places, _, _, _ in blocks]
    scores = [scores_of(query, key, score_scale) for _, _, query, key, _ in blocks]
    prob_grads = [dot(grad, block[4], NT) for grad, block in zip(grads, blocks)]
    probs = [
        jnp.exp2(score - wide(lse_ref, places, key))
        for score, (_, places, _, key, _) in zip(scores, blocks)
    ]
    score_grads = [
        (prob * (prob_grad - wide(delta_ref, places, key))).astype(BF16)
        for prob, prob_grad, (_, places, _, key, _) in zip(probs, prob_grads, blocks)
    ]
    queries = [dot(each, block[3], NN) * scale for each, block in zip(score_grads, blocks)]
    keys = [dot(each, block[2], TN) * scale for each, block in zip(score_grads, blocks)]
    values = [dot(prob.astype(BF16), grad, TN) for prob, grad in zip(probs, grads)]
    return list(zip(queries, keys, values))


def local_kernel(levels, crossing, scale, score_scale, offs_ref, x_ref, attended_ref, grad_ref, lse_ref, delta_ref, *refs):
    own_refs, (out_ref, kv_ref, dq_ref) = refs[: len(crossing)], refs[len(crossing) :]
    accumulators = (dq_ref, kv_ref.at[0], kv_ref.at[1])
    blocks = list(all_blocks(levels, offs_ref, x_ref, ()))
    for low in range(0, len(blocks), STAGED):
        some = blocks[low : low + STAGED]
        results = backward(some, grad_ref, lse_ref, delta_ref, scale, score_scale)
        for i, ref in enumerate(accumulators):
            for (level, places, *_), parts in zip(some, results):
                (put if level.index == 0 else add)(ref, places, parts[i])
    for level, own_ref in zip(crossing, own_refs):
        places = level.places(offs_ref, 0)
        for t, ref in enumerate(accumulators):
            add(ref, places, own_ref[t])
    out_ref[:, 0] = dq_ref[...].astype(BF16)
    out_ref[:, 1] = attended_ref[...]


def pack_kernel(crossing, fold, sums, offs_ref, main_ref, kv_in, *refs):
    gsum_refs, arrived_refs, (out_ref, kv_ref) = refs[:sums], refs[sums:-2], refs[-2:]
    pieces, _, rate, size, hd = main_ref.shape
    rows = rate * size
    kv_ref[...] = kv_in[...]
    for level, arrived_ref in zip(crossing, arrived_refs):
        for i, b in enumerate(level.starts(offs_ref)):
            for nb in range(level.pieces):
                for t in range(2):
                    block = (nb * 2 + t) * level.count + i
                    kv_ref[t, nb, b] += arrived_ref[block].astype(F32)
    total = functools.reduce(jnp.add, [ref[...] for ref in gsum_refs])
    if sums > 1:
        other = arrived_refs[0][arrived_refs[0].shape[0] - 1]
        total = total + jnp.sum(other.astype(F32), axis=0, keepdims=True)
    coded = three_parts(total)
    for nb in range(pieces):
        for t in range(2):
            out_ref[nb, t * rows : (t + 1) * rows] = main_ref[nb, t].reshape(rows, hd)
            out_ref[nb, (t + 2) * rows : (t + 3) * rows] = (
                kv_ref[t, nb].reshape(rows, hd).astype(BF16)
            )
        for f in range(fold):
            out_ref[nb, 4 * rows + f * TILE : 4 * rows + (f + 1) * TILE] = coded


def join_kernel(rate, factor, in_ref, dq_ref, attended_ref, dk_ref, dv_ref, gain_ref):
    group, _, hd = in_ref.shape
    tokens = dq_ref.shape[1]
    order = row_order(tokens, rate, True)
    for t, ref in enumerate((dq_ref, attended_ref, dk_ref, dv_ref)):
        for h in range(group):
            moved = dot(order, in_ref[h, t * tokens : (t + 1) * tokens, :], NN)
            ref[0, :, h * hd : (h + 1) * hd] = moved.astype(BF16)
    for h in range(group):
        coded = in_ref[h, 4 * tokens : 4 * tokens + TILE, :].astype(F32)
        gain_ref[:, h * hd : (h + 1) * hd] = jnp.sum(coded, axis=0, keepdims=True) * factor


VMEM = pl.BlockSpec(memory_space=pltpu.VMEM)


def call(body, name, inputs, outputs, scratch=(), flops=0, limit=24):
    shapes = [jax.ShapeDtypeStruct(*output) for output in outputs]
    moved = sum(x.size * x.dtype.itemsize for x in list(inputs) + shapes)
    return list(pl.pallas_call(
        body,
        name=name,
        in_specs=[VMEM] * len(inputs),
        out_specs=[VMEM] * len(shapes),
        out_shape=shapes,
        scratch_shapes=[pltpu.VMEM(*each) for each in scratch],
        cost_estimate=pl.CostEstimate(flops=flops, bytes_accessed=moved, transcendentals=0),
        compiler_params=pltpu.CompilerParams(vmem_limit_bytes=limit * 1024 * 1024),
    )(*inputs))


def flip(value, axis, bit):
    pairs = [(source, source ^ (1 << bit)) for source in range(lax.axis_size(axis))]
    return lax.ppermute(value, axis, pairs)


def cross(value):
    ctx_count, dp_count = lax.axis_size("ctx"), lax.axis_size("dp")
    count = ctx_count * dp_count
    far = ctx_count // 2 * dp_count + dp_count // 2
    pairs = [(source, source ^ far) for source in range(count)]
    return lax.ppermute(value, ("ctx", "dp"), pairs)


def shards(queries, key_rows, value_rows, out_grad, norm_gain, offsets):
    tokens, width = queries.shape[1:]
    group = offsets.shape[1]
    hd = width // group
    ctx_count = lax.axis_size("ctx")
    dp_count = lax.axis_size("dp")
    scale = hd ** (-0.5)
    score_scale = scale * LOG2E
    spans = [
        (SPAN_A, RATE_A),
        (SPAN_B, RATE_B),
        (SPAN_C, RATE_C),
        (ctx_count // 2, ctx_count // 4),
    ]
    rate = max(r for _, r in spans)
    short = tokens // rate
    fold = max(1, TILE // short)
    size = short * fold
    pieces = group // fold
    levels = [Level(i, span, r, rate, fold, group) for i, (span, r) in enumerate(spans)]
    local = [level for level in levels if not level.crossing]
    crossing = [level for level in levels if level.crossing]
    groups = [list(range(low, low + group)) for low in range(0, ctx_count, group)]
    low_bit = group.bit_length() - 1

    def exchange(value):
        return lax.all_to_all(value, "ctx", 0, 0, tiled=True, axis_index_groups=groups)

    head = lax.axis_index("ctx") % group
    offs = lax.dynamic_slice(offsets, (0, head), (offsets.shape[0], 1))
    offs_rows = jnp.broadcast_to(offs, (offsets.shape[0], hd))
    gain = lax.dynamic_slice(norm_gain, (head * hd,), (hd,))[None]

    (sent,) = call(
        functools.partial(split_kernel, rate),
        "split",
        [queries, key_rows, value_rows, out_grad],
        [((group, 4, tokens, hd), BF16)],
        limit=60,
    )
    x = exchange(sent)
    if fold > 1:
        x = x.reshape(pieces, fold, 4, rate, short, hd).transpose(0, 2, 3, 1, 4, 5)
    x = x.reshape(pieces, 4, rate, size, hd)

    others = []
    for level in crossing:
        own = [
            lax.dynamic_slice(x, (0, 1, b, 0, 0), (pieces, 2, 1, size, hd))
            for b in level.starts(offs)
        ]
        blocks = [jnp.concatenate(own, axis=2)]
        for bit in range(level.bits):
            blocks += [flip(block, "ctx", low_bit + bit) for block in blocks]
        others.append(jnp.stack(blocks[1:]))

    state = (pieces, rate, size, hd)
    chunks = group * tokens // hd
    o, lse, table = call(
        functools.partial(forward_kernel, local, score_scale),
        "local_forward",
        [offs_rows, gain, x],
        [(state, F32), (state, F32), ((hd, hd), F32)],
        flops=10**8,
    )
    attn, lse, stats = call(
        functools.partial(crossing_forward_kernel, crossing, score_scale),
        "crossing_forward",
        [offs_rows, gain, x, o, lse, table] + others,
        [(state, BF16), (state, F32), ((group, 4 * chunks, hd), F32)],
        scratch=[(state, F32), ((hd, hd), F32)],
    )
    stats = exchange(stats)
    outs = [(state, BF16), (state, BF16), (state, F32), ((1, hd), F32)]
    outs += [((3, pieces * level.count * size, hd), F32) for level in crossing]
    sent_types = [BF16 if level.bits == 1 else F32 for level in crossing]
    outs += [
        ((other.shape[0], 2 * level.pieces * level.count + 1, size, hd), kind)
        for level, other, kind in zip(crossing, others, sent_types)
    ]
    attended, grad, delta, gsum, *rest = call(
        functools.partial(norm_kernel, group, crossing, scale, score_scale),
        "norm_and_crossing",
        [offs_rows, x, attn, lse, gain, stats] + others,
        outs,
        flops=10**7,
    )
    owns, parts = rest[: len(crossing)], rest[len(crossing) :]

    arrived = []
    for level, part in zip(crossing, parts):
        partial = [None] + [part[e] for e in range(part.shape[0])]
        for bit in reversed(range(level.bits)):
            half = 1 << bit
            came = [flip(block.astype(BF16), "ctx", low_bit + bit) for block in partial[half:]]
            partial = [
                c if b is None else b.astype(F32) + c.astype(F32)
                for b, c in zip(partial[:half], came)
            ]
        arrived.append(partial[0])
    alone = ctx_count == 2 * group and dp_count == 2 and size == TILE and len(crossing) == 1
    gsums = [gsum]
    if alone:
        gsums += [flip(gsum, "dp", 0), cross(gsum)]
    else:
        for axis, count, first in (("dp", dp_count, 0), ("ctx", ctx_count, low_bit)):
            for bit in range(first, count.bit_length() - 1):
                gsums = [gsums[0] + flip(gsums[0], axis, bit)]

    main, kv = call(
        functools.partial(local_kernel, local, crossing, scale, score_scale),
        "local_backward",
        [offs_rows, x, attended, grad, lse, delta] + owns,
        [((pieces, 2, rate, size, hd), BF16), ((2,) + state, F32)],
        scratch=[(state, F32)],
        flops=3 * 10**8,
    )
    (packed,) = call(
        functools.partial(pack_kernel, crossing, fold, len(gsums)),
        "pack",
        [offs_rows, main, kv] + gsums + arrived,
        [((pieces, 4 * rate * size + TILE * fold, hd), BF16)],
        scratch=[((2,) + state, F32)],
    )
    if fold > 1:
        rows = packed[:, : 4 * rate * size].reshape(pieces, 4, rate, fold, short, hd)
        rows = rows.transpose(0, 3, 1, 2, 4, 5).reshape(group, 4 * tokens, hd)
        packed = jnp.concatenate([rows, packed[:, 4 * rate * size :].reshape(group, TILE, hd)], 1)
    back = exchange(packed)
    factor = 1.0 / math.sqrt(ctx_count * dp_count * tokens)
    row = ((1, tokens, width), BF16)
    dq, attended, dk, dv, gain_grad = call(
        functools.partial(join_kernel, rate, factor),
        "join",
        [back],
        [row, row, row, row, ((1, width), F32)],
    )
    return attended, dq, dk, dv, gain_grad[0]


def solution(mesh):
    rows = P("dp", "ctx", None)
    return jax.shard_map(
        shards,
        mesh=mesh,
        in_specs=(rows, rows, rows, rows, P(), P()),
        out_specs=(rows, rows, rows, rows, P()),
        check_vma=False,
    )
```

```python
import functools
import math

import jax
import jax.numpy as jnp
from jax import lax
from jax.experimental import pallas as pl
from jax.experimental.pallas import tpu as pltpu
from jax.sharding import PartitionSpec as P

SPAN_A = 2
RATE_A = 1
SPAN_B = 4
RATE_B = 2
SPAN_C = 16
RATE_C = 8

EPSILON = 1e-05
LOG2E = math.log2(math.e)
TILE = 16
STAGED = 4
ORDER = (0, 7, 2, 6, 1, 5, 4, 3)
F32 = jnp.float32
BF16 = jnp.bfloat16

NT = (((1,), (1,)), ((), ()))
TN = (((0,), (0,)), ((), ()))
NN = (((1,), (0,)), ((), ()))


def dot(left, right, dims):
    return lax.dot_general(left, right, dims, preferred_element_type=F32)


def two_parts(value):
    high = value.astype(BF16)
    return jnp.concatenate([high, (value - high.astype(F32)).astype(BF16)], axis=1)


def three_parts(row):
    total = jnp.broadcast_to(row, (TILE, row.shape[1]))
    high = total.astype(BF16).astype(F32)
    middle = (total - high).astype(BF16).astype(F32)
    low = total - high - middle
    place = lax.broadcasted_iota(jnp.int32, total.shape, 0)
    parts = jnp.where(place == 0, high, jnp.where(place == 1, middle, low))
    return jnp.where(place < 3, parts, 0.0).astype(BF16)


def row_order(tokens, rate, transposed):
    short = tokens // rate
    placed = lax.broadcasted_iota(jnp.int32, (tokens, tokens), 1 if transposed else 0)
    source = lax.broadcasted_iota(jnp.int32, (tokens, tokens), 0 if transposed else 1)
    return (source == (placed % short) * rate + placed // short).astype(BF16)


def split_kernel(rate, q_ref, k_ref, v_ref, g_ref, out_ref):
    group, _, tokens, hd = out_ref.shape
    order = row_order(tokens, rate, False)
    for t, ref in enumerate((q_ref, k_ref, v_ref, g_ref)):
        moved = dot(order, ref[0], NN).astype(BF16)
        for h in range(group):
            out_ref[h, t] = moved[:, h * hd : (h + 1) * hd]


class Level:
    def __init__(self, index, span, rate, top_rate, fold, order):
        group = len(order)
        self.index = index
        self.rate = rate
        self.count = top_rate // rate
        self.crossing = span > group
        self.bits = span.bit_length() - group.bit_length()
        self.pieces = min(span, group) // fold
        self.segments = 1 if self.crossing else group // span
        self.spots = [order.index(device) // fold for device in range(0, group, fold)]

    def starts(self, offs):
        first = 0 if self.index == 0 else offs[self.index - 1, 0]
        return [first + self.rate * i for i in range(self.count)]

    def places(self, offs_ref, segment):
        low = segment * self.pieces
        spots = self.spots[low : low + self.pieces]
        return [(nb, b) for b in self.starts(offs_ref) for nb in spots]


def gather(read, places):
    return jnp.concatenate([read(nb, b) for nb, b in places], axis=0)


def scores_of(query, key, scale):
    return dot(query, key, NT) * scale


def forward(query, key, value, scale):
    hd = value.shape[1]
    scores = scores_of(query, key, scale)
    top = jnp.max(scores, axis=-1, keepdims=True)
    weights = jnp.exp2(scores - top).astype(BF16)
    both = dot(weights, jnp.concatenate([value, jnp.ones_like(value)], axis=1), NN)
    mixed, total = both[:, :hd], both[:, hd:]
    return mixed / total, top + jnp.log2(total)


def merge(mixed, lse, more, more_lse):
    top = jnp.maximum(lse, more_lse)
    left, right = jnp.exp2(lse - top), jnp.exp2(more_lse - top)
    total = left + right
    return (mixed * left + more * right) / total, top + jnp.log2(total)


def merge_into(o_ref, lse_ref, places, more, more_lse):
    mixed, lse = merge(
        gather(lambda nb, b: o_ref[nb, b], places),
        gather(lambda nb, b: lse_ref[nb, b], places),
        more,
        more_lse,
    )
    put(o_ref, places, mixed)
    put(lse_ref, places, lse)


def put(ref, places, rows):
    size = ref.shape[-2]
    for i, (nb, b) in enumerate(places):
        ref[nb, b] = rows[i * size : (i + 1) * size]


def add(ref, places, rows):
    size = ref.shape[-2]
    for i, (nb, b) in enumerate(places):
        ref[nb, b] += rows[i * size : (i + 1) * size]


def crossing_keys(places, x_ref, other_ref, t):
    found = [x_ref[nb, t, b] for nb, b in places]
    others, pieces, _, count = other_ref.shape[:4]
    found += [
        other_ref[e, nb, t - 1, i]
        for e in range(others)
        for i in range(count)
        for nb in range(pieces)
    ]
    return jnp.concatenate(found, axis=0)


def all_blocks(levels, offs_ref, x_ref, others):
    crossing = 0
    for level in levels:
        if level.crossing:
            other_ref = others[crossing]
            crossing += 1
        for segment in range(level.segments):
            places = level.places(offs_ref, segment)
            query = gather(lambda nb, b: x_ref[nb, 0, b], places)
            if level.crossing:
                key, value = (crossing_keys(places, x_ref, other_ref, t) for t in (1, 2))
            else:
                key, value = (gather(lambda nb, b, t=t: x_ref[nb, t, b], places) for t in (1, 2))
            yield level, places, query, key, value


def row_sums(attn, grad, gain):
    hd = attn.shape[-1]
    attn = attn.astype(BF16).astype(F32)
    scaled = grad.astype(F32) * gain
    total = jnp.sum(attn, axis=-1, keepdims=True)
    away = attn - total * (1.0 / hd)
    return (
        total,
        jnp.sum(away * away, axis=-1, keepdims=True),
        jnp.sum(scaled, axis=-1, keepdims=True),
        jnp.sum(scaled * away, axis=-1, keepdims=True),
    )


def forward_kernel(levels, scale, offs_ref, gain_ref, x_ref, o_ref, lse_ref, table_ref):
    pieces, rate, size, hd = o_ref.shape
    for level, places, query, key, value in all_blocks(levels, offs_ref, x_ref, ()):
        mixed, lse = forward(query, key, value, scale)
        if level.index == 0:
            put(o_ref, places, mixed)
            put(lse_ref, places, lse)
        else:
            merge_into(o_ref, lse_ref, places, mixed, lse)
    per = rate * size // hd
    chunks = pieces * per
    lane = lax.broadcasted_iota(jnp.int32, (hd, hd), 1)
    table = jnp.zeros((hd, hd), F32)
    for nb in range(pieces):
        attn = o_ref[nb].reshape(rate * size, hd)
        grad = x_ref[nb, 3].reshape(rate * size, hd)
        for part in range(per):
            rows = slice(part * hd, (part + 1) * hd)
            for i, column in enumerate(row_sums(attn[rows], grad[rows], gain_ref[...])):
                table = jnp.where(lane == i * chunks + nb * per + part, column, table)
    table_ref[...] = table


def crossing_forward_kernel(levels, scale, offs_ref, gain_ref, x_ref, o_in, lse_in, table_ref, *refs):
    others, (attn_ref, lse_ref, stats_ref, o_ref, sums_ref) = refs[:-5], refs[-5:]
    pieces, rate, size, hd = o_ref.shape
    per = rate * size // hd
    chunks = pieces * per
    lane = lax.broadcasted_iota(jnp.int32, (size, hd), 1)
    o_ref[...] = o_in[...]
    lse_ref[...] = lse_in[...]
    sums_ref[...] = table_ref[...]
    for level, places, query, key, value in all_blocks(levels, offs_ref, x_ref, others):
        merge_into(o_ref, lse_ref, places, *forward(query, key, value, scale))
        sums = row_sums(
            gather(lambda nb, b: o_ref[nb, b], places),
            gather(lambda nb, b: x_ref[nb, 3, b], places),
            gain_ref[...],
        )
        for j, (nb, b) in enumerate(places):
            chunk = nb * per + b * size // hd
            rows = pl.ds(pl.multiple_of(b * size % hd, size), size)
            table = sums_ref[rows, :]
            for i, column in enumerate(sums):
                table = jnp.where(lane == i * chunks + chunk, column[j * size : (j + 1) * size], table)
            sums_ref[rows, :] = table
    attn_ref[...] = o_ref[...].astype(BF16)
    turned = sums_ref[...].T[: 4 * chunks]
    for peer in range(stats_ref.shape[0]):
        stats_ref[peer] = turned


def norm_kernel(heads, levels, scale, score_scale, offs_ref, x_ref, attn_ref, lse_ref, gain_ref, stats_ref, *refs):
    count = len(levels)
    others, refs = refs[:count], refs[count:]
    attended_ref, grad_ref, delta_ref, gsum_ref = refs[:4]
    own_refs, sent_refs = refs[4 : 4 + count], refs[4 + count :]
    pieces, rate, size, hd = attn_ref.shape
    chunks = pieces * rate * size // hd
    per = chunks // pieces
    width = heads * hd
    sums, squares, scaleds, products = (
        [stats_ref[h, i * chunks : (i + 1) * chunks, :] for h in range(heads)] for i in range(4)
    )
    mean = functools.reduce(jnp.add, sums) * (1.0 / width)
    apart = [total * (1.0 / hd) - mean for total in sums]
    variance = functools.reduce(
        jnp.add, [square + hd * a * a for square, a in zip(squares, apart)]
    ) * (1.0 / width)
    inverse = lax.rsqrt(variance + EPSILON)
    first = functools.reduce(jnp.add, scaleds) * (1.0 / width)
    second = (
        functools.reduce(jnp.add, [p + a * s for p, a, s in zip(products, apart, scaleds)])
        * (1.0 / width)
        * inverse
    )
    table = jnp.concatenate(
        [mean, inverse, first, second, jnp.zeros((hd - 4 * chunks, hd), F32)], axis=0
    )
    table = two_parts(table.T)
    lane = lax.broadcasted_iota(jnp.int32, (hd, 2 * hd), 1) % chunks
    picker = lax.broadcasted_iota(jnp.int32, (2 * hd, 4 * hd), 0) % hd // chunks
    picker = (picker == lax.broadcasted_iota(jnp.int32, (2 * hd, 4 * hd), 1) // hd).astype(BF16)
    picked = [jnp.where(lane == chunk, table, jnp.zeros_like(table)) for chunk in range(chunks)]
    columns = dot(jnp.concatenate(picked, axis=0), picker, NN)
    gsum = jnp.zeros((1, hd), F32)
    products = []
    shape = (rate, size, hd)
    for nb in range(pieces):
        attn_all = attn_ref[nb].reshape(rate * size, hd).astype(F32)
        grad_all = x_ref[nb, 3].reshape(rate * size, hd).astype(F32)
        attended, grads = [], []
        for part in range(per):
            chunk = nb * per + part
            mean_c, inv_c, first_c, second_c = (
                columns[chunk * hd : (chunk + 1) * hd, i * hd : (i + 1) * hd] for i in range(4)
            )
            attn = attn_all[part * hd : (part + 1) * hd]
            upstream = grad_all[part * hd : (part + 1) * hd]
            normed = (attn - mean_c) * inv_c
            attended.append((normed * gain_ref[...]).astype(BF16))
            grad = (inv_c * (upstream * gain_ref[...] - first_c - normed * second_c)).astype(BF16)
            grads.append(grad)
            products.append(two_parts(grad.astype(F32) * attn))
            gsum = gsum + jnp.sum(upstream * normed, axis=0, keepdims=True)
        attended_ref[nb] = jnp.concatenate(attended, axis=0).reshape(shape)
        grad_ref[nb] = jnp.concatenate(grads, axis=0).reshape(shape)
    ones = jnp.ones((2 * hd, hd), BF16)
    deltas = dot(jnp.concatenate(products, axis=0), ones, NN)
    for nb in range(pieces):
        delta_ref[nb] = deltas[nb * rate * size : (nb + 1) * rate * size].reshape(shape)
    gsum_ref[...] = gsum
    blocks = list(all_blocks(levels, offs_ref, x_ref, others))
    results = backward(blocks, grad_ref, lse_ref, delta_ref, scale, score_scale)
    for i, parts in enumerate(results):
        own = parts[0].shape[0]
        level, coded = levels[i], three_parts(gsum)
        steps = level.count
        for t, part in enumerate(parts):
            own_refs[i][t] = part[:own]
            if t > 0:
                low = own
                for e in range(sent_refs[i].shape[0]):
                    for step in range(steps):
                        for nb in range(level.pieces):
                            rows = part[low : low + size].astype(sent_refs[i].dtype)
                            sent_refs[i][e, (nb * 2 + t - 1) * steps + step] = rows
                            low += size
                    sent_refs[i][e, 2 * steps * level.pieces] = coded.astype(sent_refs[i].dtype)


def backward(blocks, grad_ref, lse_ref, delta_ref, scale, score_scale):
    def wide(ref, places, key):
        column = gather(lambda nb, b: ref[nb, b], places)
        return jnp.concatenate([column] * (key.shape[0] // column.shape[1]), axis=1)

    grads = [gather(lambda nb, b: grad_ref[nb, b], places) for _, places, _, _, _ in blocks]
    scores = [scores_of(query, key, score_scale) for _, _, query, key, _ in blocks]
    prob_grads = [dot(grad, block[4], NT) for grad, block in zip(grads, blocks)]
    probs = [
        jnp.exp2(score - wide(lse_ref, places, key))
        for score, (_, places, _, key, _) in zip(scores, blocks)
    ]
    score_grads = [
        (prob * (prob_grad - wide(delta_ref, places, key))).astype(BF16)
        for prob, prob_grad, (_, places, _, key, _) in zip(probs, prob_grads, blocks)
    ]
    queries = [dot(each, block[3], NN) * scale for each, block in zip(score_grads, blocks)]
    keys = [dot(each, block[2], TN) * scale for each, block in zip(score_grads, blocks)]
    values = [dot(prob.astype(BF16), grad, TN) for prob, grad in zip(probs, grads)]
    return list(zip(queries, keys, values))


def local_kernel(levels, crossing, scale, score_scale, offs_ref, x_ref, attended_ref, grad_ref, lse_ref, delta_ref, *refs):
    own_refs, (out_ref, kv_ref, dq_ref) = refs[: len(crossing)], refs[len(crossing) :]
    accumulators = (dq_ref, kv_ref.at[0], kv_ref.at[1])
    blocks = list(all_blocks(levels, offs_ref, x_ref, ()))
    for low in range(0, len(blocks), STAGED):
        some = blocks[low : low + STAGED]
        results = backward(some, grad_ref, lse_ref, delta_ref, scale, score_scale)
        for i, ref in enumerate(accumulators):
            for (level, places, *_), parts in zip(some, results):
                (put if level.index == 0 else add)(ref, places, parts[i])
    for level, own_ref in zip(crossing, own_refs):
        places = level.places(offs_ref, 0)
        for t, ref in enumerate(accumulators):
            add(ref, places, own_ref[t])
    out_ref[:, 0] = dq_ref[...].astype(BF16)
    out_ref[:, 1] = attended_ref[...]


def pack_kernel(crossing, fold, sums, offs_ref, main_ref, kv_in, *refs):
    gsum_refs, arrived_refs, (out_ref, kv_ref) = refs[:sums], refs[sums:-2], refs[-2:]
    pieces, _, rate, size, hd = main_ref.shape
    rows = rate * size
    kv_ref[...] = kv_in[...]
    for level, arrived_ref in zip(crossing, arrived_refs):
        for i, b in enumerate(level.starts(offs_ref)):
            for nb in range(level.pieces):
                for t in range(2):
                    block = (nb * 2 + t) * level.count + i
                    kv_ref[t, nb, b] += arrived_ref[block].astype(F32)
    total = functools.reduce(jnp.add, [ref[...] for ref in gsum_refs])
    if sums > 1:
        other = arrived_refs[0][arrived_refs[0].shape[0] - 1]
        total = total + jnp.sum(other.astype(F32), axis=0, keepdims=True)
    coded = three_parts(total)
    for nb in range(pieces):
        for t in range(2):
            out_ref[nb, t * rows : (t + 1) * rows] = main_ref[nb, t].reshape(rows, hd)
            out_ref[nb, (t + 2) * rows : (t + 3) * rows] = (
                kv_ref[t, nb].reshape(rows, hd).astype(BF16)
            )
        for f in range(fold):
            out_ref[nb, 4 * rows + f * TILE : 4 * rows + (f + 1) * TILE] = coded


def join_kernel(rate, factor, in_ref, dq_ref, attended_ref, dk_ref, dv_ref, gain_ref):
    group, _, hd = in_ref.shape
    tokens = dq_ref.shape[1]
    order = row_order(tokens, rate, True)
    for t, ref in enumerate((dq_ref, attended_ref, dk_ref, dv_ref)):
        for h in range(group):
            moved = dot(order, in_ref[h, t * tokens : (t + 1) * tokens, :], NN)
            ref[0, :, h * hd : (h + 1) * hd] = moved.astype(BF16)
    for h in range(group):
        coded = in_ref[h, 4 * tokens : 4 * tokens + TILE, :].astype(F32)
        gain_ref[:, h * hd : (h + 1) * hd] = jnp.sum(coded, axis=0, keepdims=True) * factor


VMEM = pl.BlockSpec(memory_space=pltpu.VMEM)


def call(body, name, inputs, outputs, scratch=(), flops=0, limit=24):
    shapes = [jax.ShapeDtypeStruct(*output) for output in outputs]
    moved = sum(x.size * x.dtype.itemsize for x in list(inputs) + shapes)
    return list(pl.pallas_call(
        body,
        name=name,
        in_specs=[VMEM] * len(inputs),
        out_specs=[VMEM] * len(shapes),
        out_shape=shapes,
        scratch_shapes=[pltpu.VMEM(*each) for each in scratch],
        cost_estimate=pl.CostEstimate(flops=flops, bytes_accessed=moved, transcendentals=0),
        compiler_params=pltpu.CompilerParams(vmem_limit_bytes=limit * 1024 * 1024),
    )(*inputs))


def flip(value, axis, bit):
    pairs = [(source, source ^ (1 << bit)) for source in range(lax.axis_size(axis))]
    return lax.ppermute(value, axis, pairs)


def cross(value):
    ctx_count, dp_count = lax.axis_size("ctx"), lax.axis_size("dp")
    count = ctx_count * dp_count
    far = ctx_count // 2 * dp_count + dp_count // 2
    pairs = [(source, source ^ far) for source in range(count)]
    return lax.ppermute(value, ("ctx", "dp"), pairs)


def shards(queries, key_rows, value_rows, out_grad, norm_gain, offsets):
    tokens, width = queries.shape[1:]
    group = offsets.shape[1]
    hd = width // group
    ctx_count = lax.axis_size("ctx")
    dp_count = lax.axis_size("dp")
    scale = hd ** (-0.5)
    score_scale = scale * LOG2E
    spans = [
        (SPAN_A, RATE_A),
        (SPAN_B, RATE_B),
        (SPAN_C, RATE_C),
        (ctx_count // 2, ctx_count // 4),
    ]
    rate = max(r for _, r in spans)
    short = tokens // rate
    fold = max(1, TILE // short)
    size = short * fold
    pieces = group // fold
    order = list(ORDER) if group == len(ORDER) and fold == 1 else list(range(group))
    levels = [Level(i, span, r, rate, fold, order) for i, (span, r) in enumerate(spans)]
    local = [level for level in levels if not level.crossing]
    crossing = [level for level in levels if level.crossing]
    groups = [[low + device for device in order] for low in range(0, ctx_count, group)]
    low_bit = group.bit_length() - 1

    def exchange(value):
        return lax.all_to_all(value, "ctx", 0, 0, tiled=True, axis_index_groups=groups)

    place = lax.axis_index("ctx") % group
    head = sum(order.index(device) * (place == device) for device in range(group))
    offs = lax.dynamic_slice(offsets, (0, head), (offsets.shape[0], 1))
    offs_rows = jnp.broadcast_to(offs, (offsets.shape[0], hd))
    gain = lax.dynamic_slice(norm_gain, (head * hd,), (hd,))[None]

    (sent,) = call(
        functools.partial(split_kernel, rate),
        "split",
        [queries, key_rows, value_rows, out_grad],
        [((group, 4, tokens, hd), BF16)],
        limit=60,
    )
    x = exchange(sent)
    if fold > 1:
        x = x.reshape(pieces, fold, 4, rate, short, hd).transpose(0, 2, 3, 1, 4, 5)
    x = x.reshape(pieces, 4, rate, size, hd)

    others = []
    for level in crossing:
        own = [
            lax.dynamic_slice(x, (0, 1, b, 0, 0), (pieces, 2, 1, size, hd))
            for b in level.starts(offs)
        ]
        blocks = [jnp.concatenate(own, axis=2)]
        for bit in range(level.bits):
            blocks += [flip(block, "ctx", low_bit + bit) for block in blocks]
        others.append(jnp.stack(blocks[1:]))

    state = (pieces, rate, size, hd)
    chunks = group * tokens // hd
    o, lse, table = call(
        functools.partial(forward_kernel, local, score_scale),
        "local_forward",
        [offs_rows, gain, x],
        [(state, F32), (state, F32), ((hd, hd), F32)],
        flops=10**8,
    )
    attn, lse, stats = call(
        functools.partial(crossing_forward_kernel, crossing, score_scale),
        "crossing_forward",
        [offs_rows, gain, x, o, lse, table] + others,
        [(state, BF16), (state, F32), ((group, 4 * chunks, hd), F32)],
        scratch=[(state, F32), ((hd, hd), F32)],
    )
    stats = exchange(stats)
    outs = [(state, BF16), (state, BF16), (state, F32), ((1, hd), F32)]
    outs += [((3, pieces * level.count * size, hd), F32) for level in crossing]
    sent_types = [BF16 if level.bits == 1 else F32 for level in crossing]
    outs += [
        ((other.shape[0], 2 * level.pieces * level.count + 1, size, hd), kind)
        for level, other, kind in zip(crossing, others, sent_types)
    ]
    attended, grad, delta, gsum, *rest = call(
        functools.partial(norm_kernel, group, crossing, scale, score_scale),
        "norm_and_crossing",
        [offs_rows, x, attn, lse, gain, stats] + others,
        outs,
        flops=10**7,
    )
    owns, parts = rest[: len(crossing)], rest[len(crossing) :]

    arrived = []
    for level, part in zip(crossing, parts):
        partial = [None] + [part[e] for e in range(part.shape[0])]
        for bit in reversed(range(level.bits)):
            half = 1 << bit
            came = [flip(block.astype(BF16), "ctx", low_bit + bit) for block in partial[half:]]
            partial = [
                c if b is None else b.astype(F32) + c.astype(F32)
                for b, c in zip(partial[:half], came)
            ]
        arrived.append(partial[0])
    alone = ctx_count == 2 * group and dp_count == 2 and size == TILE and len(crossing) == 1
    gsums = [gsum]
    if alone:
        gsums += [flip(gsum, "dp", 0), cross(gsum)]
    else:
        for axis, count, first in (("dp", dp_count, 0), ("ctx", ctx_count, low_bit)):
            for bit in range(first, count.bit_length() - 1):
                gsums = [gsums[0] + flip(gsums[0], axis, bit)]

    main, kv = call(
        functools.partial(local_kernel, local, crossing, scale, score_scale),
        "local_backward",
        [offs_rows, x, attended, grad, lse, delta] + owns,
        [((pieces, 2, rate, size, hd), BF16), ((2,) + state, F32)],
        scratch=[(state, F32)],
        flops=3 * 10**8,
    )
    (packed,) = call(
        functools.partial(pack_kernel, crossing, fold, len(gsums)),
        "pack",
        [offs_rows, main, kv] + gsums + arrived,
        [((pieces, 4 * rate * size + TILE * fold, hd), BF16)],
        scratch=[((2,) + state, F32)],
    )
    if fold > 1:
        rows = packed[:, : 4 * rate * size].reshape(pieces, 4, rate, fold, short, hd)
        rows = rows.transpose(0, 3, 1, 2, 4, 5).reshape(group, 4 * tokens, hd)
        packed = jnp.concatenate([rows, packed[:, 4 * rate * size :].reshape(group, TILE, hd)], 1)
    back = exchange(packed)
    factor = 1.0 / math.sqrt(ctx_count * dp_count * tokens)
    row = ((1, tokens, width), BF16)
    dq, attended, dk, dv, gain_grad = call(
        functools.partial(join_kernel, rate, factor),
        "join",
        [back],
        [row, row, row, row, ((1, width), F32)],
    )
    return attended, dq, dk, dv, gain_grad[0]


def solution(mesh):
    rows = P("dp", "ctx", None)
    return jax.shard_map(
        shards,
        mesh=mesh,
        in_specs=(rows, rows, rows, rows, P(), P()),
        out_specs=(rows, rows, rows, rows, P()),
        check_vma=False,
    )
```

```python
import functools
import math

import jax
import jax.numpy as jnp
from jax import lax
from jax.experimental import pallas as pl
from jax.experimental.pallas import tpu as pltpu
from jax.sharding import PartitionSpec as P

SPAN_A = 2
RATE_A = 1
SPAN_B = 4
RATE_B = 2
SPAN_C = 16
RATE_C = 8

EPSILON = 1e-05
LOG2E = math.log2(math.e)
TILE = 16
STAGED = 4
ORDER = (0, 7, 2, 6, 1, 5, 4, 3)
F32 = jnp.float32
BF16 = jnp.bfloat16

NT = (((1,), (1,)), ((), ()))
TN = (((0,), (0,)), ((), ()))
NN = (((1,), (0,)), ((), ()))


def dot(left, right, dims):
    return lax.dot_general(left, right, dims, preferred_element_type=F32)


def two_parts(value):
    high = value.astype(BF16)
    return jnp.concatenate([high, (value - high.astype(F32)).astype(BF16)], axis=1)


def three_parts(row):
    total = jnp.broadcast_to(row, (TILE, row.shape[1]))
    high = total.astype(BF16).astype(F32)
    middle = (total - high).astype(BF16).astype(F32)
    low = total - high - middle
    place = lax.broadcasted_iota(jnp.int32, total.shape, 0)
    parts = jnp.where(place == 0, high, jnp.where(place == 1, middle, low))
    return jnp.where(place < 3, parts, 0.0).astype(BF16)


def row_order(tokens, rate, transposed):
    short = tokens // rate
    placed = lax.broadcasted_iota(jnp.int32, (tokens, tokens), 1 if transposed else 0)
    source = lax.broadcasted_iota(jnp.int32, (tokens, tokens), 0 if transposed else 1)
    return (source == (placed % short) * rate + placed // short).astype(BF16)


def split_kernel(rate, q_ref, k_ref, v_ref, g_ref, out_ref):
    group, _, tokens, hd = out_ref.shape
    order = row_order(tokens, rate, False)
    for t, ref in enumerate((q_ref, k_ref, v_ref, g_ref)):
        moved = dot(order, ref[0], NN).astype(BF16)
        for h in range(group):
            out_ref[h, t] = moved[:, h * hd : (h + 1) * hd]


class Level:
    def __init__(self, index, span, rate, top_rate, fold, order):
        group = len(order)
        self.index = index
        self.rate = rate
        self.count = top_rate // rate
        self.crossing = span > group
        self.bits = span.bit_length() - group.bit_length()
        self.pieces = min(span, group) // fold
        self.segments = 1 if self.crossing else group // span
        self.spots = [order.index(device) // fold for device in range(0, group, fold)]

    def starts(self, offs):
        first = 0 if self.index == 0 else offs[self.index - 1, 0]
        return [first + self.rate * i for i in range(self.count)]

    def places(self, offs_ref, segment):
        low = segment * self.pieces
        spots = self.spots[low : low + self.pieces]
        return [(nb, b) for b in self.starts(offs_ref) for nb in spots]


def gather(read, places):
    return jnp.concatenate([read(nb, b) for nb, b in places], axis=0)


def scores_of(query, key, scale):
    return dot(query, key, NT) * scale


def forward(query, key, value, scale):
    hd = value.shape[1]
    scores = scores_of(query, key, scale)
    top = jnp.max(scores, axis=-1, keepdims=True)
    weights = jnp.exp2(scores - top).astype(BF16)
    both = dot(weights, jnp.concatenate([value, jnp.ones_like(value)], axis=1), NN)
    mixed, total = both[:, :hd], both[:, hd:]
    return mixed / total, top + jnp.log2(total)


def merge(mixed, lse, more, more_lse):
    top = jnp.maximum(lse, more_lse)
    left, right = jnp.exp2(lse - top), jnp.exp2(more_lse - top)
    total = left + right
    return (mixed * left + more * right) / total, top + jnp.log2(total)


def merge_into(o_ref, lse_ref, places, more, more_lse):
    mixed, lse = merge(
        gather(lambda nb, b: o_ref[nb, b], places),
        gather(lambda nb, b: lse_ref[nb, b], places),
        more,
        more_lse,
    )
    put(o_ref, places, mixed)
    put(lse_ref, places, lse)


def put(ref, places, rows):
    size = ref.shape[-2]
    for i, (nb, b) in enumerate(places):
        ref[nb, b] = rows[i * size : (i + 1) * size]


def add(ref, places, rows):
    size = ref.shape[-2]
    for i, (nb, b) in enumerate(places):
        ref[nb, b] += rows[i * size : (i + 1) * size]


def crossing_keys(places, x_ref, other_ref, t):
    found = [x_ref[nb, t, b] for nb, b in places]
    others, pieces, _, count = other_ref.shape[:4]
    found += [
        other_ref[e, nb, t - 1, i]
        for e in range(others)
        for i in range(count)
        for nb in range(pieces)
    ]
    return jnp.concatenate(found, axis=0)


def all_blocks(levels, offs_ref, x_ref, others):
    crossing = 0
    for level in levels:
        if level.crossing:
            other_ref = others[crossing]
            crossing += 1
        for segment in range(level.segments):
            places = level.places(offs_ref, segment)
            query = gather(lambda nb, b: x_ref[nb, 0, b], places)
            if level.crossing:
                key, value = (crossing_keys(places, x_ref, other_ref, t) for t in (1, 2))
            else:
                key, value = (gather(lambda nb, b, t=t: x_ref[nb, t, b], places) for t in (1, 2))
            yield level, places, query, key, value


def row_sums(attn, grad, gain):
    hd = attn.shape[-1]
    attn = attn.astype(BF16).astype(F32)
    scaled = grad.astype(F32) * gain
    total = jnp.sum(attn, axis=-1, keepdims=True)
    away = attn - total * (1.0 / hd)
    return (
        total,
        jnp.sum(away * away, axis=-1, keepdims=True),
        jnp.sum(scaled, axis=-1, keepdims=True),
        jnp.sum(scaled * away, axis=-1, keepdims=True),
    )


def forward_kernel(levels, scale, offs_ref, gain_ref, x_ref, o_ref, lse_ref, table_ref):
    pieces, rate, size, hd = o_ref.shape
    for level, places, query, key, value in all_blocks(levels, offs_ref, x_ref, ()):
        mixed, lse = forward(query, key, value, scale)
        if level.index == 0:
            put(o_ref, places, mixed)
            put(lse_ref, places, lse)
        else:
            merge_into(o_ref, lse_ref, places, mixed, lse)
    per = rate * size // hd
    chunks = pieces * per
    lane = lax.broadcasted_iota(jnp.int32, (hd, hd), 1)
    table = jnp.zeros((hd, hd), F32)
    for nb in range(pieces):
        attn = o_ref[nb].reshape(rate * size, hd)
        grad = x_ref[nb, 3].reshape(rate * size, hd)
        for part in range(per):
            rows = slice(part * hd, (part + 1) * hd)
            for i, column in enumerate(row_sums(attn[rows], grad[rows], gain_ref[...])):
                table = jnp.where(lane == i * chunks + nb * per + part, column, table)
    table_ref[...] = table


def crossing_forward_kernel(levels, scale, offs_ref, gain_ref, x_ref, o_in, lse_in, table_ref, *refs):
    others, (attn_ref, lse_ref, stats_ref, o_ref, sums_ref) = refs[:-5], refs[-5:]
    pieces, rate, size, hd = o_ref.shape
    per = rate * size // hd
    chunks = pieces * per
    lane = lax.broadcasted_iota(jnp.int32, (size, hd), 1)
    o_ref[...] = o_in[...]
    lse_ref[...] = lse_in[...]
    sums_ref[...] = table_ref[...]
    for level, places, query, key, value in all_blocks(levels, offs_ref, x_ref, others):
        merge_into(o_ref, lse_ref, places, *forward(query, key, value, scale))
        sums = row_sums(
            gather(lambda nb, b: o_ref[nb, b], places),
            gather(lambda nb, b: x_ref[nb, 3, b], places),
            gain_ref[...],
        )
        for j, (nb, b) in enumerate(places):
            chunk = nb * per + b * size // hd
            rows = pl.ds(pl.multiple_of(b * size % hd, size), size)
            table = sums_ref[rows, :]
            for i, column in enumerate(sums):
                table = jnp.where(lane == i * chunks + chunk, column[j * size : (j + 1) * size], table)
            sums_ref[rows, :] = table
    attn_ref[...] = o_ref[...].astype(BF16)
    turned = sums_ref[...].T[: 4 * chunks]
    for peer in range(stats_ref.shape[0]):
        stats_ref[peer] = turned


def norm_kernel(heads, levels, scale, score_scale, offs_ref, x_ref, attn_ref, lse_ref, gain_ref, stats_ref, *refs):
    count = len(levels)
    others, refs = refs[:count], refs[count:]
    attended_ref, grad_ref, delta_ref, gsum_ref = refs[:4]
    own_refs, sent_refs = refs[4 : 4 + count], refs[4 + count :]
    pieces, rate, size, hd = attn_ref.shape
    chunks = pieces * rate * size // hd
    per = chunks // pieces
    width = heads * hd
    sums, squares, scaleds, products = (
        [stats_ref[h, i * chunks : (i + 1) * chunks, :] for h in range(heads)] for i in range(4)
    )
    mean = functools.reduce(jnp.add, sums) * (1.0 / width)
    apart = [total * (1.0 / hd) - mean for total in sums]
    variance = functools.reduce(
        jnp.add, [square + hd * a * a for square, a in zip(squares, apart)]
    ) * (1.0 / width)
    inverse = lax.rsqrt(variance + EPSILON)
    first = functools.reduce(jnp.add, scaleds) * (1.0 / width)
    second = (
        functools.reduce(jnp.add, [p + a * s for p, a, s in zip(products, apart, scaleds)])
        * (1.0 / width)
        * inverse
    )
    table = jnp.concatenate(
        [mean, inverse, first, second, jnp.zeros((hd - 4 * chunks, hd), F32)], axis=0
    )
    table = two_parts(table.T)
    lane = lax.broadcasted_iota(jnp.int32, (hd, 2 * hd), 1) % chunks
    picker = lax.broadcasted_iota(jnp.int32, (2 * hd, 4 * hd), 0) % hd // chunks
    picker = (picker == lax.broadcasted_iota(jnp.int32, (2 * hd, 4 * hd), 1) // hd).astype(BF16)
    picked = [jnp.where(lane == chunk, table, jnp.zeros_like(table)) for chunk in range(chunks)]
    columns = dot(jnp.concatenate(picked, axis=0), picker, NN)
    gsum = jnp.zeros((1, hd), F32)
    products = []
    shape = (rate, size, hd)
    for nb in range(pieces):
        attn_all = attn_ref[nb].reshape(rate * size, hd).astype(F32)
        grad_all = x_ref[nb, 3].reshape(rate * size, hd).astype(F32)
        attended, grads = [], []
        for part in range(per):
            chunk = nb * per + part
            mean_c, inv_c, first_c, second_c = (
                columns[chunk * hd : (chunk + 1) * hd, i * hd : (i + 1) * hd] for i in range(4)
            )
            attn = attn_all[part * hd : (part + 1) * hd]
            upstream = grad_all[part * hd : (part + 1) * hd]
            normed = (attn - mean_c) * inv_c
            attended.append((normed * gain_ref[...]).astype(BF16))
            grad = (inv_c * (upstream * gain_ref[...] - first_c - normed * second_c)).astype(BF16)
            grads.append(grad)
            products.append(two_parts(grad.astype(F32) * attn))
            gsum = gsum + jnp.sum(upstream * normed, axis=0, keepdims=True)
        attended_ref[nb] = jnp.concatenate(attended, axis=0).reshape(shape)
        grad_ref[nb] = jnp.concatenate(grads, axis=0).reshape(shape)
    ones = jnp.ones((2 * hd, hd), BF16)
    deltas = dot(jnp.concatenate(products, axis=0), ones, NN)
    for nb in range(pieces):
        delta_ref[nb] = deltas[nb * rate * size : (nb + 1) * rate * size].reshape(shape)
    gsum_ref[...] = gsum
    blocks = list(all_blocks(levels, offs_ref, x_ref, others))
    results = backward(blocks, grad_ref, lse_ref, delta_ref, scale, score_scale)
    for i, parts in enumerate(results):
        own = parts[0].shape[0]
        level, coded = levels[i], three_parts(gsum)
        steps = level.count
        for t, part in enumerate(parts):
            own_refs[i][t] = part[:own]
            if t > 0:
                low = own
                for e in range(sent_refs[i].shape[0]):
                    for step in range(steps):
                        for nb in range(level.pieces):
                            rows = part[low : low + size].astype(sent_refs[i].dtype)
                            sent_refs[i][e, (nb * 2 + t - 1) * steps + step] = rows
                            low += size
                    sent_refs[i][e, 2 * steps * level.pieces] = coded.astype(sent_refs[i].dtype)


def backward(blocks, grad_ref, lse_ref, delta_ref, scale, score_scale):
    def wide(ref, places, key):
        column = gather(lambda nb, b: ref[nb, b], places)
        return jnp.concatenate([column] * (key.shape[0] // column.shape[1]), axis=1)

    grads = [gather(lambda nb, b: grad_ref[nb, b], places) for _, places, _, _, _ in blocks]
    scores = [scores_of(query, key, score_scale) for _, _, query, key, _ in blocks]
    prob_grads = [dot(grad, block[4], NT) for grad, block in zip(grads, blocks)]
    probs = [
        jnp.exp2(score - wide(lse_ref, places, key))
        for score, (_, places, _, key, _) in zip(scores, blocks)
    ]
    score_grads = [
        (prob * (prob_grad - wide(delta_ref, places, key))).astype(BF16)
        for prob, prob_grad, (_, places, _, key, _) in zip(probs, prob_grads, blocks)
    ]
    queries = [dot(each, block[3], NN) * scale for each, block in zip(score_grads, blocks)]
    keys = [dot(each, block[2], TN) * scale for each, block in zip(score_grads, blocks)]
    values = [dot(prob.astype(BF16), grad, TN) for prob, grad in zip(probs, grads)]
    return list(zip(queries, keys, values))


def local_kernel(levels, crossing, scale, score_scale, offs_ref, x_ref, attended_ref, grad_ref, lse_ref, delta_ref, *refs):
    own_refs, (out_ref, kv_ref, dq_ref) = refs[: len(crossing)], refs[len(crossing) :]
    accumulators = (dq_ref, kv_ref.at[0], kv_ref.at[1])
    blocks = list(all_blocks(levels, offs_ref, x_ref, ()))
    for low in range(0, len(blocks), STAGED):
        some = blocks[low : low + STAGED]
        results = backward(some, grad_ref, lse_ref, delta_ref, scale, score_scale)
        for i, ref in enumerate(accumulators):
            for (level, places, *_), parts in zip(some, results):
                (put if level.index == 0 else add)(ref, places, parts[i])
    for level, own_ref in zip(crossing, own_refs):
        places = level.places(offs_ref, 0)
        for t, ref in enumerate(accumulators):
            add(ref, places, own_ref[t])
    out_ref[:, 0] = dq_ref[...].astype(BF16)
    out_ref[:, 1] = attended_ref[...]


def pack_kernel(crossing, fold, alone, offs_ref, main_ref, kv_in, gsum_ref, *refs):
    arrived_refs, (out_ref, kv_ref) = refs[:-2], refs[-2:]
    pieces, _, rate, size, hd = main_ref.shape
    rows = rate * size
    kv_ref[...] = kv_in[...]
    for level, arrived_ref in zip(crossing, arrived_refs):
        for i, b in enumerate(level.starts(offs_ref)):
            for nb in range(level.pieces):
                for t in range(2):
                    block = (nb * 2 + t) * level.count + i
                    kv_ref[t, nb, b] += arrived_ref[block].astype(F32)
    total = gsum_ref[...]
    if alone:
        other = arrived_refs[0][arrived_refs[0].shape[0] - 1]
        total = total + jnp.sum(other.astype(F32), axis=0, keepdims=True)
    coded = three_parts(total)
    for nb in range(pieces):
        for t in range(2):
            out_ref[nb, t * rows : (t + 1) * rows] = main_ref[nb, t].reshape(rows, hd)
            out_ref[nb, (t + 2) * rows : (t + 3) * rows] = (
                kv_ref[t, nb].reshape(rows, hd).astype(BF16)
            )
        for f in range(fold):
            out_ref[nb, 4 * rows + f * TILE : 4 * rows + (f + 1) * TILE] = coded


def join_kernel(rate, in_ref, dq_ref, attended_ref, dk_ref, dv_ref):
    group, _, hd = in_ref.shape
    tokens = dq_ref.shape[1]
    order = row_order(tokens, rate, True)
    for t, ref in enumerate((dq_ref, attended_ref, dk_ref, dv_ref)):
        for h in range(group):
            moved = dot(order, in_ref[h, t * tokens : (t + 1) * tokens, :], NN)
            ref[0, :, h * hd : (h + 1) * hd] = moved.astype(BF16)


VMEM = pl.BlockSpec(memory_space=pltpu.VMEM)


def call(body, name, inputs, outputs, scratch=(), flops=0, limit=24):
    shapes = [jax.ShapeDtypeStruct(*output) for output in outputs]
    moved = sum(x.size * x.dtype.itemsize for x in list(inputs) + shapes)
    return list(pl.pallas_call(
        body,
        name=name,
        in_specs=[VMEM] * len(inputs),
        out_specs=[VMEM] * len(shapes),
        out_shape=shapes,
        scratch_shapes=[pltpu.VMEM(*each) for each in scratch],
        cost_estimate=pl.CostEstimate(flops=flops, bytes_accessed=moved, transcendentals=0),
        compiler_params=pltpu.CompilerParams(vmem_limit_bytes=limit * 1024 * 1024),
    )(*inputs))


def flip(value, axis, bit):
    pairs = [(source, source ^ (1 << bit)) for source in range(lax.axis_size(axis))]
    return lax.ppermute(value, axis, pairs)


def shards(queries, key_rows, value_rows, out_grad, norm_gain, offsets):
    tokens, width = queries.shape[1:]
    group = offsets.shape[1]
    hd = width // group
    ctx_count = lax.axis_size("ctx")
    dp_count = lax.axis_size("dp")
    scale = hd ** (-0.5)
    score_scale = scale * LOG2E
    spans = [
        (SPAN_A, RATE_A),
        (SPAN_B, RATE_B),
        (SPAN_C, RATE_C),
        (ctx_count // 2, ctx_count // 4),
    ]
    rate = max(r for _, r in spans)
    short = tokens // rate
    fold = max(1, TILE // short)
    size = short * fold
    pieces = group // fold
    order = list(ORDER) if group == len(ORDER) and fold == 1 else list(range(group))
    levels = [Level(i, span, r, rate, fold, order) for i, (span, r) in enumerate(spans)]
    local = [level for level in levels if not level.crossing]
    crossing = [level for level in levels if level.crossing]
    groups = [[low + device for device in order] for low in range(0, ctx_count, group)]
    low_bit = group.bit_length() - 1

    def exchange(value):
        return lax.all_to_all(value, "ctx", 0, 0, tiled=True, axis_index_groups=groups)

    place = lax.axis_index("ctx") % group
    head = sum(order.index(device) * (place == device) for device in range(group))
    offs = lax.dynamic_slice(offsets, (0, head), (offsets.shape[0], 1))
    offs_rows = jnp.broadcast_to(offs, (offsets.shape[0], hd))
    gain = lax.dynamic_slice(norm_gain, (head * hd,), (hd,))[None]

    (sent,) = call(
        functools.partial(split_kernel, rate),
        "split",
        [queries, key_rows, value_rows, out_grad],
        [((group, 4, tokens, hd), BF16)],
        limit=60,
    )
    x = exchange(sent)
    if fold > 1:
        x = x.reshape(pieces, fold, 4, rate, short, hd).transpose(0, 2, 3, 1, 4, 5)
    x = x.reshape(pieces, 4, rate, size, hd)

    others = []
    for level in crossing:
        own = [
            lax.dynamic_slice(x, (0, 1, b, 0, 0), (pieces, 2, 1, size, hd))
            for b in level.starts(offs)
        ]
        blocks = [jnp.concatenate(own, axis=2)]
        for bit in range(level.bits):
            blocks += [flip(block, "ctx", low_bit + bit) for block in blocks]
        others.append(jnp.stack(blocks[1:]))

    state = (pieces, rate, size, hd)
    chunks = group * tokens // hd
    o, lse, table = call(
        functools.partial(forward_kernel, local, score_scale),
        "local_forward",
        [offs_rows, gain, x],
        [(state, F32), (state, F32), ((hd, hd), F32)],
        flops=10**8,
    )
    attn, lse, stats = call(
        functools.partial(crossing_forward_kernel, crossing, score_scale),
        "crossing_forward",
        [offs_rows, gain, x, o, lse, table] + others,
        [(state, BF16), (state, F32), ((group, 4 * chunks, hd), F32)],
        scratch=[(state, F32), ((hd, hd), F32)],
    )
    stats = exchange(stats)
    outs = [(state, BF16), (state, BF16), (state, F32), ((1, hd), F32)]
    outs += [((3, pieces * level.count * size, hd), F32) for level in crossing]
    sent_types = [BF16 if level.bits == 1 else F32 for level in crossing]
    outs += [
        ((other.shape[0], 2 * level.pieces * level.count + 1, size, hd), kind)
        for level, other, kind in zip(crossing, others, sent_types)
    ]
    attended, grad, delta, gsum, *rest = call(
        functools.partial(norm_kernel, group, crossing, scale, score_scale),
        "norm_and_crossing",
        [offs_rows, x, attn, lse, gain, stats] + others,
        outs,
        flops=10**7,
    )
    owns, parts = rest[: len(crossing)], rest[len(crossing) :]

    arrived = []
    for level, part in zip(crossing, parts):
        partial = [None] + [part[e] for e in range(part.shape[0])]
        for bit in reversed(range(level.bits)):
            half = 1 << bit
            came = [flip(block.astype(BF16), "ctx", low_bit + bit) for block in partial[half:]]
            partial = [
                c if b is None else b.astype(F32) + c.astype(F32)
                for b, c in zip(partial[:half], came)
            ]
        arrived.append(partial[0])
    alone = ctx_count == 2 * group and dp_count == 2 and size == TILE and len(crossing) == 1
    if not alone:
        for axis, count, first in (("dp", dp_count, 0), ("ctx", ctx_count, low_bit)):
            for bit in range(first, count.bit_length() - 1):
                gsum = gsum + flip(gsum, axis, bit)

    main, kv = call(
        functools.partial(local_kernel, local, crossing, scale, score_scale),
        "local_backward",
        [offs_rows, x, attended, grad, lse, delta] + owns,
        [((pieces, 2, rate, size, hd), BF16), ((2,) + state, F32)],
        scratch=[(state, F32)],
        flops=3 * 10**8,
    )
    (packed,) = call(
        functools.partial(pack_kernel, crossing, fold, alone),
        "pack",
        [offs_rows, main, kv, gsum] + arrived,
        [((pieces, 4 * rate * size + TILE * fold, hd), BF16)],
        scratch=[((2,) + state, F32)],
    )
    if fold > 1:
        rows = packed[:, : 4 * rate * size].reshape(pieces, 4, rate, fold, short, hd)
        rows = rows.transpose(0, 3, 1, 2, 4, 5).reshape(group, 4 * tokens, hd)
        packed = jnp.concatenate([rows, packed[:, 4 * rate * size :].reshape(group, TILE, hd)], 1)
    back = exchange(packed)
    gains = jnp.sum(back[:, 4 * tokens :].astype(F32), axis=1)
    if alone:
        gains = gains + flip(gains, "dp", 0)
    gain_grad = gains.reshape(width) / math.sqrt(ctx_count * dp_count * tokens)
    row = ((1, tokens, width), BF16)
    dq, attended, dk, dv = call(
        functools.partial(join_kernel, rate),
        "join",
        [back],
        [row, row, row, row],
        flops=10**8,
    )
    return attended, dq, dk, dv, gain_grad


def solution(mesh):
    rows = P("dp", "ctx", None)
    return jax.shard_map(
        shards,
        mesh=mesh,
        in_specs=(rows, rows, rows, rows, P(), P()),
        out_specs=(rows, rows, rows, rows, P()),
        check_vma=False,
    )
```

```python
import functools
import math

import jax
import jax.numpy as jnp
from jax import lax
from jax.experimental import pallas as pl
from jax.experimental.pallas import tpu as pltpu
from jax.sharding import PartitionSpec as P

SPAN_A = 2
RATE_A = 1
SPAN_B = 4
RATE_B = 2
SPAN_C = 16
RATE_C = 8

EPSILON = 1e-05
LOG2E = math.log2(math.e)
TILE = 16
STAGED = 4
ORDER = (0, 7, 2, 6, 1, 5, 4, 3)
FAR_FIRST = (7, 6, 5, 3, 4, 2, 1)
F32 = jnp.float32
BF16 = jnp.bfloat16

NT = (((1,), (1,)), ((), ()))
TN = (((0,), (0,)), ((), ()))
NN = (((1,), (0,)), ((), ()))


def dot(left, right, dims):
    return lax.dot_general(left, right, dims, preferred_element_type=F32)


def two_parts(value):
    high = value.astype(BF16)
    return jnp.concatenate([high, (value - high.astype(F32)).astype(BF16)], axis=1)


def three_parts(row):
    total = jnp.broadcast_to(row, (TILE, row.shape[1]))
    high = total.astype(BF16).astype(F32)
    middle = (total - high).astype(BF16).astype(F32)
    low = total - high - middle
    place = lax.broadcasted_iota(jnp.int32, total.shape, 0)
    parts = jnp.where(place == 0, high, jnp.where(place == 1, middle, low))
    return jnp.where(place < 3, parts, 0.0).astype(BF16)


def row_order(tokens, rate, transposed):
    short = tokens // rate
    placed = lax.broadcasted_iota(jnp.int32, (tokens, tokens), 1 if transposed else 0)
    source = lax.broadcasted_iota(jnp.int32, (tokens, tokens), 0 if transposed else 1)
    return (source == (placed % short) * rate + placed // short).astype(BF16)


def split_kernel(rate, q_ref, k_ref, v_ref, g_ref, out_ref):
    group, _, tokens, hd = out_ref.shape
    order = row_order(tokens, rate, False)
    for t, ref in enumerate((q_ref, k_ref, v_ref, g_ref)):
        moved = dot(order, ref[0], NN).astype(BF16)
        for h in range(group):
            out_ref[h, t] = moved[:, h * hd : (h + 1) * hd]


def head_at(order, apart):
    place = lax.axis_index("ctx") % len(order) ^ apart
    return sum(order.index(device) * (place == device) for device in range(len(order)))


def split_apart_kernel(rate, order, q_ref, k_ref, v_ref, g_ref, *refs):
    outs, moved_ref = refs[:-1], refs[-1]
    group, _, tokens, hd = moved_ref.shape
    change = row_order(tokens, rate, False)
    for t, ref in enumerate((q_ref, k_ref, v_ref, g_ref)):
        moved = dot(change, ref[0], NN).astype(BF16)
        for h in range(group):
            moved_ref[h, t] = moved[:, h * hd : (h + 1) * hd]
    for apart, out_ref in enumerate(outs):
        out_ref[...] = moved_ref[head_at(order, apart)]


def collect_kernel(levels, order, offs_ref, *refs):
    blocks, x_ref, own_refs = refs[: len(order)], refs[len(order)], refs[len(order) + 1 :]
    for apart, block_ref in enumerate(blocks):
        spot = head_at(order, apart)
        x_ref[spot] = block_ref[...]
        for level, own_ref in zip(levels, own_refs):
            for i, b in enumerate(level.starts(offs_ref)):
                for t in range(2):
                    own_ref[spot, t, i] = block_ref[t + 1, b]


class Level:
    def __init__(self, index, span, rate, top_rate, fold, order):
        group = len(order)
        self.index = index
        self.rate = rate
        self.count = top_rate // rate
        self.crossing = span > group
        self.bits = span.bit_length() - group.bit_length()
        self.pieces = min(span, group) // fold
        self.segments = 1 if self.crossing else group // span
        self.spots = [order.index(device) // fold for device in range(0, group, fold)]

    def starts(self, offs):
        first = 0 if self.index == 0 else offs[self.index - 1, 0]
        return [first + self.rate * i for i in range(self.count)]

    def places(self, offs_ref, segment):
        low = segment * self.pieces
        spots = self.spots[low : low + self.pieces]
        return [(nb, b) for b in self.starts(offs_ref) for nb in spots]


def gather(read, places):
    return jnp.concatenate([read(nb, b) for nb, b in places], axis=0)


def scores_of(query, key, scale):
    return dot(query, key, NT) * scale


def forward(query, key, value, scale):
    hd = value.shape[1]
    scores = scores_of(query, key, scale)
    top = jnp.max(scores, axis=-1, keepdims=True)
    weights = jnp.exp2(scores - top).astype(BF16)
    both = dot(weights, jnp.concatenate([value, jnp.ones_like(value)], axis=1), NN)
    mixed, total = both[:, :hd], both[:, hd:]
    return mixed / total, top + jnp.log2(total)


def merge(mixed, lse, more, more_lse):
    top = jnp.maximum(lse, more_lse)
    left, right = jnp.exp2(lse - top), jnp.exp2(more_lse - top)
    total = left + right
    return (mixed * left + more * right) / total, top + jnp.log2(total)


def merge_into(o_ref, lse_ref, places, more, more_lse):
    mixed, lse = merge(
        gather(lambda nb, b: o_ref[nb, b], places),
        gather(lambda nb, b: lse_ref[nb, b], places),
        more,
        more_lse,
    )
    put(o_ref, places, mixed)
    put(lse_ref, places, lse)


def put(ref, places, rows):
    size = ref.shape[-2]
    for i, (nb, b) in enumerate(places):
        ref[nb, b] = rows[i * size : (i + 1) * size]


def add(ref, places, rows):
    size = ref.shape[-2]
    for i, (nb, b) in enumerate(places):
        ref[nb, b] += rows[i * size : (i + 1) * size]


def crossing_keys(places, x_ref, other_ref, t):
    found = [x_ref[nb, t, b] for nb, b in places]
    others, pieces, _, count = other_ref.shape[:4]
    found += [
        other_ref[e, nb, t - 1, i]
        for e in range(others)
        for i in range(count)
        for nb in range(pieces)
    ]
    return jnp.concatenate(found, axis=0)


def all_blocks(levels, offs_ref, x_ref, others):
    crossing = 0
    for level in levels:
        if level.crossing:
            other_ref = others[crossing]
            crossing += 1
        for segment in range(level.segments):
            places = level.places(offs_ref, segment)
            query = gather(lambda nb, b: x_ref[nb, 0, b], places)
            if level.crossing:
                key, value = (crossing_keys(places, x_ref, other_ref, t) for t in (1, 2))
            else:
                key, value = (gather(lambda nb, b, t=t: x_ref[nb, t, b], places) for t in (1, 2))
            yield level, places, query, key, value


def row_sums(attn, grad, gain):
    hd = attn.shape[-1]
    attn = attn.astype(BF16).astype(F32)
    scaled = grad.astype(F32) * gain
    total = jnp.sum(attn, axis=-1, keepdims=True)
    away = attn - total * (1.0 / hd)
    return (
        total,
        jnp.sum(away * away, axis=-1, keepdims=True),
        jnp.sum(scaled, axis=-1, keepdims=True),
        jnp.sum(scaled * away, axis=-1, keepdims=True),
    )


def forward_kernel(levels, scale, offs_ref, gain_ref, x_ref, o_ref, attn_ref, lse_ref, table_ref):
    pieces, rate, size, hd = o_ref.shape
    for level, places, query, key, value in all_blocks(levels, offs_ref, x_ref, ()):
        mixed, lse = forward(query, key, value, scale)
        if level.index == 0:
            put(o_ref, places, mixed)
            put(lse_ref, places, lse)
        else:
            merge_into(o_ref, lse_ref, places, mixed, lse)
    per = rate * size // hd
    chunks = pieces * per
    lane = lax.broadcasted_iota(jnp.int32, (hd, hd), 1)
    table = jnp.zeros((hd, hd), F32)
    for nb in range(pieces):
        attn_ref[nb] = o_ref[nb].astype(BF16)
        attn = attn_ref[nb].reshape(rate * size, hd)
        grad = x_ref[nb, 3].reshape(rate * size, hd)
        for part in range(per):
            rows = slice(part * hd, (part + 1) * hd)
            for i, column in enumerate(row_sums(attn[rows], grad[rows], gain_ref[...])):
                table = jnp.where(lane == i * chunks + nb * per + part, column, table)
    table_ref[...] = table


def crossing_forward_kernel(levels, scale, offs_ref, gain_ref, x_ref, o_in, attn_in, lse_in, table_ref, *refs):
    others, (attn_ref, lse_ref, stats_ref, o_ref, sums_ref) = refs[:-5], refs[-5:]
    pieces, rate, size, hd = o_ref.shape
    per = rate * size // hd
    chunks = pieces * per
    lane = lax.broadcasted_iota(jnp.int32, (size, hd), 1)
    if len(levels) > 1:
        o_ref[...] = o_in[...]
        o_in = o_ref
    attn_ref[...] = attn_in[...]
    lse_ref[...] = lse_in[...]
    sums_ref[...] = table_ref[...]
    for level, places, query, key, value in all_blocks(levels, offs_ref, x_ref, others):
        mixed, lse = merge(
            gather(lambda nb, b: o_in[nb, b], places),
            gather(lambda nb, b: lse_ref[nb, b], places),
            *forward(query, key, value, scale),
        )
        if len(levels) > 1:
            put(o_ref, places, mixed)
        put(attn_ref, places, mixed.astype(BF16))
        put(lse_ref, places, lse)
        sums = row_sums(
            mixed,
            gather(lambda nb, b: x_ref[nb, 3, b], places),
            gain_ref[...],
        )
        for j, (nb, b) in enumerate(places):
            chunk = nb * per + b * size // hd
            rows = pl.ds(pl.multiple_of(b * size % hd, size), size)
            table = sums_ref[rows, :]
            for i, column in enumerate(sums):
                table = jnp.where(lane == i * chunks + chunk, column[j * size : (j + 1) * size], table)
            sums_ref[rows, :] = table
    turned = sums_ref[...].T[: 4 * chunks]
    for peer in range(stats_ref.shape[0]):
        stats_ref[peer] = turned


def norm_kernel(heads, levels, scale, score_scale, offs_ref, x_ref, attn_ref, lse_ref, gain_ref, stats_ref, *refs):
    count = len(levels)
    others, refs = refs[:count], refs[count:]
    attended_ref, grad_ref, gsum_ref = refs[:3]
    own_refs, sent_refs = refs[3 : 3 + count], refs[3 + count :]
    pieces, rate, size, hd = attn_ref.shape
    chunks = pieces * rate * size // hd
    per = chunks // pieces
    width = heads * hd
    sums, squares, scaleds, products = (
        [stats_ref[h, i * chunks : (i + 1) * chunks, :] for h in range(heads)] for i in range(4)
    )
    mean = functools.reduce(jnp.add, sums) * (1.0 / width)
    apart = [total * (1.0 / hd) - mean for total in sums]
    variance = functools.reduce(
        jnp.add, [square + hd * a * a for square, a in zip(squares, apart)]
    ) * (1.0 / width)
    inverse = lax.rsqrt(variance + EPSILON)
    first = functools.reduce(jnp.add, scaleds) * (1.0 / width)
    second = (
        functools.reduce(jnp.add, [p + a * s for p, a, s in zip(products, apart, scaleds)])
        * (1.0 / width)
        * inverse
    )
    table = jnp.concatenate(
        [mean, inverse, first, second, jnp.zeros((hd - 4 * chunks, hd), F32)], axis=0
    )
    table = two_parts(table.T)
    lane = lax.broadcasted_iota(jnp.int32, (hd, 2 * hd), 1) % chunks
    picker = lax.broadcasted_iota(jnp.int32, (2 * hd, 4 * hd), 0) % hd // chunks
    picker = (picker == lax.broadcasted_iota(jnp.int32, (2 * hd, 4 * hd), 1) // hd).astype(BF16)
    picked = [jnp.where(lane == chunk, table, jnp.zeros_like(table)) for chunk in range(chunks)]
    columns = dot(jnp.concatenate(picked, axis=0), picker, NN)
    gsum = jnp.zeros((1, hd), F32)
    shape = (rate, size, hd)
    for nb in range(pieces):
        attn_all = attn_ref[nb].reshape(rate * size, hd).astype(F32)
        grad_all = x_ref[nb, 3].reshape(rate * size, hd).astype(F32)
        attended, grads = [], []
        for part in range(per):
            chunk = nb * per + part
            mean_c, inv_c, first_c, second_c = (
                columns[chunk * hd : (chunk + 1) * hd, i * hd : (i + 1) * hd] for i in range(4)
            )
            attn = attn_all[part * hd : (part + 1) * hd]
            upstream = grad_all[part * hd : (part + 1) * hd]
            normed = (attn - mean_c) * inv_c
            attended.append((normed * gain_ref[...]).astype(BF16))
            grad = (inv_c * (upstream * gain_ref[...] - first_c - normed * second_c)).astype(BF16)
            grads.append(grad)
            gsum = gsum + jnp.sum(upstream * normed, axis=0, keepdims=True)
        attended_ref[nb] = jnp.concatenate(attended, axis=0).reshape(shape)
        grad_ref[nb] = jnp.concatenate(grads, axis=0).reshape(shape)
    gsum_ref[...] = gsum
    blocks = list(all_blocks(levels, offs_ref, x_ref, others))
    deltas = []
    for _, places, *_ in blocks:
        grad = gather(lambda nb, b: grad_ref[nb, b], places).astype(F32)
        attn = gather(lambda nb, b: attn_ref[nb, b], places).astype(F32)
        delta = jnp.sum(grad * attn, axis=-1, keepdims=True)
        deltas.append(jnp.broadcast_to(delta, grad.shape))
    results = backward(blocks, grad_ref, lse_ref, deltas, scale, score_scale)
    for i, parts in enumerate(results):
        own = parts[0].shape[0]
        level, coded = levels[i], three_parts(gsum)
        steps = level.count
        for t, part in enumerate(parts):
            own_refs[i][t] = part[:own]
            if t > 0:
                low = own
                for e in range(sent_refs[i].shape[0]):
                    for step in range(steps):
                        for nb in range(level.pieces):
                            rows = part[low : low + size].astype(sent_refs[i].dtype)
                            sent_refs[i][e, (nb * 2 + t - 1) * steps + step] = rows
                            low += size
                    sent_refs[i][e, 2 * steps * level.pieces] = coded.astype(sent_refs[i].dtype)


def backward(blocks, grad_ref, lse_ref, deltas, scale, score_scale):
    def wide(column, key):
        return jnp.concatenate([column] * (key.shape[0] // column.shape[1]), axis=1)

    grads = [gather(lambda nb, b: grad_ref[nb, b], places) for _, places, _, _, _ in blocks]
    scores = [scores_of(query, key, score_scale) for _, _, query, key, _ in blocks]
    prob_grads = [dot(grad, block[4], NT) for grad, block in zip(grads, blocks)]
    probs = [
        jnp.exp2(score - wide(gather(lambda nb, b: lse_ref[nb, b], places), key))
        for score, (_, places, _, key, _) in zip(scores, blocks)
    ]
    score_grads = [
        (prob * (prob_grad - wide(delta, block[3]))).astype(BF16)
        for prob, prob_grad, delta, block in zip(probs, prob_grads, deltas, blocks)
    ]
    queries = [dot(each, block[3], NN) * scale for each, block in zip(score_grads, blocks)]
    keys = [dot(each, block[2], TN) * scale for each, block in zip(score_grads, blocks)]
    values = [dot(prob.astype(BF16), grad, TN) for prob, grad in zip(probs, grads)]
    return list(zip(queries, keys, values))


def local_kernel(levels, crossing, scale, score_scale, offs_ref, x_ref, attended_ref, grad_ref, lse_ref, attn_ref, *refs):
    own_refs, (out_ref, kv_ref, dq_ref, delta_ref) = refs[: len(crossing)], refs[len(crossing) :]
    pieces, rate, size, hd = dq_ref.shape
    products = [
        two_parts((grad_ref[nb].astype(F32) * attn_ref[nb].astype(F32)).reshape(rate * size, hd))
        for nb in range(pieces)
    ]
    sums = dot(jnp.concatenate(products, axis=0), jnp.ones((2 * hd, hd), BF16), NN)
    delta_ref[...] = sums.reshape(delta_ref.shape)
    accumulators = (dq_ref, kv_ref.at[0], kv_ref.at[1])
    blocks = list(all_blocks(levels, offs_ref, x_ref, ()))
    for low in range(0, len(blocks), STAGED):
        some = blocks[low : low + STAGED]
        deltas = [gather(lambda nb, b: delta_ref[nb, b], places) for _, places, *_ in some]
        results = backward(some, grad_ref, lse_ref, deltas, scale, score_scale)
        for i, ref in enumerate(accumulators):
            for (level, places, *_), parts in zip(some, results):
                (put if level.index == 0 else add)(ref, places, parts[i])
    for level, own_ref in zip(crossing, own_refs):
        places = level.places(offs_ref, 0)
        for t, ref in enumerate(accumulators):
            add(ref, places, own_ref[t])
    out_ref[:, 0] = dq_ref[...].astype(BF16)
    out_ref[:, 1] = attended_ref[...]


def pack_kernel(crossing, fold, alone, offs_ref, main_ref, kv_in, gsum_ref, *refs):
    arrived_refs, (out_ref, kv_ref) = refs[:-2], refs[-2:]
    pieces, _, rate, size, hd = main_ref.shape
    rows = rate * size
    kv_ref[...] = kv_in[...]
    for level, arrived_ref in zip(crossing, arrived_refs):
        for i, b in enumerate(level.starts(offs_ref)):
            for nb in range(level.pieces):
                for t in range(2):
                    block = (nb * 2 + t) * level.count + i
                    kv_ref[t, nb, b] += arrived_ref[block].astype(F32)
    total = gsum_ref[...]
    if alone:
        other = arrived_refs[0][arrived_refs[0].shape[0] - 1]
        total = total + jnp.sum(other.astype(F32), axis=0, keepdims=True)
    coded = three_parts(total)
    for nb in range(pieces):
        for t in range(2):
            out_ref[nb, t * rows : (t + 1) * rows] = main_ref[nb, t].reshape(rows, hd)
            out_ref[nb, (t + 2) * rows : (t + 3) * rows] = (
                kv_ref[t, nb].reshape(rows, hd).astype(BF16)
            )
        for f in range(fold):
            out_ref[nb, 4 * rows + f * TILE : 4 * rows + (f + 1) * TILE] = coded


def join_kernel(rate, in_ref, dq_ref, attended_ref, dk_ref, dv_ref):
    group, _, hd = in_ref.shape
    tokens = dq_ref.shape[1]
    order = row_order(tokens, rate, True)
    for t, ref in enumerate((dq_ref, attended_ref, dk_ref, dv_ref)):
        for h in range(group):
            moved = dot(order, in_ref[h, t * tokens : (t + 1) * tokens, :], NN)
            ref[0, :, h * hd : (h + 1) * hd] = moved.astype(BF16)


VMEM = pl.BlockSpec(memory_space=pltpu.VMEM)


def call(body, name, inputs, outputs, scratch=(), flops=0, limit=24):
    shapes = [jax.ShapeDtypeStruct(*output) for output in outputs]
    moved = sum(x.size * x.dtype.itemsize for x in list(inputs) + shapes)
    return list(pl.pallas_call(
        body,
        name=name,
        in_specs=[VMEM] * len(inputs),
        out_specs=[VMEM] * len(shapes),
        out_shape=shapes,
        scratch_shapes=[pltpu.VMEM(*each) for each in scratch],
        cost_estimate=pl.CostEstimate(flops=flops, bytes_accessed=moved, transcendentals=0),
        compiler_params=pltpu.CompilerParams(vmem_limit_bytes=limit * 1024 * 1024),
    )(*inputs))


def flip(value, axis, bit):
    pairs = [(source, source ^ (1 << bit)) for source in range(lax.axis_size(axis))]
    return lax.ppermute(value, axis, pairs)


def shards(queries, key_rows, value_rows, out_grad, norm_gain, offsets):
    tokens, width = queries.shape[1:]
    group = offsets.shape[1]
    hd = width // group
    ctx_count = lax.axis_size("ctx")
    dp_count = lax.axis_size("dp")
    scale = hd ** (-0.5)
    score_scale = scale * LOG2E
    spans = [
        (SPAN_A, RATE_A),
        (SPAN_B, RATE_B),
        (SPAN_C, RATE_C),
        (ctx_count // 2, ctx_count // 4),
    ]
    rate = max(r for _, r in spans)
    short = tokens // rate
    fold = max(1, TILE // short)
    size = short * fold
    pieces = group // fold
    order = list(ORDER) if group == len(ORDER) and fold == 1 else list(range(group))
    levels = [Level(i, span, r, rate, fold, order) for i, (span, r) in enumerate(spans)]
    local = [level for level in levels if not level.crossing]
    crossing = [level for level in levels if level.crossing]
    groups = [[low + device for device in order] for low in range(0, ctx_count, group)]
    low_bit = group.bit_length() - 1

    def exchange(value):
        return lax.all_to_all(value, "ctx", 0, 0, tiled=True, axis_index_groups=groups)

    place = lax.axis_index("ctx") % group
    head = sum(order.index(device) * (place == device) for device in range(group))
    offs = lax.dynamic_slice(offsets, (0, head), (offsets.shape[0], 1))
    offs_rows = jnp.broadcast_to(offs, (offsets.shape[0], hd))
    gain = lax.dynamic_slice(norm_gain, (head * hd,), (hd,))[None]

    alone = ctx_count == 2 * group and dp_count == 2 and size == TILE and len(crossing) == 1
    alone = alone and group == len(ORDER)
    if alone:
        far = call(
            functools.partial(split_apart_kernel, rate, order),
            "split",
            [queries, key_rows, value_rows, out_grad],
            [((4, tokens, hd), BF16)] * group,
            scratch=[((group, 4, tokens, hd), BF16)],
            limit=60,
        )
        for apart in FAR_FIRST:
            pairs = [(source, source ^ apart) for source in range(ctx_count)]
            far[apart] = lax.ppermute(far[apart], "ctx", pairs)
        x, *owns = call(
            functools.partial(collect_kernel, crossing, order),
            "collect",
            [offs_rows] + [block.reshape(4, rate, size, hd) for block in far],
            [((pieces, 4, rate, size, hd), BF16)]
            + [((pieces, 2, level.count, size, hd), BF16) for level in crossing],
        )
    else:
        (sent,) = call(
            functools.partial(split_kernel, rate),
            "split",
            [queries, key_rows, value_rows, out_grad],
            [((group, 4, tokens, hd), BF16)],
            limit=60,
        )
        x = exchange(sent)
        if fold > 1:
            x = x.reshape(pieces, fold, 4, rate, short, hd).transpose(0, 2, 3, 1, 4, 5)
        x = x.reshape(pieces, 4, rate, size, hd)
        owns = []
        for level in crossing:
            own = [
                lax.dynamic_slice(x, (0, 1, b, 0, 0), (pieces, 2, 1, size, hd))
                for b in level.starts(offs)
            ]
            owns.append(jnp.concatenate(own, axis=2))

    others = []
    for level, own in zip(crossing, owns):
        blocks = [own]
        for bit in range(level.bits):
            blocks += [flip(block, "ctx", low_bit + bit) for block in blocks]
        others.append(jnp.stack(blocks[1:]))

    state = (pieces, rate, size, hd)
    chunks = group * tokens // hd
    o, attn, lse, table = call(
        functools.partial(forward_kernel, local, score_scale),
        "local_forward",
        [offs_rows, gain, x],
        [(state, F32), (state, BF16), (state, F32), ((hd, hd), F32)],
        flops=10**8,
    )
    attn, lse, stats = call(
        functools.partial(crossing_forward_kernel, crossing, score_scale),
        "crossing_forward",
        [offs_rows, gain, x, o, attn, lse, table] + others,
        [(state, BF16), (state, F32), ((group, 4 * chunks, hd), F32)],
        scratch=[(state, F32), ((hd, hd), F32)],
    )
    stats = exchange(stats)
    outs = [(state, BF16), (state, BF16), ((1, hd), F32)]
    outs += [((3, pieces * level.count * size, hd), F32) for level in crossing]
    sent_types = [BF16 if level.bits == 1 else F32 for level in crossing]
    outs += [
        ((other.shape[0], 2 * level.pieces * level.count + 1, size, hd), kind)
        for level, other, kind in zip(crossing, others, sent_types)
    ]
    attended, grad, gsum, *rest = call(
        functools.partial(norm_kernel, group, crossing, scale, score_scale),
        "norm_and_crossing",
        [offs_rows, x, attn, lse, gain, stats] + others,
        outs,
        flops=10**7,
    )
    owns, parts = rest[: len(crossing)], rest[len(crossing) :]

    arrived = []
    for level, part in zip(crossing, parts):
        partial = [None] + [part[e] for e in range(part.shape[0])]
        for bit in reversed(range(level.bits)):
            half = 1 << bit
            came = [flip(block.astype(BF16), "ctx", low_bit + bit) for block in partial[half:]]
            partial = [
                c if b is None else b.astype(F32) + c.astype(F32)
                for b, c in zip(partial[:half], came)
            ]
        arrived.append(partial[0])
    if not alone:
        for axis, count, first in (("dp", dp_count, 0), ("ctx", ctx_count, low_bit)):
            for bit in range(first, count.bit_length() - 1):
                gsum = gsum + flip(gsum, axis, bit)

    main, kv = call(
        functools.partial(local_kernel, local, crossing, scale, score_scale),
        "local_backward",
        [offs_rows, x, attended, grad, lse, attn] + owns,
        [((pieces, 2, rate, size, hd), BF16), ((2,) + state, F32)],
        scratch=[(state, F32)] * 2,
        flops=3 * 10**8,
    )
    (packed,) = call(
        functools.partial(pack_kernel, crossing, fold, alone),
        "pack",
        [offs_rows, main, kv, gsum] + arrived,
        [((pieces, 4 * rate * size + TILE * fold, hd), BF16)],
        scratch=[((2,) + state, F32)],
    )
    if fold > 1:
        rows = packed[:, : 4 * rate * size].reshape(pieces, 4, rate, fold, short, hd)
        rows = rows.transpose(0, 3, 1, 2, 4, 5).reshape(group, 4 * tokens, hd)
        packed = jnp.concatenate([rows, packed[:, 4 * rate * size :].reshape(group, TILE, hd)], 1)
    back = exchange(packed)
    gains = jnp.sum(back[:, 4 * tokens :].astype(F32), axis=1)
    if alone:
        gains = gains + flip(gains, "dp", 0)
    gain_grad = gains.reshape(width) / math.sqrt(ctx_count * dp_count * tokens)
    row = ((1, tokens, width), BF16)
    dq, attended, dk, dv = call(
        functools.partial(join_kernel, rate),
        "join",
        [back],
        [row, row, row, row],
        flops=10**8,
    )
    return attended, dq, dk, dv, gain_grad


def solution(mesh):
    rows = P("dp", "ctx", None)
    return jax.shard_map(
        shards,
        mesh=mesh,
        in_specs=(rows, rows, rows, rows, P(), P()),
        out_specs=(rows, rows, rows, rows, P()),
        check_vma=False,
    )
```

```python
import functools
import math

import jax
import jax.numpy as jnp
from jax import lax
from jax.experimental import pallas as pl
from jax.experimental.pallas import tpu as pltpu
from jax.sharding import PartitionSpec as P

SPAN_A = 2
RATE_A = 1
SPAN_B = 4
RATE_B = 2
SPAN_C = 16
RATE_C = 8

EPSILON = 1e-05
LOG2E = math.log2(math.e)
TILE = 16
STAGED = 4
ORDER = (0, 7, 2, 6, 1, 5, 4, 3)
FAR_FIRST = (7, 6, 5, 3, 4, 2, 1)
F32 = jnp.float32
BF16 = jnp.bfloat16

NT = (((1,), (1,)), ((), ()))
TN = (((0,), (0,)), ((), ()))
NN = (((1,), (0,)), ((), ()))


def dot(left, right, dims):
    return lax.dot_general(left, right, dims, preferred_element_type=F32)


def two_parts(value):
    high = value.astype(BF16)
    return jnp.concatenate([high, (value - high.astype(F32)).astype(BF16)], axis=1)


def three_parts(row):
    total = jnp.broadcast_to(row, (TILE, row.shape[1]))
    high = total.astype(BF16).astype(F32)
    middle = (total - high).astype(BF16).astype(F32)
    low = total - high - middle
    place = lax.broadcasted_iota(jnp.int32, total.shape, 0)
    parts = jnp.where(place == 0, high, jnp.where(place == 1, middle, low))
    return jnp.where(place < 3, parts, 0.0).astype(BF16)


def row_order(tokens, rate, transposed):
    short = tokens // rate
    placed = lax.broadcasted_iota(jnp.int32, (tokens, tokens), 1 if transposed else 0)
    source = lax.broadcasted_iota(jnp.int32, (tokens, tokens), 0 if transposed else 1)
    return (source == (placed % short) * rate + placed // short).astype(BF16)


def split_kernel(rate, q_ref, k_ref, v_ref, g_ref, out_ref):
    group, _, tokens, hd = out_ref.shape
    order = row_order(tokens, rate, False)
    for t, ref in enumerate((q_ref, k_ref, v_ref, g_ref)):
        moved = dot(order, ref[0], NN).astype(BF16)
        for h in range(group):
            out_ref[h, t] = moved[:, h * hd : (h + 1) * hd]


def head_at(order, apart):
    place = lax.axis_index("ctx") % len(order) ^ apart
    return sum(order.index(device) * (place == device) for device in range(len(order)))


def split_apart_kernel(rate, order, rows_ref, *refs):
    outs, moved_ref = refs[:-1], refs[-1]
    group, _, tokens, hd = moved_ref.shape
    change = row_order(tokens, rate, False)
    for t in range(4):
        moved = dot(change, rows_ref[t], NN).astype(BF16)
        for h in range(group):
            moved_ref[h, t] = moved[:, h * hd : (h + 1) * hd]
    for apart, out_ref in enumerate(outs):
        out_ref[...] = moved_ref[head_at(order, apart)]


def collect_kernel(levels, order, offs_ref, *refs):
    blocks, x_ref, own_refs = refs[: len(order)], refs[len(order)], refs[len(order) + 1 :]
    for apart, block_ref in enumerate(blocks):
        spot = head_at(order, apart)
        x_ref[spot] = block_ref[...]
        for level, own_ref in zip(levels, own_refs):
            for i, b in enumerate(level.starts(offs_ref)):
                for t in range(2):
                    own_ref[spot, t, i] = block_ref[t + 1, b]


class Level:
    def __init__(self, index, span, rate, top_rate, fold, order):
        group = len(order)
        self.index = index
        self.rate = rate
        self.count = top_rate // rate
        self.crossing = span > group
        self.bits = span.bit_length() - group.bit_length()
        self.pieces = min(span, group) // fold
        self.segments = 1 if self.crossing else group // span
        self.spots = [order.index(device) // fold for device in range(0, group, fold)]

    def starts(self, offs):
        first = 0 if self.index == 0 else offs[self.index - 1, 0]
        return [first + self.rate * i for i in range(self.count)]

    def places(self, offs_ref, segment):
        low = segment * self.pieces
        spots = self.spots[low : low + self.pieces]
        return [(nb, b) for b in self.starts(offs_ref) for nb in spots]


def gather(read, places):
    return jnp.concatenate([read(nb, b) for nb, b in places], axis=0)


def scores_of(query, key, scale):
    return dot(query, key, NT) * scale


def forward(query, key, value, scale):
    hd = value.shape[1]
    scores = scores_of(query, key, scale)
    top = jnp.max(scores, axis=-1, keepdims=True)
    weights = jnp.exp2(scores - top).astype(BF16)
    both = dot(weights, jnp.concatenate([value, jnp.ones_like(value)], axis=1), NN)
    mixed, total = both[:, :hd], both[:, hd:]
    return mixed / total, top + jnp.log2(total)


def merge(mixed, lse, more, more_lse):
    top = jnp.maximum(lse, more_lse)
    left, right = jnp.exp2(lse - top), jnp.exp2(more_lse - top)
    total = left + right
    return (mixed * left + more * right) / total, top + jnp.log2(total)


def merge_into(o_ref, lse_ref, places, more, more_lse):
    mixed, lse = merge(
        gather(lambda nb, b: o_ref[nb, b], places),
        gather(lambda nb, b: lse_ref[nb, b], places),
        more,
        more_lse,
    )
    put(o_ref, places, mixed)
    put(lse_ref, places, lse)


def put(ref, places, rows):
    size = ref.shape[-2]
    for i, (nb, b) in enumerate(places):
        ref[nb, b] = rows[i * size : (i + 1) * size]


def add(ref, places, rows):
    size = ref.shape[-2]
    for i, (nb, b) in enumerate(places):
        ref[nb, b] += rows[i * size : (i + 1) * size]


def crossing_keys(places, x_ref, other_ref, t):
    found = [x_ref[nb, t, b] for nb, b in places]
    others, pieces, _, count = other_ref.shape[:4]
    found += [
        other_ref[e, nb, t - 1, i]
        for e in range(others)
        for i in range(count)
        for nb in range(pieces)
    ]
    return jnp.concatenate(found, axis=0)


def all_blocks(levels, offs_ref, x_ref, others):
    crossing = 0
    for level in levels:
        if level.crossing:
            other_ref = others[crossing]
            crossing += 1
        for segment in range(level.segments):
            places = level.places(offs_ref, segment)
            query = gather(lambda nb, b: x_ref[nb, 0, b], places)
            if level.crossing:
                key, value = (crossing_keys(places, x_ref, other_ref, t) for t in (1, 2))
            else:
                key, value = (gather(lambda nb, b, t=t: x_ref[nb, t, b], places) for t in (1, 2))
            yield level, places, query, key, value


def row_sums(attn, grad, gain):
    hd = attn.shape[-1]
    attn = attn.astype(BF16).astype(F32)
    scaled = grad.astype(F32) * gain
    total = jnp.sum(attn, axis=-1, keepdims=True)
    away = attn - total * (1.0 / hd)
    return (
        total,
        jnp.sum(away * away, axis=-1, keepdims=True),
        jnp.sum(scaled, axis=-1, keepdims=True),
        jnp.sum(scaled * away, axis=-1, keepdims=True),
    )


def forward_kernel(levels, scale, offs_ref, gain_ref, x_ref, o_ref, attn_ref, lse_ref, table_ref):
    pieces, rate, size, hd = o_ref.shape
    for level, places, query, key, value in all_blocks(levels, offs_ref, x_ref, ()):
        mixed, lse = forward(query, key, value, scale)
        if level.index == 0:
            put(o_ref, places, mixed)
            put(lse_ref, places, lse)
        else:
            merge_into(o_ref, lse_ref, places, mixed, lse)
    per = rate * size // hd
    chunks = pieces * per
    lane = lax.broadcasted_iota(jnp.int32, (hd, hd), 1)
    table = jnp.zeros((hd, hd), F32)
    for nb in range(pieces):
        attn_ref[nb] = o_ref[nb].astype(BF16)
        attn = attn_ref[nb].reshape(rate * size, hd)
        grad = x_ref[nb, 3].reshape(rate * size, hd)
        for part in range(per):
            rows = slice(part * hd, (part + 1) * hd)
            for i, column in enumerate(row_sums(attn[rows], grad[rows], gain_ref[...])):
                table = jnp.where(lane == i * chunks + nb * per + part, column, table)
    table_ref[...] = table


def crossing_forward_kernel(levels, scale, offs_ref, gain_ref, x_ref, o_in, attn_in, lse_in, table_ref, *refs):
    others, (attn_ref, lse_ref, stats_ref, o_ref, sums_ref) = refs[:-5], refs[-5:]
    pieces, rate, size, hd = o_ref.shape
    per = rate * size // hd
    chunks = pieces * per
    lane = lax.broadcasted_iota(jnp.int32, (size, hd), 1)
    if len(levels) > 1:
        o_ref[...] = o_in[...]
        o_in = o_ref
    attn_ref[...] = attn_in[...]
    lse_ref[...] = lse_in[...]
    sums_ref[...] = table_ref[...]
    for level, places, query, key, value in all_blocks(levels, offs_ref, x_ref, others):
        mixed, lse = merge(
            gather(lambda nb, b: o_in[nb, b], places),
            gather(lambda nb, b: lse_ref[nb, b], places),
            *forward(query, key, value, scale),
        )
        if len(levels) > 1:
            put(o_ref, places, mixed)
        put(attn_ref, places, mixed.astype(BF16))
        put(lse_ref, places, lse)
        sums = row_sums(
            mixed,
            gather(lambda nb, b: x_ref[nb, 3, b], places),
            gain_ref[...],
        )
        for j, (nb, b) in enumerate(places):
            chunk = nb * per + b * size // hd
            rows = pl.ds(pl.multiple_of(b * size % hd, size), size)
            table = sums_ref[rows, :]
            for i, column in enumerate(sums):
                table = jnp.where(lane == i * chunks + chunk, column[j * size : (j + 1) * size], table)
            sums_ref[rows, :] = table
    turned = sums_ref[...].T[: 4 * chunks]
    for peer in range(stats_ref.shape[0]):
        stats_ref[peer] = turned


def norm_kernel(heads, levels, scale, score_scale, offs_ref, x_ref, attn_ref, lse_ref, gain_ref, stats_ref, *refs):
    count = len(levels)
    others, refs = refs[:count], refs[count:]
    attended_ref, grad_ref, gsum_ref = refs[:3]
    own_refs, sent_refs = refs[3 : 3 + count], refs[3 + count :]
    pieces, rate, size, hd = attn_ref.shape
    chunks = pieces * rate * size // hd
    per = chunks // pieces
    width = heads * hd
    sums, squares, scaleds, products = (
        [stats_ref[h, i * chunks : (i + 1) * chunks, :] for h in range(heads)] for i in range(4)
    )
    mean = functools.reduce(jnp.add, sums) * (1.0 / width)
    apart = [total * (1.0 / hd) - mean for total in sums]
    variance = functools.reduce(
        jnp.add, [square + hd * a * a for square, a in zip(squares, apart)]
    ) * (1.0 / width)
    inverse = lax.rsqrt(variance + EPSILON)
    first = functools.reduce(jnp.add, scaleds) * (1.0 / width)
    second = (
        functools.reduce(jnp.add, [p + a * s for p, a, s in zip(products, apart, scaleds)])
        * (1.0 / width)
        * inverse
    )
    table = jnp.concatenate(
        [mean, inverse, first, second, jnp.zeros((hd - 4 * chunks, hd), F32)], axis=0
    )
    table = two_parts(table.T)
    lane = lax.broadcasted_iota(jnp.int32, (hd, 2 * hd), 1) % chunks
    picker = lax.broadcasted_iota(jnp.int32, (2 * hd, 4 * hd), 0) % hd // chunks
    picker = (picker == lax.broadcasted_iota(jnp.int32, (2 * hd, 4 * hd), 1) // hd).astype(BF16)
    picked = [jnp.where(lane == chunk, table, jnp.zeros_like(table)) for chunk in range(chunks)]
    columns = dot(jnp.concatenate(picked, axis=0), picker, NN)
    gsum = jnp.zeros((1, hd), F32)
    shape = (rate, size, hd)
    for nb in range(pieces):
        attn_all = attn_ref[nb].reshape(rate * size, hd).astype(F32)
        grad_all = x_ref[nb, 3].reshape(rate * size, hd).astype(F32)
        attended, grads = [], []
        for part in range(per):
            chunk = nb * per + part
            mean_c, inv_c, first_c, second_c = (
                columns[chunk * hd : (chunk + 1) * hd, i * hd : (i + 1) * hd] for i in range(4)
            )
            attn = attn_all[part * hd : (part + 1) * hd]
            upstream = grad_all[part * hd : (part + 1) * hd]
            normed = (attn - mean_c) * inv_c
            attended.append((normed * gain_ref[...]).astype(BF16))
            grad = (inv_c * (upstream * gain_ref[...] - first_c - normed * second_c)).astype(BF16)
            grads.append(grad)
            gsum = gsum + jnp.sum(upstream * normed, axis=0, keepdims=True)
        attended_ref[nb] = jnp.concatenate(attended, axis=0).reshape(shape)
        grad_ref[nb] = jnp.concatenate(grads, axis=0).reshape(shape)
    gsum_ref[...] = gsum
    blocks = list(all_blocks(levels, offs_ref, x_ref, others))
    deltas = []
    for _, places, *_ in blocks:
        grad = gather(lambda nb, b: grad_ref[nb, b], places).astype(F32)
        attn = gather(lambda nb, b: attn_ref[nb, b], places).astype(F32)
        delta = jnp.sum(grad * attn, axis=-1, keepdims=True)
        deltas.append(jnp.broadcast_to(delta, grad.shape))
    results = backward(blocks, grad_ref, lse_ref, deltas, scale, score_scale)
    for i, parts in enumerate(results):
        own = parts[0].shape[0]
        level, coded = levels[i], three_parts(gsum)
        steps = level.count
        for t, part in enumerate(parts):
            own_refs[i][t] = part[:own]
            if t > 0:
                low = own
                for e in range(sent_refs[i].shape[0]):
                    for step in range(steps):
                        for nb in range(level.pieces):
                            rows = part[low : low + size].astype(sent_refs[i].dtype)
                            sent_refs[i][e, (nb * 2 + t - 1) * steps + step] = rows
                            low += size
                    sent_refs[i][e, 2 * steps * level.pieces] = coded.astype(sent_refs[i].dtype)


def backward(blocks, grad_ref, lse_ref, deltas, scale, score_scale):
    def wide(column, key):
        return jnp.concatenate([column] * (key.shape[0] // column.shape[1]), axis=1)

    grads = [gather(lambda nb, b: grad_ref[nb, b], places) for _, places, _, _, _ in blocks]
    scores = [scores_of(query, key, score_scale) for _, _, query, key, _ in blocks]
    prob_grads = [dot(grad, block[4], NT) for grad, block in zip(grads, blocks)]
    probs = [
        jnp.exp2(score - wide(gather(lambda nb, b: lse_ref[nb, b], places), key))
        for score, (_, places, _, key, _) in zip(scores, blocks)
    ]
    score_grads = [
        (prob * (prob_grad - wide(delta, block[3]))).astype(BF16)
        for prob, prob_grad, delta, block in zip(probs, prob_grads, deltas, blocks)
    ]
    queries = [dot(each, block[3], NN) * scale for each, block in zip(score_grads, blocks)]
    keys = [dot(each, block[2], TN) * scale for each, block in zip(score_grads, blocks)]
    values = [dot(prob.astype(BF16), grad, TN) for prob, grad in zip(probs, grads)]
    return list(zip(queries, keys, values))


def local_kernel(levels, crossing, scale, score_scale, offs_ref, x_ref, attended_ref, grad_ref, lse_ref, attn_ref, *refs):
    own_refs, (out_ref, kv_ref, dq_ref, delta_ref) = refs[: len(crossing)], refs[len(crossing) :]
    pieces, rate, size, hd = dq_ref.shape
    products = [
        two_parts((grad_ref[nb].astype(F32) * attn_ref[nb].astype(F32)).reshape(rate * size, hd))
        for nb in range(pieces)
    ]
    sums = dot(jnp.concatenate(products, axis=0), jnp.ones((2 * hd, hd), BF16), NN)
    delta_ref[...] = sums.reshape(delta_ref.shape)
    accumulators = (dq_ref, kv_ref.at[0], kv_ref.at[1])
    blocks = list(all_blocks(levels, offs_ref, x_ref, ()))
    for low in range(0, len(blocks), STAGED):
        some = blocks[low : low + STAGED]
        deltas = [gather(lambda nb, b: delta_ref[nb, b], places) for _, places, *_ in some]
        results = backward(some, grad_ref, lse_ref, deltas, scale, score_scale)
        for i, ref in enumerate(accumulators):
            for (level, places, *_), parts in zip(some, results):
                (put if level.index == 0 else add)(ref, places, parts[i])
    for level, own_ref in zip(crossing, own_refs):
        places = level.places(offs_ref, 0)
        for t, ref in enumerate(accumulators):
            add(ref, places, own_ref[t])
    out_ref[:, 0] = dq_ref[...].astype(BF16)
    out_ref[:, 1] = attended_ref[...]


def pack_kernel(crossing, fold, alone, offs_ref, main_ref, kv_in, gsum_ref, *refs):
    arrived_refs, (out_ref, kv_ref) = refs[:-2], refs[-2:]
    pieces, _, rate, size, hd = main_ref.shape
    rows = rate * size
    kv_ref[...] = kv_in[...]
    for level, arrived_ref in zip(crossing, arrived_refs):
        for i, b in enumerate(level.starts(offs_ref)):
            for nb in range(level.pieces):
                for t in range(2):
                    block = (nb * 2 + t) * level.count + i
                    kv_ref[t, nb, b] += arrived_ref[block].astype(F32)
    total = gsum_ref[...]
    if alone:
        other = arrived_refs[0][arrived_refs[0].shape[0] - 1]
        total = total + jnp.sum(other.astype(F32), axis=0, keepdims=True)
    coded = three_parts(total)
    for nb in range(pieces):
        for t in range(2):
            out_ref[nb, t * rows : (t + 1) * rows] = main_ref[nb, t].reshape(rows, hd)
            out_ref[nb, (t + 2) * rows : (t + 3) * rows] = (
                kv_ref[t, nb].reshape(rows, hd).astype(BF16)
            )
        for f in range(fold):
            out_ref[nb, 4 * rows + f * TILE : 4 * rows + (f + 1) * TILE] = coded


def join_kernel(rate, in_ref, dq_ref, attended_ref, dk_ref, dv_ref):
    group, _, hd = in_ref.shape
    tokens = dq_ref.shape[1]
    order = row_order(tokens, rate, True)
    for t, ref in enumerate((dq_ref, attended_ref, dk_ref, dv_ref)):
        for h in range(group):
            moved = dot(order, in_ref[h, t * tokens : (t + 1) * tokens, :], NN)
            ref[0, :, h * hd : (h + 1) * hd] = moved.astype(BF16)


VMEM = pl.BlockSpec(memory_space=pltpu.VMEM)


def call(body, name, inputs, outputs, scratch=(), flops=0, limit=24):
    shapes = [jax.ShapeDtypeStruct(*output) for output in outputs]
    moved = sum(x.size * x.dtype.itemsize for x in list(inputs) + shapes)
    return list(pl.pallas_call(
        body,
        name=name,
        in_specs=[VMEM] * len(inputs),
        out_specs=[VMEM] * len(shapes),
        out_shape=shapes,
        scratch_shapes=[pltpu.VMEM(*each) for each in scratch],
        cost_estimate=pl.CostEstimate(flops=flops, bytes_accessed=moved, transcendentals=0),
        compiler_params=pltpu.CompilerParams(vmem_limit_bytes=limit * 1024 * 1024),
    )(*inputs))


def flip(value, axis, bit):
    pairs = [(source, source ^ (1 << bit)) for source in range(lax.axis_size(axis))]
    return lax.ppermute(value, axis, pairs)


def shards(queries, key_rows, value_rows, out_grad, norm_gain, offsets):
    tokens, width = queries.shape[1:]
    group = offsets.shape[1]
    hd = width // group
    ctx_count = lax.axis_size("ctx")
    dp_count = lax.axis_size("dp")
    scale = hd ** (-0.5)
    score_scale = scale * LOG2E
    spans = [
        (SPAN_A, RATE_A),
        (SPAN_B, RATE_B),
        (SPAN_C, RATE_C),
        (ctx_count // 2, ctx_count // 4),
    ]
    rate = max(r for _, r in spans)
    short = tokens // rate
    fold = max(1, TILE // short)
    size = short * fold
    pieces = group // fold
    order = list(ORDER) if group == len(ORDER) and fold == 1 else list(range(group))
    levels = [Level(i, span, r, rate, fold, order) for i, (span, r) in enumerate(spans)]
    local = [level for level in levels if not level.crossing]
    crossing = [level for level in levels if level.crossing]
    groups = [[low + device for device in order] for low in range(0, ctx_count, group)]
    low_bit = group.bit_length() - 1

    def exchange(value):
        return lax.all_to_all(value, "ctx", 0, 0, tiled=True, axis_index_groups=groups)

    place = lax.axis_index("ctx") % group
    head = sum(order.index(device) * (place == device) for device in range(group))
    offs = lax.dynamic_slice(offsets, (0, head), (offsets.shape[0], 1))
    offs_rows = jnp.broadcast_to(offs, (offsets.shape[0], hd))
    gain = lax.dynamic_slice(norm_gain, (head * hd,), (hd,))[None]

    alone = ctx_count == 2 * group and dp_count == 2 and size == TILE and len(crossing) == 1
    alone = alone and group == len(ORDER)
    if alone:
        far = call(
            functools.partial(split_apart_kernel, rate, order),
            "split",
            [jnp.concatenate([queries, key_rows, value_rows, out_grad], axis=0)],
            [((4, tokens, hd), BF16)] * group,
            scratch=[((group, 4, tokens, hd), BF16)],
        )
        for apart in FAR_FIRST:
            pairs = [(source, source ^ apart) for source in range(ctx_count)]
            far[apart] = lax.ppermute(far[apart], "ctx", pairs)
        x, *owns = call(
            functools.partial(collect_kernel, crossing, order),
            "collect",
            [offs_rows] + [block.reshape(4, rate, size, hd) for block in far],
            [((pieces, 4, rate, size, hd), BF16)]
            + [((pieces, 2, level.count, size, hd), BF16) for level in crossing],
        )
    else:
        (sent,) = call(
            functools.partial(split_kernel, rate),
            "split",
            [queries, key_rows, value_rows, out_grad],
            [((group, 4, tokens, hd), BF16)],
            limit=60,
        )
        x = exchange(sent)
        if fold > 1:
            x = x.reshape(pieces, fold, 4, rate, short, hd).transpose(0, 2, 3, 1, 4, 5)
        x = x.reshape(pieces, 4, rate, size, hd)
        owns = []
        for level in crossing:
            own = [
                lax.dynamic_slice(x, (0, 1, b, 0, 0), (pieces, 2, 1, size, hd))
                for b in level.starts(offs)
            ]
            owns.append(jnp.concatenate(own, axis=2))

    others = []
    for level, own in zip(crossing, owns):
        blocks = [own]
        for bit in range(level.bits):
            blocks += [flip(block, "ctx", low_bit + bit) for block in blocks]
        others.append(jnp.stack(blocks[1:]))

    state = (pieces, rate, size, hd)
    chunks = group * tokens // hd
    o, attn, lse, table = call(
        functools.partial(forward_kernel, local, score_scale),
        "local_forward",
        [offs_rows, gain, x],
        [(state, F32), (state, BF16), (state, F32), ((hd, hd), F32)],
        flops=10**8,
    )
    attn, lse, stats = call(
        functools.partial(crossing_forward_kernel, crossing, score_scale),
        "crossing_forward",
        [offs_rows, gain, x, o, attn, lse, table] + others,
        [(state, BF16), (state, F32), ((group, 4 * chunks, hd), F32)],
        scratch=[(state, F32), ((hd, hd), F32)],
    )
    stats = exchange(stats)
    outs = [(state, BF16), (state, BF16), ((1, hd), F32)]
    outs += [((3, pieces * level.count * size, hd), F32) for level in crossing]
    sent_types = [BF16 if level.bits == 1 else F32 for level in crossing]
    outs += [
        ((other.shape[0], 2 * level.pieces * level.count + 1, size, hd), kind)
        for level, other, kind in zip(crossing, others, sent_types)
    ]
    attended, grad, gsum, *rest = call(
        functools.partial(norm_kernel, group, crossing, scale, score_scale),
        "norm_and_crossing",
        [offs_rows, x, attn, lse, gain, stats] + others,
        outs,
        flops=10**7,
    )
    owns, parts = rest[: len(crossing)], rest[len(crossing) :]

    arrived = []
    for level, part in zip(crossing, parts):
        partial = [None] + [part[e] for e in range(part.shape[0])]
        for bit in reversed(range(level.bits)):
            half = 1 << bit
            came = [flip(block.astype(BF16), "ctx", low_bit + bit) for block in partial[half:]]
            partial = [
                c if b is None else b.astype(F32) + c.astype(F32)
                for b, c in zip(partial[:half], came)
            ]
        arrived.append(partial[0])
    if not alone:
        for axis, count, first in (("dp", dp_count, 0), ("ctx", ctx_count, low_bit)):
            for bit in range(first, count.bit_length() - 1):
                gsum = gsum + flip(gsum, axis, bit)

    main, kv = call(
        functools.partial(local_kernel, local, crossing, scale, score_scale),
        "local_backward",
        [offs_rows, x, attended, grad, lse, attn] + owns,
        [((pieces, 2, rate, size, hd), BF16), ((2,) + state, F32)],
        scratch=[(state, F32)] * 2,
        flops=3 * 10**8,
    )
    (packed,) = call(
        functools.partial(pack_kernel, crossing, fold, alone),
        "pack",
        [offs_rows, main, kv, gsum] + arrived,
        [((pieces, 4 * rate * size + TILE * fold, hd), BF16)],
        scratch=[((2,) + state, F32)],
    )
    if fold > 1:
        rows = packed[:, : 4 * rate * size].reshape(pieces, 4, rate, fold, short, hd)
        rows = rows.transpose(0, 3, 1, 2, 4, 5).reshape(group, 4 * tokens, hd)
        packed = jnp.concatenate([rows, packed[:, 4 * rate * size :].reshape(group, TILE, hd)], 1)
    back = exchange(packed)
    gains = jnp.sum(back[:, 4 * tokens :].astype(F32), axis=1)
    if alone:
        gains = gains + flip(gains, "dp", 0)
    gain_grad = gains.reshape(width) / math.sqrt(ctx_count * dp_count * tokens)
    row = ((1, tokens, width), BF16)
    dq, attended, dk, dv = call(
        functools.partial(join_kernel, rate),
        "join",
        [back],
        [row, row, row, row],
        flops=10**8,
    )
    return attended, dq, dk, dv, gain_grad


def solution(mesh):
    rows = P("dp", "ctx", None)
    return jax.shard_map(
        shards,
        mesh=mesh,
        in_specs=(rows, rows, rows, rows, P(), P()),
        out_specs=(rows, rows, rows, rows, P()),
        check_vma=False,
    )
```

```python
import functools
import math

import jax
import jax.numpy as jnp
from jax import lax
from jax.experimental import pallas as pl
from jax.experimental.pallas import tpu as pltpu
from jax.sharding import PartitionSpec as P

SPAN_A = 2
RATE_A = 1
SPAN_B = 4
RATE_B = 2
SPAN_C = 16
RATE_C = 8

EPSILON = 1e-05
LOG2E = math.log2(math.e)
TILE = 16
STAGED = 4
ORDER = (0, 7, 2, 6, 1, 5, 4, 3)
FAR_FIRST = (7, 6, 5, 3, 4, 2, 1)
F32 = jnp.float32
BF16 = jnp.bfloat16

NT = (((1,), (1,)), ((), ()))
TN = (((0,), (0,)), ((), ()))
NN = (((1,), (0,)), ((), ()))


def dot(left, right, dims):
    return lax.dot_general(left, right, dims, preferred_element_type=F32)


def two_parts(value):
    high = value.astype(BF16)
    return jnp.concatenate([high, (value - high.astype(F32)).astype(BF16)], axis=1)


def three_parts(row):
    total = jnp.broadcast_to(row, (TILE, row.shape[1]))
    high = total.astype(BF16).astype(F32)
    middle = (total - high).astype(BF16).astype(F32)
    low = total - high - middle
    place = lax.broadcasted_iota(jnp.int32, total.shape, 0)
    parts = jnp.where(place == 0, high, jnp.where(place == 1, middle, low))
    return jnp.where(place < 3, parts, 0.0).astype(BF16)


def row_order(tokens, rate, transposed):
    short = tokens // rate
    placed = lax.broadcasted_iota(jnp.int32, (tokens, tokens), 1 if transposed else 0)
    source = lax.broadcasted_iota(jnp.int32, (tokens, tokens), 0 if transposed else 1)
    return (source == (placed % short) * rate + placed // short).astype(BF16)


def split_kernel(rate, q_ref, k_ref, v_ref, g_ref, out_ref):
    group, _, tokens, hd = out_ref.shape
    order = row_order(tokens, rate, False)
    for t, ref in enumerate((q_ref, k_ref, v_ref, g_ref)):
        moved = dot(order, ref[0], NN).astype(BF16)
        for h in range(group):
            out_ref[h, t] = moved[:, h * hd : (h + 1) * hd]


def head_at(order, apart):
    place = lax.axis_index("ctx") % len(order) ^ apart
    return sum(order.index(device) * (place == device) for device in range(len(order)))


def split_apart_kernel(rate, order, aparts, rows_ref, *outs):
    _, tokens, hd = outs[0].shape
    change = row_order(tokens, rate, False)
    for apart, out_ref in zip(aparts, outs):
        columns = pl.ds(pl.multiple_of(head_at(order, apart) * hd, hd), hd)
        for t in range(4):
            out_ref[t] = dot(change, rows_ref[t, :, columns], NN).astype(BF16)


def collect_kernel(levels, order, offs_ref, *refs):
    blocks, x_ref, own_refs = refs[: len(order)], refs[len(order)], refs[len(order) + 1 :]
    for apart, block_ref in enumerate(blocks):
        spot = head_at(order, apart)
        x_ref[spot] = block_ref[...]
        for level, own_ref in zip(levels, own_refs):
            for i, b in enumerate(level.starts(offs_ref)):
                for t in range(2):
                    own_ref[spot, t, i] = block_ref[t + 1, b]


class Level:
    def __init__(self, index, span, rate, top_rate, fold, order):
        group = len(order)
        self.index = index
        self.rate = rate
        self.count = top_rate // rate
        self.crossing = span > group
        self.bits = span.bit_length() - group.bit_length()
        self.pieces = min(span, group) // fold
        self.segments = 1 if self.crossing else group // span
        self.spots = [order.index(device) // fold for device in range(0, group, fold)]

    def starts(self, offs):
        first = 0 if self.index == 0 else offs[self.index - 1, 0]
        return [first + self.rate * i for i in range(self.count)]

    def places(self, offs_ref, segment):
        low = segment * self.pieces
        spots = self.spots[low : low + self.pieces]
        return [(nb, b) for b in self.starts(offs_ref) for nb in spots]


def gather(read, places):
    return jnp.concatenate([read(nb, b) for nb, b in places], axis=0)


def scores_of(query, key, scale):
    return dot(query, key, NT) * scale


def forward(query, key, value, scale):
    hd = value.shape[1]
    scores = scores_of(query, key, scale)
    top = jnp.max(scores, axis=-1, keepdims=True)
    weights = jnp.exp2(scores - top).astype(BF16)
    both = dot(weights, jnp.concatenate([value, jnp.ones_like(value)], axis=1), NN)
    mixed, total = both[:, :hd], both[:, hd:]
    return mixed / total, top + jnp.log2(total)


def merge(mixed, lse, more, more_lse):
    top = jnp.maximum(lse, more_lse)
    left, right = jnp.exp2(lse - top), jnp.exp2(more_lse - top)
    total = left + right
    return (mixed * left + more * right) / total, top + jnp.log2(total)


def merge_into(o_ref, lse_ref, places, more, more_lse):
    mixed, lse = merge(
        gather(lambda nb, b: o_ref[nb, b], places),
        gather(lambda nb, b: lse_ref[nb, b], places),
        more,
        more_lse,
    )
    put(o_ref, places, mixed)
    put(lse_ref, places, lse)


def put(ref, places, rows):
    size = ref.shape[-2]
    for i, (nb, b) in enumerate(places):
        ref[nb, b] = rows[i * size : (i + 1) * size]


def add(ref, places, rows):
    size = ref.shape[-2]
    for i, (nb, b) in enumerate(places):
        ref[nb, b] += rows[i * size : (i + 1) * size]


def crossing_keys(places, x_ref, other_ref, t):
    found = [x_ref[nb, t, b] for nb, b in places]
    others, pieces, _, count = other_ref.shape[:4]
    found += [
        other_ref[e, nb, t - 1, i]
        for e in range(others)
        for i in range(count)
        for nb in range(pieces)
    ]
    return jnp.concatenate(found, axis=0)


def all_blocks(levels, offs_ref, x_ref, others):
    crossing = 0
    for level in levels:
        if level.crossing:
            other_ref = others[crossing]
            crossing += 1
        for segment in range(level.segments):
            places = level.places(offs_ref, segment)
            query = gather(lambda nb, b: x_ref[nb, 0, b], places)
            if level.crossing:
                key, value = (crossing_keys(places, x_ref, other_ref, t) for t in (1, 2))
            else:
                key, value = (gather(lambda nb, b, t=t: x_ref[nb, t, b], places) for t in (1, 2))
            yield level, places, query, key, value


def row_sums(attn, grad, gain):
    hd = attn.shape[-1]
    attn = attn.astype(BF16).astype(F32)
    scaled = grad.astype(F32) * gain
    total = jnp.sum(attn, axis=-1, keepdims=True)
    away = attn - total * (1.0 / hd)
    return (
        total,
        jnp.sum(away * away, axis=-1, keepdims=True),
        jnp.sum(scaled, axis=-1, keepdims=True),
        jnp.sum(scaled * away, axis=-1, keepdims=True),
    )


def forward_kernel(levels, scale, offs_ref, gain_ref, x_ref, o_ref, attn_ref, lse_ref, table_ref):
    pieces, rate, size, hd = o_ref.shape
    for level, places, query, key, value in all_blocks(levels, offs_ref, x_ref, ()):
        mixed, lse = forward(query, key, value, scale)
        if level.index == 0:
            put(o_ref, places, mixed)
            put(lse_ref, places, lse)
        else:
            merge_into(o_ref, lse_ref, places, mixed, lse)
    per = rate * size // hd
    chunks = pieces * per
    lane = lax.broadcasted_iota(jnp.int32, (hd, hd), 1)
    table = jnp.zeros((hd, hd), F32)
    for nb in range(pieces):
        attn_ref[nb] = o_ref[nb].astype(BF16)
        attn = attn_ref[nb].reshape(rate * size, hd)
        grad = x_ref[nb, 3].reshape(rate * size, hd)
        for part in range(per):
            rows = slice(part * hd, (part + 1) * hd)
            for i, column in enumerate(row_sums(attn[rows], grad[rows], gain_ref[...])):
                table = jnp.where(lane == i * chunks + nb * per + part, column, table)
    table_ref[...] = table


def crossing_forward_kernel(levels, scale, offs_ref, gain_ref, x_ref, o_in, attn_in, lse_in, table_ref, *refs):
    others, (attn_ref, lse_ref, stats_ref, o_ref, sums_ref) = refs[:-5], refs[-5:]
    pieces, rate, size, hd = o_ref.shape
    per = rate * size // hd
    chunks = pieces * per
    lane = lax.broadcasted_iota(jnp.int32, (size, hd), 1)
    if len(levels) > 1:
        o_ref[...] = o_in[...]
        o_in = o_ref
    attn_ref[...] = attn_in[...]
    lse_ref[...] = lse_in[...]
    sums_ref[...] = table_ref[...]
    for level, places, query, key, value in all_blocks(levels, offs_ref, x_ref, others):
        mixed, lse = merge(
            gather(lambda nb, b: o_in[nb, b], places),
            gather(lambda nb, b: lse_ref[nb, b], places),
            *forward(query, key, value, scale),
        )
        if len(levels) > 1:
            put(o_ref, places, mixed)
        put(attn_ref, places, mixed.astype(BF16))
        put(lse_ref, places, lse)
        sums = row_sums(
            mixed,
            gather(lambda nb, b: x_ref[nb, 3, b], places),
            gain_ref[...],
        )
        for j, (nb, b) in enumerate(places):
            chunk = nb * per + b * size // hd
            rows = pl.ds(pl.multiple_of(b * size % hd, size), size)
            table = sums_ref[rows, :]
            for i, column in enumerate(sums):
                table = jnp.where(lane == i * chunks + chunk, column[j * size : (j + 1) * size], table)
            sums_ref[rows, :] = table
    turned = sums_ref[...].T[: 4 * chunks]
    for peer in range(stats_ref.shape[0]):
        stats_ref[peer] = turned


def norm_kernel(heads, levels, scale, score_scale, offs_ref, x_ref, attn_ref, lse_ref, gain_ref, stats_ref, *refs):
    count = len(levels)
    others, refs = refs[:count], refs[count:]
    attended_ref, grad_ref, gsum_ref = refs[:3]
    own_refs, sent_refs = refs[3 : 3 + count], refs[3 + count :]
    pieces, rate, size, hd = attn_ref.shape
    chunks = pieces * rate * size // hd
    per = chunks // pieces
    width = heads * hd
    sums, squares, scaleds, products = (
        [stats_ref[h, i * chunks : (i + 1) * chunks, :] for h in range(heads)] for i in range(4)
    )
    mean = functools.reduce(jnp.add, sums) * (1.0 / width)
    apart = [total * (1.0 / hd) - mean for total in sums]
    variance = functools.reduce(
        jnp.add, [square + hd * a * a for square, a in zip(squares, apart)]
    ) * (1.0 / width)
    inverse = lax.rsqrt(variance + EPSILON)
    first = functools.reduce(jnp.add, scaleds) * (1.0 / width)
    second = (
        functools.reduce(jnp.add, [p + a * s for p, a, s in zip(products, apart, scaleds)])
        * (1.0 / width)
        * inverse
    )
    table = jnp.concatenate(
        [mean, inverse, first, second, jnp.zeros((hd - 4 * chunks, hd), F32)], axis=0
    )
    table = two_parts(table.T)
    lane = lax.broadcasted_iota(jnp.int32, (hd, 2 * hd), 1) % chunks
    picker = lax.broadcasted_iota(jnp.int32, (2 * hd, 4 * hd), 0) % hd // chunks
    picker = (picker == lax.broadcasted_iota(jnp.int32, (2 * hd, 4 * hd), 1) // hd).astype(BF16)
    picked = [jnp.where(lane == chunk, table, jnp.zeros_like(table)) for chunk in range(chunks)]
    columns = dot(jnp.concatenate(picked, axis=0), picker, NN)
    gsum = jnp.zeros((1, hd), F32)
    shape = (rate, size, hd)
    for nb in range(pieces):
        attn_all = attn_ref[nb].reshape(rate * size, hd).astype(F32)
        grad_all = x_ref[nb, 3].reshape(rate * size, hd).astype(F32)
        attended, grads = [], []
        for part in range(per):
            chunk = nb * per + part
            mean_c, inv_c, first_c, second_c = (
                columns[chunk * hd : (chunk + 1) * hd, i * hd : (i + 1) * hd] for i in range(4)
            )
            attn = attn_all[part * hd : (part + 1) * hd]
            upstream = grad_all[part * hd : (part + 1) * hd]
            normed = (attn - mean_c) * inv_c
            attended.append((normed * gain_ref[...]).astype(BF16))
            grad = (inv_c * (upstream * gain_ref[...] - first_c - normed * second_c)).astype(BF16)
            grads.append(grad)
            gsum = gsum + jnp.sum(upstream * normed, axis=0, keepdims=True)
        attended_ref[nb] = jnp.concatenate(attended, axis=0).reshape(shape)
        grad_ref[nb] = jnp.concatenate(grads, axis=0).reshape(shape)
    gsum_ref[...] = gsum
    blocks = list(all_blocks(levels, offs_ref, x_ref, others))
    deltas = []
    for _, places, *_ in blocks:
        grad = gather(lambda nb, b: grad_ref[nb, b], places).astype(F32)
        attn = gather(lambda nb, b: attn_ref[nb, b], places).astype(F32)
        delta = jnp.sum(grad * attn, axis=-1, keepdims=True)
        deltas.append(jnp.broadcast_to(delta, grad.shape))
    results = backward(blocks, grad_ref, lse_ref, deltas, scale, score_scale)
    for i, parts in enumerate(results):
        own = parts[0].shape[0]
        level, coded = levels[i], three_parts(gsum)
        steps = level.count
        for t, part in enumerate(parts):
            own_refs[i][t] = part[:own]
            if t > 0:
                low = own
                for e in range(sent_refs[i].shape[0]):
                    for step in range(steps):
                        for nb in range(level.pieces):
                            rows = part[low : low + size].astype(sent_refs[i].dtype)
                            sent_refs[i][e, (nb * 2 + t - 1) * steps + step] = rows
                            low += size
                    sent_refs[i][e, 2 * steps * level.pieces] = coded.astype(sent_refs[i].dtype)


def backward(blocks, grad_ref, lse_ref, deltas, scale, score_scale):
    def wide(column, key):
        return jnp.concatenate([column] * (key.shape[0] // column.shape[1]), axis=1)

    grads = [gather(lambda nb, b: grad_ref[nb, b], places) for _, places, _, _, _ in blocks]
    scores = [scores_of(query, key, score_scale) for _, _, query, key, _ in blocks]
    prob_grads = [dot(grad, block[4], NT) for grad, block in zip(grads, blocks)]
    probs = [
        jnp.exp2(score - wide(gather(lambda nb, b: lse_ref[nb, b], places), key))
        for score, (_, places, _, key, _) in zip(scores, blocks)
    ]
    score_grads = [
        (prob * (prob_grad - wide(delta, block[3]))).astype(BF16)
        for prob, prob_grad, delta, block in zip(probs, prob_grads, deltas, blocks)
    ]
    queries = [dot(each, block[3], NN) * scale for each, block in zip(score_grads, blocks)]
    keys = [dot(each, block[2], TN) * scale for each, block in zip(score_grads, blocks)]
    values = [dot(prob.astype(BF16), grad, TN) for prob, grad in zip(probs, grads)]
    return list(zip(queries, keys, values))


def local_kernel(levels, crossing, scale, score_scale, offs_ref, x_ref, attended_ref, grad_ref, lse_ref, attn_ref, *refs):
    own_refs, (out_ref, kv_ref, dq_ref, delta_ref) = refs[: len(crossing)], refs[len(crossing) :]
    pieces, rate, size, hd = dq_ref.shape
    products = [
        two_parts((grad_ref[nb].astype(F32) * attn_ref[nb].astype(F32)).reshape(rate * size, hd))
        for nb in range(pieces)
    ]
    sums = dot(jnp.concatenate(products, axis=0), jnp.ones((2 * hd, hd), BF16), NN)
    delta_ref[...] = sums.reshape(delta_ref.shape)
    accumulators = (dq_ref, kv_ref.at[0], kv_ref.at[1])
    blocks = list(all_blocks(levels, offs_ref, x_ref, ()))
    for low in range(0, len(blocks), STAGED):
        some = blocks[low : low + STAGED]
        deltas = [gather(lambda nb, b: delta_ref[nb, b], places) for _, places, *_ in some]
        results = backward(some, grad_ref, lse_ref, deltas, scale, score_scale)
        for i, ref in enumerate(accumulators):
            for (level, places, *_), parts in zip(some, results):
                (put if level.index == 0 else add)(ref, places, parts[i])
    for level, own_ref in zip(crossing, own_refs):
        places = level.places(offs_ref, 0)
        for t, ref in enumerate(accumulators):
            add(ref, places, own_ref[t])
    out_ref[:, 0] = dq_ref[...].astype(BF16)
    out_ref[:, 1] = attended_ref[...]


def pack_kernel(crossing, fold, alone, offs_ref, main_ref, kv_in, gsum_ref, *refs):
    arrived_refs, (out_ref, kv_ref) = refs[:-2], refs[-2:]
    pieces, _, rate, size, hd = main_ref.shape
    rows = rate * size
    kv_ref[...] = kv_in[...]
    for level, arrived_ref in zip(crossing, arrived_refs):
        for i, b in enumerate(level.starts(offs_ref)):
            for nb in range(level.pieces):
                for t in range(2):
                    block = (nb * 2 + t) * level.count + i
                    kv_ref[t, nb, b] += arrived_ref[block].astype(F32)
    total = gsum_ref[...]
    if alone:
        other = arrived_refs[0][arrived_refs[0].shape[0] - 1]
        total = total + jnp.sum(other.astype(F32), axis=0, keepdims=True)
    coded = three_parts(total)
    for nb in range(pieces):
        for t in range(2):
            out_ref[nb, t * rows : (t + 1) * rows] = main_ref[nb, t].reshape(rows, hd)
            out_ref[nb, (t + 2) * rows : (t + 3) * rows] = (
                kv_ref[t, nb].reshape(rows, hd).astype(BF16)
            )
        for f in range(fold):
            out_ref[nb, 4 * rows + f * TILE : 4 * rows + (f + 1) * TILE] = coded


def join_kernel(rate, in_ref, dq_ref, attended_ref, dk_ref, dv_ref):
    group, _, hd = in_ref.shape
    tokens = dq_ref.shape[1]
    order = row_order(tokens, rate, True)
    for t, ref in enumerate((dq_ref, attended_ref, dk_ref, dv_ref)):
        for h in range(group):
            moved = dot(order, in_ref[h, t * tokens : (t + 1) * tokens, :], NN)
            ref[0, :, h * hd : (h + 1) * hd] = moved.astype(BF16)


VMEM = pl.BlockSpec(memory_space=pltpu.VMEM)


def call(body, name, inputs, outputs, scratch=(), flops=0, limit=24):
    shapes = [jax.ShapeDtypeStruct(*output) for output in outputs]
    moved = sum(x.size * x.dtype.itemsize for x in list(inputs) + shapes)
    return list(pl.pallas_call(
        body,
        name=name,
        in_specs=[VMEM] * len(inputs),
        out_specs=[VMEM] * len(shapes),
        out_shape=shapes,
        scratch_shapes=[pltpu.VMEM(*each) for each in scratch],
        cost_estimate=pl.CostEstimate(flops=flops, bytes_accessed=moved, transcendentals=0),
        compiler_params=pltpu.CompilerParams(vmem_limit_bytes=limit * 1024 * 1024),
    )(*inputs))


def flip(value, axis, bit):
    pairs = [(source, source ^ (1 << bit)) for source in range(lax.axis_size(axis))]
    return lax.ppermute(value, axis, pairs)


def shards(queries, key_rows, value_rows, out_grad, norm_gain, offsets):
    tokens, width = queries.shape[1:]
    group = offsets.shape[1]
    hd = width // group
    ctx_count = lax.axis_size("ctx")
    dp_count = lax.axis_size("dp")
    scale = hd ** (-0.5)
    score_scale = scale * LOG2E
    spans = [
        (SPAN_A, RATE_A),
        (SPAN_B, RATE_B),
        (SPAN_C, RATE_C),
        (ctx_count // 2, ctx_count // 4),
    ]
    rate = max(r for _, r in spans)
    short = tokens // rate
    fold = max(1, TILE // short)
    size = short * fold
    pieces = group // fold
    order = list(ORDER) if group == len(ORDER) and fold == 1 else list(range(group))
    levels = [Level(i, span, r, rate, fold, order) for i, (span, r) in enumerate(spans)]
    local = [level for level in levels if not level.crossing]
    crossing = [level for level in levels if level.crossing]
    groups = [[low + device for device in order] for low in range(0, ctx_count, group)]
    low_bit = group.bit_length() - 1

    def exchange(value):
        return lax.all_to_all(value, "ctx", 0, 0, tiled=True, axis_index_groups=groups)

    place = lax.axis_index("ctx") % group
    head = sum(order.index(device) * (place == device) for device in range(group))
    offs = lax.dynamic_slice(offsets, (0, head), (offsets.shape[0], 1))
    offs_rows = jnp.broadcast_to(offs, (offsets.shape[0], hd))
    gain = lax.dynamic_slice(norm_gain, (head * hd,), (hd,))[None]

    alone = ctx_count == 2 * group and dp_count == 2 and size == TILE and len(crossing) == 1
    alone = alone and group == len(ORDER)
    if alone:
        whole = jnp.concatenate([queries, key_rows, value_rows, out_grad], axis=0)
        far = [None] * group
        for aparts in (FAR_FIRST + (0,),):
            made = call(
                functools.partial(split_apart_kernel, rate, order, aparts),
                "split",
                [whole],
                [((4, tokens, hd), BF16)] * len(aparts),
            )
            for apart, block in zip(aparts, made):
                far[apart] = block
        for apart in FAR_FIRST:
            pairs = [(source, source ^ apart) for source in range(ctx_count)]
            far[apart] = lax.ppermute(far[apart], "ctx", pairs)
        x, *owns = call(
            functools.partial(collect_kernel, crossing, order),
            "collect",
            [offs_rows] + [block.reshape(4, rate, size, hd) for block in far],
            [((pieces, 4, rate, size, hd), BF16)]
            + [((pieces, 2, level.count, size, hd), BF16) for level in crossing],
        )
    else:
        (sent,) = call(
            functools.partial(split_kernel, rate),
            "split",
            [queries, key_rows, value_rows, out_grad],
            [((group, 4, tokens, hd), BF16)],
            limit=60,
        )
        x = exchange(sent)
        if fold > 1:
            x = x.reshape(pieces, fold, 4, rate, short, hd).transpose(0, 2, 3, 1, 4, 5)
        x = x.reshape(pieces, 4, rate, size, hd)
        owns = []
        for level in crossing:
            own = [
                lax.dynamic_slice(x, (0, 1, b, 0, 0), (pieces, 2, 1, size, hd))
                for b in level.starts(offs)
            ]
            owns.append(jnp.concatenate(own, axis=2))

    others = []
    for level, own in zip(crossing, owns):
        blocks = [own]
        for bit in range(level.bits):
            blocks += [flip(block, "ctx", low_bit + bit) for block in blocks]
        others.append(jnp.stack(blocks[1:]))

    state = (pieces, rate, size, hd)
    chunks = group * tokens // hd
    o, attn, lse, table = call(
        functools.partial(forward_kernel, local, score_scale),
        "local_forward",
        [offs_rows, gain, x],
        [(state, F32), (state, BF16), (state, F32), ((hd, hd), F32)],
        flops=10**8,
    )
    attn, lse, stats = call(
        functools.partial(crossing_forward_kernel, crossing, score_scale),
        "crossing_forward",
        [offs_rows, gain, x, o, attn, lse, table] + others,
        [(state, BF16), (state, F32), ((group, 4 * chunks, hd), F32)],
        scratch=[(state, F32), ((hd, hd), F32)],
    )
    stats = exchange(stats)
    outs = [(state, BF16), (state, BF16), ((1, hd), F32)]
    outs += [((3, pieces * level.count * size, hd), F32) for level in crossing]
    sent_types = [BF16 if level.bits == 1 else F32 for level in crossing]
    outs += [
        ((other.shape[0], 2 * level.pieces * level.count + 1, size, hd), kind)
        for level, other, kind in zip(crossing, others, sent_types)
    ]
    attended, grad, gsum, *rest = call(
        functools.partial(norm_kernel, group, crossing, scale, score_scale),
        "norm_and_crossing",
        [offs_rows, x, attn, lse, gain, stats] + others,
        outs,
        flops=10**7,
    )
    owns, parts = rest[: len(crossing)], rest[len(crossing) :]

    arrived = []
    for level, part in zip(crossing, parts):
        partial = [None] + [part[e] for e in range(part.shape[0])]
        for bit in reversed(range(level.bits)):
            half = 1 << bit
            came = [flip(block.astype(BF16), "ctx", low_bit + bit) for block in partial[half:]]
            partial = [
                c if b is None else b.astype(F32) + c.astype(F32)
                for b, c in zip(partial[:half], came)
            ]
        arrived.append(partial[0])
    if not alone:
        for axis, count, first in (("dp", dp_count, 0), ("ctx", ctx_count, low_bit)):
            for bit in range(first, count.bit_length() - 1):
                gsum = gsum + flip(gsum, axis, bit)

    main, kv = call(
        functools.partial(local_kernel, local, crossing, scale, score_scale),
        "local_backward",
        [offs_rows, x, attended, grad, lse, attn] + owns,
        [((pieces, 2, rate, size, hd), BF16), ((2,) + state, F32)],
        scratch=[(state, F32)] * 2,
        flops=3 * 10**8,
    )
    (packed,) = call(
        functools.partial(pack_kernel, crossing, fold, alone),
        "pack",
        [offs_rows, main, kv, gsum] + arrived,
        [((pieces, 4 * rate * size + TILE * fold, hd), BF16)],
        scratch=[((2,) + state, F32)],
    )
    if fold > 1:
        rows = packed[:, : 4 * rate * size].reshape(pieces, 4, rate, fold, short, hd)
        rows = rows.transpose(0, 3, 1, 2, 4, 5).reshape(group, 4 * tokens, hd)
        packed = jnp.concatenate([rows, packed[:, 4 * rate * size :].reshape(group, TILE, hd)], 1)
    back = exchange(packed)
    gains = jnp.sum(back[:, 4 * tokens :].astype(F32), axis=1)
    if alone:
        gains = gains + flip(gains, "dp", 0)
    gain_grad = gains.reshape(width) / math.sqrt(ctx_count * dp_count * tokens)
    row = ((1, tokens, width), BF16)
    dq, attended, dk, dv = call(
        functools.partial(join_kernel, rate),
        "join",
        [back],
        [row, row, row, row],
        flops=10**8,
    )
    return attended, dq, dk, dv, gain_grad


def solution(mesh):
    rows = P("dp", "ctx", None)
    return jax.shard_map(
        shards,
        mesh=mesh,
        in_specs=(rows, rows, rows, rows, P(), P()),
        out_specs=(rows, rows, rows, rows, P()),
        check_vma=False,
    )
```

```python
import functools
import math

import jax
import jax.numpy as jnp
from jax import lax
from jax.experimental import pallas as pl
from jax.experimental.pallas import tpu as pltpu
from jax.sharding import PartitionSpec as P

SPAN_A = 2
RATE_A = 1
SPAN_B = 4
RATE_B = 2
SPAN_C = 16
RATE_C = 8

EPSILON = 1e-05
LOG2E = math.log2(math.e)
TILE = 16
STAGED = 4
ORDER = (0, 7, 2, 6, 1, 5, 4, 3)
FAR_FIRST = (4, 7, 6, 5, 3, 2, 1)
F32 = jnp.float32
BF16 = jnp.bfloat16

NT = (((1,), (1,)), ((), ()))
TN = (((0,), (0,)), ((), ()))
NN = (((1,), (0,)), ((), ()))


def dot(left, right, dims):
    return lax.dot_general(left, right, dims, preferred_element_type=F32)


def two_parts(value):
    high = value.astype(BF16)
    return jnp.concatenate([high, (value - high.astype(F32)).astype(BF16)], axis=1)


def three_parts(row):
    total = jnp.broadcast_to(row, (TILE, row.shape[1]))
    high = total.astype(BF16).astype(F32)
    middle = (total - high).astype(BF16).astype(F32)
    low = total - high - middle
    place = lax.broadcasted_iota(jnp.int32, total.shape, 0)
    parts = jnp.where(place == 0, high, jnp.where(place == 1, middle, low))
    return jnp.where(place < 3, parts, 0.0).astype(BF16)


def row_order(tokens, rate, transposed):
    short = tokens // rate
    placed = lax.broadcasted_iota(jnp.int32, (tokens, tokens), 1 if transposed else 0)
    source = lax.broadcasted_iota(jnp.int32, (tokens, tokens), 0 if transposed else 1)
    return (source == (placed % short) * rate + placed // short).astype(BF16)


def split_kernel(rate, q_ref, k_ref, v_ref, g_ref, out_ref):
    group, _, tokens, hd = out_ref.shape
    order = row_order(tokens, rate, False)
    for t, ref in enumerate((q_ref, k_ref, v_ref, g_ref)):
        moved = dot(order, ref[0], NN).astype(BF16)
        for h in range(group):
            out_ref[h, t] = moved[:, h * hd : (h + 1) * hd]


def head_at(order, apart):
    place = lax.axis_index("ctx") % len(order) ^ apart
    return sum(order.index(device) * (place == device) for device in range(len(order)))


def split_apart_kernel(rate, order, aparts, rows_ref, *outs):
    _, tokens, hd = outs[0].shape
    change = row_order(tokens, rate, False)
    for apart, out_ref in zip(aparts, outs):
        columns = pl.ds(pl.multiple_of(head_at(order, apart) * hd, hd), hd)
        for t in range(4):
            out_ref[t] = dot(change, rows_ref[t, :, columns], NN).astype(BF16)


def collect_kernel(levels, order, offs_ref, *refs):
    blocks, x_ref, own_refs = refs[: len(order)], refs[len(order)], refs[len(order) + 1 :]
    for apart, block_ref in enumerate(blocks):
        spot = head_at(order, apart)
        x_ref[spot] = block_ref[...]
        for level, own_ref in zip(levels, own_refs):
            for i, b in enumerate(level.starts(offs_ref)):
                for t in range(2):
                    own_ref[spot, t, i] = block_ref[t + 1, b]


class Level:
    def __init__(self, index, span, rate, top_rate, fold, order):
        group = len(order)
        self.index = index
        self.rate = rate
        self.count = top_rate // rate
        self.crossing = span > group
        self.bits = span.bit_length() - group.bit_length()
        self.pieces = min(span, group) // fold
        self.segments = 1 if self.crossing else group // span
        self.spots = [order.index(device) // fold for device in range(0, group, fold)]

    def starts(self, offs):
        first = 0 if self.index == 0 else offs[self.index - 1, 0]
        return [first + self.rate * i for i in range(self.count)]

    def places(self, offs_ref, segment):
        low = segment * self.pieces
        spots = self.spots[low : low + self.pieces]
        return [(nb, b) for b in self.starts(offs_ref) for nb in spots]


def gather(read, places):
    return jnp.concatenate([read(nb, b) for nb, b in places], axis=0)


def scores_of(query, key, scale):
    return dot(query, key, NT) * scale


def forward(query, key, value, scale):
    hd = value.shape[1]
    scores = scores_of(query, key, scale)
    top = jnp.max(scores, axis=-1, keepdims=True)
    weights = jnp.exp2(scores - top).astype(BF16)
    both = dot(weights, jnp.concatenate([value, jnp.ones_like(value)], axis=1), NN)
    mixed, total = both[:, :hd], both[:, hd:]
    return mixed / total, top + jnp.log2(total)


def merge(mixed, lse, more, more_lse):
    top = jnp.maximum(lse, more_lse)
    left, right = jnp.exp2(lse - top), jnp.exp2(more_lse - top)
    total = left + right
    return (mixed * left + more * right) / total, top + jnp.log2(total)


def merge_into(o_ref, lse_ref, places, more, more_lse):
    mixed, lse = merge(
        gather(lambda nb, b: o_ref[nb, b], places),
        gather(lambda nb, b: lse_ref[nb, b], places),
        more,
        more_lse,
    )
    put(o_ref, places, mixed)
    put(lse_ref, places, lse)


def put(ref, places, rows):
    size = ref.shape[-2]
    for i, (nb, b) in enumerate(places):
        ref[nb, b] = rows[i * size : (i + 1) * size]


def add(ref, places, rows):
    size = ref.shape[-2]
    for i, (nb, b) in enumerate(places):
        ref[nb, b] += rows[i * size : (i + 1) * size]


def crossing_keys(places, x_ref, other_ref, t):
    found = [x_ref[nb, t, b] for nb, b in places]
    others, pieces, _, count = other_ref.shape[:4]
    found += [
        other_ref[e, nb, t - 1, i]
        for e in range(others)
        for i in range(count)
        for nb in range(pieces)
    ]
    return jnp.concatenate(found, axis=0)


def all_blocks(levels, offs_ref, x_ref, others):
    crossing = 0
    for level in levels:
        if level.crossing:
            other_ref = others[crossing]
            crossing += 1
        for segment in range(level.segments):
            places = level.places(offs_ref, segment)
            query = gather(lambda nb, b: x_ref[nb, 0, b], places)
            if level.crossing:
                key, value = (crossing_keys(places, x_ref, other_ref, t) for t in (1, 2))
            else:
                key, value = (gather(lambda nb, b, t=t: x_ref[nb, t, b], places) for t in (1, 2))
            yield level, places, query, key, value


def row_sums(attn, grad, gain):
    hd = attn.shape[-1]
    attn = attn.astype(BF16).astype(F32)
    scaled = grad.astype(F32) * gain
    total = jnp.sum(attn, axis=-1, keepdims=True)
    away = attn - total * (1.0 / hd)
    return (
        total,
        jnp.sum(away * away, axis=-1, keepdims=True),
        jnp.sum(scaled, axis=-1, keepdims=True),
        jnp.sum(scaled * away, axis=-1, keepdims=True),
    )


def forward_kernel(levels, scale, offs_ref, gain_ref, x_ref, o_ref, attn_ref, lse_ref, table_ref):
    pieces, rate, size, hd = o_ref.shape
    for level, places, query, key, value in all_blocks(levels, offs_ref, x_ref, ()):
        mixed, lse = forward(query, key, value, scale)
        if level.index == 0:
            put(o_ref, places, mixed)
            put(lse_ref, places, lse)
        else:
            merge_into(o_ref, lse_ref, places, mixed, lse)
    per = rate * size // hd
    chunks = pieces * per
    lane = lax.broadcasted_iota(jnp.int32, (hd, hd), 1)
    table = jnp.zeros((hd, hd), F32)
    for nb in range(pieces):
        attn_ref[nb] = o_ref[nb].astype(BF16)
        attn = attn_ref[nb].reshape(rate * size, hd)
        grad = x_ref[nb, 3].reshape(rate * size, hd)
        for part in range(per):
            rows = slice(part * hd, (part + 1) * hd)
            for i, column in enumerate(row_sums(attn[rows], grad[rows], gain_ref[...])):
                table = jnp.where(lane == i * chunks + nb * per + part, column, table)
    table_ref[...] = table


def crossing_forward_kernel(levels, scale, offs_ref, gain_ref, x_ref, o_in, attn_in, lse_in, table_ref, *refs):
    others, (attn_ref, lse_ref, stats_ref, o_ref, sums_ref) = refs[:-5], refs[-5:]
    pieces, rate, size, hd = o_ref.shape
    per = rate * size // hd
    chunks = pieces * per
    lane = lax.broadcasted_iota(jnp.int32, (size, hd), 1)
    if len(levels) > 1:
        o_ref[...] = o_in[...]
        o_in = o_ref
    attn_ref[...] = attn_in[...]
    lse_ref[...] = lse_in[...]
    sums_ref[...] = table_ref[...]
    for level, places, query, key, value in all_blocks(levels, offs_ref, x_ref, others):
        mixed, lse = merge(
            gather(lambda nb, b: o_in[nb, b], places),
            gather(lambda nb, b: lse_ref[nb, b], places),
            *forward(query, key, value, scale),
        )
        if len(levels) > 1:
            put(o_ref, places, mixed)
        put(attn_ref, places, mixed.astype(BF16))
        put(lse_ref, places, lse)
        sums = row_sums(
            mixed,
            gather(lambda nb, b: x_ref[nb, 3, b], places),
            gain_ref[...],
        )
        for j, (nb, b) in enumerate(places):
            chunk = nb * per + b * size // hd
            rows = pl.ds(pl.multiple_of(b * size % hd, size), size)
            table = sums_ref[rows, :]
            for i, column in enumerate(sums):
                table = jnp.where(lane == i * chunks + chunk, column[j * size : (j + 1) * size], table)
            sums_ref[rows, :] = table
    turned = sums_ref[...].T[: 4 * chunks]
    for peer in range(stats_ref.shape[0]):
        stats_ref[peer] = turned


def norm_kernel(heads, levels, scale, score_scale, offs_ref, x_ref, attn_ref, lse_ref, gain_ref, stats_ref, *refs):
    count = len(levels)
    others, refs = refs[:count], refs[count:]
    attended_ref, grad_ref, gsum_ref = refs[:3]
    own_refs, sent_refs = refs[3 : 3 + count], refs[3 + count :]
    pieces, rate, size, hd = attn_ref.shape
    chunks = pieces * rate * size // hd
    per = chunks // pieces
    width = heads * hd
    sums, squares, scaleds, products = (
        [stats_ref[h, i * chunks : (i + 1) * chunks, :] for h in range(heads)] for i in range(4)
    )
    mean = functools.reduce(jnp.add, sums) * (1.0 / width)
    apart = [total * (1.0 / hd) - mean for total in sums]
    variance = functools.reduce(
        jnp.add, [square + hd * a * a for square, a in zip(squares, apart)]
    ) * (1.0 / width)
    inverse = lax.rsqrt(variance + EPSILON)
    first = functools.reduce(jnp.add, scaleds) * (1.0 / width)
    second = (
        functools.reduce(jnp.add, [p + a * s for p, a, s in zip(products, apart, scaleds)])
        * (1.0 / width)
        * inverse
    )
    table = jnp.concatenate(
        [mean, inverse, first, second, jnp.zeros((hd - 4 * chunks, hd), F32)], axis=0
    )
    table = two_parts(table.T)
    lane = lax.broadcasted_iota(jnp.int32, (hd, 2 * hd), 1) % chunks
    picker = lax.broadcasted_iota(jnp.int32, (2 * hd, 4 * hd), 0) % hd // chunks
    picker = (picker == lax.broadcasted_iota(jnp.int32, (2 * hd, 4 * hd), 1) // hd).astype(BF16)
    picked = [jnp.where(lane == chunk, table, jnp.zeros_like(table)) for chunk in range(chunks)]
    columns = dot(jnp.concatenate(picked, axis=0), picker, NN)
    gsum = jnp.zeros((1, hd), F32)
    shape = (rate, size, hd)
    for nb in range(pieces):
        attn_all = attn_ref[nb].reshape(rate * size, hd).astype(F32)
        grad_all = x_ref[nb, 3].reshape(rate * size, hd).astype(F32)
        attended, grads = [], []
        for part in range(per):
            chunk = nb * per + part
            mean_c, inv_c, first_c, second_c = (
                columns[chunk * hd : (chunk + 1) * hd, i * hd : (i + 1) * hd] for i in range(4)
            )
            attn = attn_all[part * hd : (part + 1) * hd]
            upstream = grad_all[part * hd : (part + 1) * hd]
            normed = (attn - mean_c) * inv_c
            attended.append((normed * gain_ref[...]).astype(BF16))
            grad = (inv_c * (upstream * gain_ref[...] - first_c - normed * second_c)).astype(BF16)
            grads.append(grad)
            gsum = gsum + jnp.sum(upstream * normed, axis=0, keepdims=True)
        attended_ref[nb] = jnp.concatenate(attended, axis=0).reshape(shape)
        grad_ref[nb] = jnp.concatenate(grads, axis=0).reshape(shape)
    gsum_ref[...] = gsum
    blocks = list(all_blocks(levels, offs_ref, x_ref, others))
    deltas = []
    for _, places, *_ in blocks:
        grad = gather(lambda nb, b: grad_ref[nb, b], places).astype(F32)
        attn = gather(lambda nb, b: attn_ref[nb, b], places).astype(F32)
        delta = jnp.sum(grad * attn, axis=-1, keepdims=True)
        deltas.append(jnp.broadcast_to(delta, grad.shape))
    results = backward(blocks, grad_ref, lse_ref, deltas, scale, score_scale)
    for i, parts in enumerate(results):
        own = parts[0].shape[0]
        level, coded = levels[i], three_parts(gsum)
        steps = level.count
        for t, part in enumerate(parts):
            own_refs[i][t] = part[:own]
            if t > 0:
                low = own
                for e in range(sent_refs[i].shape[0]):
                    for step in range(steps):
                        for nb in range(level.pieces):
                            rows = part[low : low + size].astype(sent_refs[i].dtype)
                            sent_refs[i][e, (nb * 2 + t - 1) * steps + step] = rows
                            low += size
                    sent_refs[i][e, 2 * steps * level.pieces] = coded.astype(sent_refs[i].dtype)


def backward(blocks, grad_ref, lse_ref, deltas, scale, score_scale):
    def wide(column, key):
        return jnp.concatenate([column] * (key.shape[0] // column.shape[1]), axis=1)

    grads = [gather(lambda nb, b: grad_ref[nb, b], places) for _, places, _, _, _ in blocks]
    scores = [scores_of(query, key, score_scale) for _, _, query, key, _ in blocks]
    prob_grads = [dot(grad, block[4], NT) for grad, block in zip(grads, blocks)]
    probs = [
        jnp.exp2(score - wide(gather(lambda nb, b: lse_ref[nb, b], places), key))
        for score, (_, places, _, key, _) in zip(scores, blocks)
    ]
    score_grads = [
        (prob * (prob_grad - wide(delta, block[3]))).astype(BF16)
        for prob, prob_grad, delta, block in zip(probs, prob_grads, deltas, blocks)
    ]
    queries = [dot(each, block[3], NN) * scale for each, block in zip(score_grads, blocks)]
    keys = [dot(each, block[2], TN) * scale for each, block in zip(score_grads, blocks)]
    values = [dot(prob.astype(BF16), grad, TN) for prob, grad in zip(probs, grads)]
    return list(zip(queries, keys, values))


def local_kernel(levels, crossing, scale, score_scale, offs_ref, x_ref, attended_ref, grad_ref, lse_ref, attn_ref, *refs):
    own_refs, (out_ref, kv_ref, dq_ref, delta_ref) = refs[: len(crossing)], refs[len(crossing) :]
    pieces, rate, size, hd = dq_ref.shape
    products = [
        two_parts((grad_ref[nb].astype(F32) * attn_ref[nb].astype(F32)).reshape(rate * size, hd))
        for nb in range(pieces)
    ]
    sums = dot(jnp.concatenate(products, axis=0), jnp.ones((2 * hd, hd), BF16), NN)
    delta_ref[...] = sums.reshape(delta_ref.shape)
    accumulators = (dq_ref, kv_ref.at[0], kv_ref.at[1])
    blocks = list(all_blocks(levels, offs_ref, x_ref, ()))
    for low in range(0, len(blocks), STAGED):
        some = blocks[low : low + STAGED]
        deltas = [gather(lambda nb, b: delta_ref[nb, b], places) for _, places, *_ in some]
        results = backward(some, grad_ref, lse_ref, deltas, scale, score_scale)
        for i, ref in enumerate(accumulators):
            for (level, places, *_), parts in zip(some, results):
                (put if level.index == 0 else add)(ref, places, parts[i])
    for level, own_ref in zip(crossing, own_refs):
        places = level.places(offs_ref, 0)
        for t, ref in enumerate(accumulators):
            add(ref, places, own_ref[t])
    out_ref[:, 0] = dq_ref[...].astype(BF16)
    out_ref[:, 1] = attended_ref[...]


def pack_kernel(crossing, fold, alone, offs_ref, main_ref, kv_in, gsum_ref, *refs):
    arrived_refs, (out_ref, kv_ref) = refs[:-2], refs[-2:]
    pieces, _, rate, size, hd = main_ref.shape
    rows = rate * size
    kv_ref[...] = kv_in[...]
    for level, arrived_ref in zip(crossing, arrived_refs):
        for i, b in enumerate(level.starts(offs_ref)):
            for nb in range(level.pieces):
                for t in range(2):
                    block = (nb * 2 + t) * level.count + i
                    kv_ref[t, nb, b] += arrived_ref[block].astype(F32)
    total = gsum_ref[...]
    if alone:
        other = arrived_refs[0][arrived_refs[0].shape[0] - 1]
        total = total + jnp.sum(other.astype(F32), axis=0, keepdims=True)
    coded = three_parts(total)
    for nb in range(pieces):
        for t in range(2):
            out_ref[nb, t * rows : (t + 1) * rows] = main_ref[nb, t].reshape(rows, hd)
            out_ref[nb, (t + 2) * rows : (t + 3) * rows] = (
                kv_ref[t, nb].reshape(rows, hd).astype(BF16)
            )
        for f in range(fold):
            out_ref[nb, 4 * rows + f * TILE : 4 * rows + (f + 1) * TILE] = coded


def join_kernel(rate, in_ref, dq_ref, attended_ref, dk_ref, dv_ref):
    group, _, hd = in_ref.shape
    tokens = dq_ref.shape[1]
    order = row_order(tokens, rate, True)
    for t, ref in enumerate((dq_ref, attended_ref, dk_ref, dv_ref)):
        for h in range(group):
            moved = dot(order, in_ref[h, t * tokens : (t + 1) * tokens, :], NN)
            ref[0, :, h * hd : (h + 1) * hd] = moved.astype(BF16)


VMEM = pl.BlockSpec(memory_space=pltpu.VMEM)


def call(body, name, inputs, outputs, scratch=(), flops=0, limit=24):
    shapes = [jax.ShapeDtypeStruct(*output) for output in outputs]
    moved = sum(x.size * x.dtype.itemsize for x in list(inputs) + shapes)
    return list(pl.pallas_call(
        body,
        name=name,
        in_specs=[VMEM] * len(inputs),
        out_specs=[VMEM] * len(shapes),
        out_shape=shapes,
        scratch_shapes=[pltpu.VMEM(*each) for each in scratch],
        cost_estimate=pl.CostEstimate(flops=flops, bytes_accessed=moved, transcendentals=0),
        compiler_params=pltpu.CompilerParams(vmem_limit_bytes=limit * 1024 * 1024),
    )(*inputs))


def flip(value, axis, bit):
    pairs = [(source, source ^ (1 << bit)) for source in range(lax.axis_size(axis))]
    return lax.ppermute(value, axis, pairs)


def shards(queries, key_rows, value_rows, out_grad, norm_gain, offsets):
    tokens, width = queries.shape[1:]
    group = offsets.shape[1]
    hd = width // group
    ctx_count = lax.axis_size("ctx")
    dp_count = lax.axis_size("dp")
    scale = hd ** (-0.5)
    score_scale = scale * LOG2E
    spans = [
        (SPAN_A, RATE_A),
        (SPAN_B, RATE_B),
        (SPAN_C, RATE_C),
        (ctx_count // 2, ctx_count // 4),
    ]
    rate = max(r for _, r in spans)
    short = tokens // rate
    fold = max(1, TILE // short)
    size = short * fold
    pieces = group // fold
    order = list(ORDER) if group == len(ORDER) and fold == 1 else list(range(group))
    levels = [Level(i, span, r, rate, fold, order) for i, (span, r) in enumerate(spans)]
    local = [level for level in levels if not level.crossing]
    crossing = [level for level in levels if level.crossing]
    groups = [[low + device for device in order] for low in range(0, ctx_count, group)]
    low_bit = group.bit_length() - 1

    def exchange(value):
        return lax.all_to_all(value, "ctx", 0, 0, tiled=True, axis_index_groups=groups)

    place = lax.axis_index("ctx") % group
    head = sum(order.index(device) * (place == device) for device in range(group))
    offs = lax.dynamic_slice(offsets, (0, head), (offsets.shape[0], 1))
    offs_rows = jnp.broadcast_to(offs, (offsets.shape[0], hd))
    gain = lax.dynamic_slice(norm_gain, (head * hd,), (hd,))[None]

    alone = ctx_count == 2 * group and dp_count == 2 and size == TILE and len(crossing) == 1
    alone = alone and group == len(ORDER)
    if alone:
        whole = jnp.concatenate([queries, key_rows, value_rows, out_grad], axis=0)
        far = [None] * group
        for aparts in (FAR_FIRST + (0,),):
            made = call(
                functools.partial(split_apart_kernel, rate, order, aparts),
                "split",
                [whole],
                [((4, tokens, hd), BF16)] * len(aparts),
            )
            for apart, block in zip(aparts, made):
                far[apart] = block
        for apart in FAR_FIRST:
            pairs = [(source, source ^ apart) for source in range(ctx_count)]
            far[apart] = lax.ppermute(far[apart], "ctx", pairs)
        x, *owns = call(
            functools.partial(collect_kernel, crossing, order),
            "collect",
            [offs_rows] + [block.reshape(4, rate, size, hd) for block in far],
            [((pieces, 4, rate, size, hd), BF16)]
            + [((pieces, 2, level.count, size, hd), BF16) for level in crossing],
        )
    else:
        (sent,) = call(
            functools.partial(split_kernel, rate),
            "split",
            [queries, key_rows, value_rows, out_grad],
            [((group, 4, tokens, hd), BF16)],
            limit=60,
        )
        x = exchange(sent)
        if fold > 1:
            x = x.reshape(pieces, fold, 4, rate, short, hd).transpose(0, 2, 3, 1, 4, 5)
        x = x.reshape(pieces, 4, rate, size, hd)
        owns = []
        for level in crossing:
            own = [
                lax.dynamic_slice(x, (0, 1, b, 0, 0), (pieces, 2, 1, size, hd))
                for b in level.starts(offs)
            ]
            owns.append(jnp.concatenate(own, axis=2))

    others = []
    for level, own in zip(crossing, owns):
        blocks = [own]
        for bit in range(level.bits):
            blocks += [flip(block, "ctx", low_bit + bit) for block in blocks]
        others.append(jnp.stack(blocks[1:]))

    state = (pieces, rate, size, hd)
    chunks = group * tokens // hd
    o, attn, lse, table = call(
        functools.partial(forward_kernel, local, score_scale),
        "local_forward",
        [offs_rows, gain, x],
        [(state, F32), (state, BF16), (state, F32), ((hd, hd), F32)],
        flops=10**8,
    )
    attn, lse, stats = call(
        functools.partial(crossing_forward_kernel, crossing, score_scale),
        "crossing_forward",
        [offs_rows, gain, x, o, attn, lse, table] + others,
        [(state, BF16), (state, F32), ((group, 4 * chunks, hd), F32)],
        scratch=[(state, F32), ((hd, hd), F32)],
    )
    stats = exchange(stats)
    outs = [(state, BF16), (state, BF16), ((1, hd), F32)]
    outs += [((3, pieces * level.count * size, hd), F32) for level in crossing]
    sent_types = [BF16 if level.bits == 1 else F32 for level in crossing]
    outs += [
        ((other.shape[0], 2 * level.pieces * level.count + 1, size, hd), kind)
        for level, other, kind in zip(crossing, others, sent_types)
    ]
    attended, grad, gsum, *rest = call(
        functools.partial(norm_kernel, group, crossing, scale, score_scale),
        "norm_and_crossing",
        [offs_rows, x, attn, lse, gain, stats] + others,
        outs,
        flops=10**7,
    )
    owns, parts = rest[: len(crossing)], rest[len(crossing) :]

    arrived = []
    for level, part in zip(crossing, parts):
        partial = [None] + [part[e] for e in range(part.shape[0])]
        for bit in reversed(range(level.bits)):
            half = 1 << bit
            came = [flip(block.astype(BF16), "ctx", low_bit + bit) for block in partial[half:]]
            partial = [
                c if b is None else b.astype(F32) + c.astype(F32)
                for b, c in zip(partial[:half], came)
            ]
        arrived.append(partial[0])
    if not alone:
        for axis, count, first in (("dp", dp_count, 0), ("ctx", ctx_count, low_bit)):
            for bit in range(first, count.bit_length() - 1):
                gsum = gsum + flip(gsum, axis, bit)

    main, kv = call(
        functools.partial(local_kernel, local, crossing, scale, score_scale),
        "local_backward",
        [offs_rows, x, attended, grad, lse, attn] + owns,
        [((pieces, 2, rate, size, hd), BF16), ((2,) + state, F32)],
        scratch=[(state, F32)] * 2,
        flops=3 * 10**8,
    )
    (packed,) = call(
        functools.partial(pack_kernel, crossing, fold, alone),
        "pack",
        [offs_rows, main, kv, gsum] + arrived,
        [((pieces, 4 * rate * size + TILE * fold, hd), BF16)],
        scratch=[((2,) + state, F32)],
    )
    if fold > 1:
        rows = packed[:, : 4 * rate * size].reshape(pieces, 4, rate, fold, short, hd)
        rows = rows.transpose(0, 3, 1, 2, 4, 5).reshape(group, 4 * tokens, hd)
        packed = jnp.concatenate([rows, packed[:, 4 * rate * size :].reshape(group, TILE, hd)], 1)
    back = exchange(packed)
    gains = jnp.sum(back[:, 4 * tokens :].astype(F32), axis=1)
    if alone:
        gains = gains + flip(gains, "dp", 0)
    gain_grad = gains.reshape(width) / math.sqrt(ctx_count * dp_count * tokens)
    row = ((1, tokens, width), BF16)
    dq, attended, dk, dv = call(
        functools.partial(join_kernel, rate),
        "join",
        [back],
        [row, row, row, row],
        flops=10**8,
    )
    return attended, dq, dk, dv, gain_grad


def solution(mesh):
    rows = P("dp", "ctx", None)
    return jax.shard_map(
        shards,
        mesh=mesh,
        in_specs=(rows, rows, rows, rows, P(), P()),
        out_specs=(rows, rows, rows, rows, P()),
        check_vma=False,
    )
```
